256 devices in a mesh: atoms: 32 (over x, z), samples: 8 (over y, core).
Axes of the slice: x: 4, y: 4, z: 8, core: 2. Of those that a mesh axis runs over, the one named last changes fastest.
Arguments:
- token_feats: bfloat16 [8192, 768], P('atoms', 'samples'), may hold values from -6 to 6
- proj_w: bfloat16 [768, 128], P('samples'), may hold values from -0.21875 to 0.21875
- atom_single: bfloat16 [65536, 128], P('atoms'), may hold values from -6 to 6
- atom_token: int32 [65536], P('atoms'), may hold values from 0 to 8191, as said below
- true_coords: float32 [3, 65536], P(None, 'atoms'), may hold values from -12 to 12
- noise: float32 [8, 3, 65536], P('samples', None, 'atoms'), may hold values from -6 to 6
- sigma: float32 [8], P('samples'), may hold values from 0.5 to 4
- coord_in: float32 [3, 128], replicated, may hold values from -3.5 to 3.5
- w_qkv: bfloat16 [3, 128, 384], replicated, as said below
- w_o: bfloat16 [3, 128, 128], replicated, may hold values from -0.5 to 0.5
- w_gu: bfloat16 [3, 128, 512], replicated, may hold values from -0.5 to 0.5
- w_down: bfloat16 [3, 256, 128], replicated, may hold values from -0.375 to 0.375
- gains: float32 [3, 2, 128], replicated, may hold values from 0.1 to 1.9
- w_out: float32 [128, 3], replicated, may hold values from -0.5 to 0.5
- pair_blocks: int32 [512, 13], P('atoms'), may hold values from 0 to 511, as said below
- pair_count: int32 [512], P('atoms'), may hold values from 1 to 13, as said below
Outputs:
- coord_grad: float32 [8, 3, 65536], P('samples', None, 'atoms')
- lddt_grad: float32 [8, 3, 65536], P('samples', None, 'atoms')
The draws below stay inside these ranges and needn't reach their ends.
Inputs may be any that keep to these rules, and one draw needn't show every extreme that they name: `atom_token`: atom a belongs to a token that differs from a // 8 by at most 16 before clipping to the token range; in each aligned run of 2048 atoms the first atom is -16 and the last +16 from that value before clipping. `pair_blocks`: the first pair_count[b] entries of row b are distinct blocks, the first being b itself; entries past pair_count[b] are b. Listing is symmetric: c is among the live entries of row b exactly when b is among the live entries of row c. `pair_count`: some block has 13 live entries. `w_qkv`: Queries, keys and values stand side by side along the last dimension.
All inputs are finite; a program needn't handle non-finite values.
Results may differ from the reference program's by a relative error of at most 0.018.
Values may be sent and summed in bfloat16 or wider, within the bound.
A program may use at most 64 MiB of HBM per device.

```python
import math
import jax
import jax.numpy as jnp
from jax import lax

C_TOKEN = 768
C_ATOM = 128
HEADS = 4
FF_ATOM = 256
ATOMS_TOK = 8
LAYERS = 3
QBLK = 32
KWIN = 128
HALO_TOK = 16
PAIR_BLK = 128
NOFF = 6
MAXP = 13
ATOM_DEV = 2048
TOKENS = 8192
NATOM = 65536
SAMPLES = 8
NBLK = 512


def draw_atom_token(key, part):
    position = jnp.arange(NATOM, dtype=jnp.int32)
    offset = jax.random.randint(jax.random.fold_in(key, 11), (NATOM,), -HALO_TOK, HALO_TOK + 1)
    inside = position % ATOM_DEV
    offset = jnp.where(inside == 0, -HALO_TOK, offset)
    offset = jnp.where(inside == ATOM_DEV - 1, HALO_TOK, offset)
    return jnp.clip(position // ATOMS_TOK + offset, 0, TOKENS - 1).astype(jnp.int32)


def pair_tables(key):
    blocks_dev = ATOM_DEV // PAIR_BLK
    devices = NBLK // blocks_dev
    far_shift = NBLK // 2 - 1
    other_shifts = jax.random.permutation(jax.random.fold_in(key, 21), NBLK // 2 - 2)[:NOFF - 1].astype(jnp.int32) + 1
    shifts = jnp.concatenate([jnp.full((1,), far_shift, jnp.int32), other_shifts])
    block_ids = jnp.arange(NBLK, dtype=jnp.int32)
    step_offsets = jnp.concatenate([jnp.zeros((1,), jnp.int32), shifts, -shifts])
    partner = (block_ids[:, None] + step_offsets[None, :]) % NBLK
    random_draws = jax.random.randint(jax.random.fold_in(key, 22), (NBLK, NBLK), 0, 9 * devices * devices)
    low_block = jnp.minimum(block_ids[:, None], partner)
    high_block = jnp.maximum(block_ids[:, None], partner)
    chance = random_draws[low_block, high_block]
    own_dev = block_ids // blocks_dev
    other_dev = partner // blocks_dev
    keep_limit = (devices + 2 * own_dev)[:, None] * (devices + 2 * other_dev)
    far_step = jnp.abs(step_offsets[None, :]) == far_shift
    keep_mask = (chance < keep_limit) | (step_offsets[None, :] == 0) | (high_block == NBLK - 1) | far_step
    slot_ids = jnp.arange(MAXP, dtype=jnp.int32)
    sort_key = (1 - keep_mask.astype(jnp.int32)) * MAXP + slot_ids[None, :]
    sort_order = jnp.argsort(sort_key, axis=1, stable=True)
    ordered = jnp.take_along_axis(partner, sort_order, axis=1)
    counts = jnp.sum(keep_mask.astype(jnp.int32), axis=1)
    listed = jnp.where(slot_ids[None, :] < counts[:, None], ordered, block_ids[:, None])
    return (listed.astype(jnp.int32), counts.astype(jnp.int32))


def draw_pair_blocks(key, part):
    return pair_tables(key)[0]


def draw_pair_count(key, part):
    return pair_tables(key)[1]


def draw_w_qkv(key, part):
    base_draw = jax.random.truncated_normal(key, -6.0, 6.0, (LAYERS, C_ATOM, 3 * C_ATOM), jnp.float32) * C_ATOM ** (-0.5)
    return base_draw.astype(jnp.bfloat16)


def shard_levels(stream_key, extent, split, least, largest):
    def one(dim, shards_of):
        steps = jax.random.uniform(jax.random.fold_in(jax.random.fold_in(stream_key, 6), dim), (shards_of,), jnp.float32, least / len(split), largest / len(split))
        return jnp.repeat(jnp.exp(steps), extent[dim] // shards_of).reshape((-1,) + (1,) * (len(extent) - dim - 1))

    gain = one(*split[0])
    for cut in split[1:]:
        gain = gain * one(*cut)
    return gain


def bell_draw(stream_key, shape, deviation, limit, cuts=(), kind=jnp.bfloat16):
    result = deviation * jax.random.normal(stream_key, shape, jnp.float32)
    if cuts:
        result = result * shard_levels(stream_key, shape, cuts, -0.22, 0.18)
    return jnp.clip(result, -limit, limit).astype(kind)


def setup_inputs(seed: int = 0) -> dict:
    key_list = jax.random.split(jax.random.key(seed), 17)
    token_feats = bell_draw(key_list[0], (TOKENS, C_TOKEN), 1.0, 6.0, ((0, 32), (1, 8)))
    proj_w = bell_draw(key_list[1], (C_TOKEN, C_ATOM), C_TOKEN ** -0.5, 0.21875, ((0, 8),))
    atom_single = bell_draw(key_list[2], (NATOM, C_ATOM), 1.0, 6.0, ((0, 32),))
    atom_token = draw_atom_token(jax.random.fold_in(key_list[16], 71), 0)
    true_coords = bell_draw(key_list[4], (3, NATOM), 2.0, 12.0, ((1, 32),), jnp.float32)
    noise = bell_draw(key_list[5], (SAMPLES, 3, NATOM), 1.0, 6.0, ((0, 8), (2, 32)), jnp.float32)
    sigma = jnp.clip(jnp.exp(math.log(4.0) - 2.0794415 * jax.random.uniform(key_list[6], (SAMPLES,), jnp.float32) ** shard_levels(key_list[6], (SAMPLES,), ((0, 8),), -0.2, 0.2)), 0.5, 4.0)
    coord_in = bell_draw(key_list[7], (3, C_ATOM), 3 ** -0.5, 3.5, (), jnp.float32)
    w_qkv = draw_w_qkv(jax.random.fold_in(key_list[16], 71), 0)
    w_o = bell_draw(key_list[9], (LAYERS, C_ATOM, C_ATOM), C_ATOM ** -0.5, 0.5)
    w_gu = bell_draw(key_list[10], (LAYERS, C_ATOM, 2 * FF_ATOM), C_ATOM ** -0.5, 0.5)
    w_down = bell_draw(key_list[11], (LAYERS, FF_ATOM, C_ATOM), FF_ATOM ** -0.5, 0.375)
    gains = jnp.clip(1.0 + 0.18 * jax.random.normal(key_list[12], (LAYERS, 2, C_ATOM), jnp.float32), 0.1, 1.9)
    w_out = bell_draw(key_list[13], (C_ATOM, 3), C_ATOM ** -0.5, 0.5, (), jnp.float32)
    pair_blocks = draw_pair_blocks(jax.random.fold_in(key_list[16], 71), 0)
    pair_count = draw_pair_count(jax.random.fold_in(key_list[16], 71), 0)
    return {"token_feats": token_feats, "proj_w": proj_w, "atom_single": atom_single, "atom_token": atom_token, "true_coords": true_coords, "noise": noise, "sigma": sigma, "coord_in": coord_in, "w_qkv": w_qkv, "w_o": w_o, "w_gu": w_gu, "w_down": w_down, "gains": gains, "w_out": w_out, "pair_blocks": pair_blocks, "pair_count": pair_count}


sigma_data = 2.0
norm_epsilon = 1e-05
thresholds = (0.5, 1.0, 2.0, 4.0)

def rms_norm(tensor):
    return tensor * lax.rsqrt(lax.optimization_barrier(jnp.mean(tensor * tensor, axis=-1, keepdims=True)) + norm_epsilon)

def window_attend(queries, padded_keys, padded_values, valid):
    samples, atoms, channels = queries.shape
    blocks = atoms // QBLK
    spread = KWIN // QBLK
    head_dim = channels // HEADS

    def windows(source):
        shaped = source.reshape((source.shape[0], blocks + spread - 1, QBLK) + source.shape[2:])
        return jnp.concatenate([shaped[:, shift_index:shift_index + blocks] for shift_index in range(spread)], axis=2)
    key_win = windows(padded_keys).reshape(samples, blocks, KWIN, HEADS, head_dim).astype(jnp.float32)
    value_win = windows(padded_values).reshape(samples, blocks, KWIN, HEADS, head_dim).astype(jnp.float32)
    mask_win = windows(valid[None])
    query_blk = queries.reshape(samples, blocks, QBLK, HEADS, head_dim).astype(jnp.float32)
    scores = jnp.einsum('sbqhe,sbkhe->sbhqk', query_blk, key_win) * head_dim ** (-0.5)
    scores = jnp.where(mask_win[:, :, None, None, :], scores, -1e+30)
    row_max = lax.optimization_barrier(jnp.max(scores, axis=-1, keepdims=True))
    exp_scores = jnp.exp(scores - row_max)
    weights = (exp_scores / lax.optimization_barrier(jnp.sum(exp_scores, axis=-1, keepdims=True))).astype(jnp.bfloat16)
    attended = jnp.einsum('sbhqk,sbkhe->sbqhe', weights.astype(jnp.float32), value_win)
    return attended.astype(jnp.bfloat16).reshape(samples, atoms, channels)

def tile_terms(own_pred, own_true, part_pred, part_true, keep_mask):
    square_pred = 0.0
    square_true = 0.0
    for axis_index in range(3):
        coord_gap = own_pred[:, axis_index, :, :, None] - part_pred[:, axis_index, :, None, :]
        square_pred = square_pred + coord_gap * coord_gap
        true_gap = own_true[axis_index, :, :, None] - part_true[axis_index, :, None, :]
        square_true = square_true + true_gap * true_gap
    dist_pred = jnp.sqrt(square_pred + 1.0)
    dist_true = jnp.sqrt(square_true + 1.0)
    gap_dist = dist_pred - dist_true
    error_soft = jnp.sqrt(gap_dist * gap_dist + 0.01)
    slope_sum = 0.0
    for threshold_value in thresholds:
        sig_value = jax.nn.sigmoid(threshold_value - error_soft)
        slope_sum = slope_sum + sig_value * (1.0 - sig_value)
    pair_coef = -0.25 * slope_sum * gap_dist / (error_soft * dist_pred) * keep_mask
    row_coef = lax.optimization_barrier(jnp.sum(pair_coef, axis=-1))
    col_coef = lax.optimization_barrier(jnp.sum(pair_coef, axis=-2))
    own_side = own_pred * row_coef[:, None] - jnp.einsum('stij,sdtj->sdti', pair_coef, part_pred, precision=lax.Precision.HIGHEST)
    part_side = part_pred * col_coef[:, None] - jnp.einsum('stij,sdti->sdtj', pair_coef, own_pred, precision=lax.Precision.HIGHEST)
    return (own_side, part_side)

def dense(left, right):
    return jnp.einsum('sac,cf->saf', left.astype(jnp.float32), right.astype(jnp.float32))

def reference(token_feats, proj_w, atom_single, atom_token, true_coords, noise, sigma, coord_in, w_qkv, w_o, w_gu, w_down, gains, w_out, pair_blocks, pair_count):
    token_proj = jnp.dot(token_feats, proj_w, preferred_element_type=jnp.float32).astype(jnp.bfloat16)
    atom_base = atom_single.astype(jnp.float32) + token_proj[atom_token].astype(jnp.float32)
    sigma_col = sigma[:, None, None]
    noisy = true_coords[None] + sigma_col * noise
    noise_total = sigma_col * sigma_col + sigma_data * sigma_data
    scaled = noisy / jnp.sqrt(noise_total)
    hidden = atom_base[None] + jnp.einsum('sda,dc->sac', scaled, coord_in, precision=lax.Precision.HIGHEST)
    key_halo = (KWIN - QBLK) // 2
    position = jnp.arange(NATOM + 2 * key_halo) - key_halo
    valid = (position >= 0) & (position < NATOM)
    channels = C_ATOM
    for layer_index in range(LAYERS):
        normed = (rms_norm(hidden) * gains[layer_index, 0]).astype(jnp.bfloat16)
        qkv_all = dense(normed, w_qkv[layer_index]).astype(jnp.bfloat16)
        queries = qkv_all[:, :, :channels]
        key_value = jnp.pad(qkv_all[:, :, channels:], ((0, 0), (key_halo, key_halo), (0, 0)))
        attended = window_attend(queries, key_value[:, :, :channels], key_value[:, :, channels:], valid)
        hidden = hidden + dense(attended, w_o[layer_index])
        normed = (rms_norm(hidden) * gains[layer_index, 1]).astype(jnp.bfloat16)
        gate_up = dense(normed, w_gu[layer_index])
        inner_act = (jax.nn.silu(gate_up[..., :FF_ATOM]) * gate_up[..., FF_ATOM:]).astype(jnp.bfloat16)
        hidden = hidden + dense(inner_act, w_down[layer_index])
    update = jnp.einsum('sac,cd->sda', rms_norm(hidden), w_out, precision=lax.Precision.HIGHEST)
    predicted = sigma_data * sigma_data / noise_total * noisy + sigma_col * sigma_data / jnp.sqrt(noise_total) * update
    mse_part = 2.0 / 3.0 * (noise_total / (sigma_col * sigma_data) ** 2) * (predicted - true_coords[None])
    blocks_pred = predicted.reshape(SAMPLES, 3, NBLK, PAIR_BLK)
    blocks_true = true_coords.reshape(3, NBLK, PAIR_BLK)
    diagonal_mask = jnp.eye(PAIR_BLK, dtype=jnp.float32)
    slot_ids = jnp.arange(MAXP, dtype=jnp.int32)

    def visit(back_grads, block_index):
        partners = pair_blocks[block_index]
        live_slot = (slot_ids < pair_count[block_index]).astype(jnp.float32)
        keep_mask = live_slot[:, None, None] * (1.0 - (partners == block_index).astype(jnp.float32)[:, None, None] * diagonal_mask)
        own_one = lax.dynamic_index_in_dim(blocks_pred, block_index, 2, keepdims=True)
        own_pred = jnp.broadcast_to(own_one, (SAMPLES, 3, MAXP, PAIR_BLK))
        true_one = lax.dynamic_index_in_dim(blocks_true, block_index, 1, keepdims=True)
        own_true = jnp.broadcast_to(true_one, (3, MAXP, PAIR_BLK))
        part_pred = jnp.take(blocks_pred, partners, axis=2)
        part_true = jnp.take(blocks_true, partners, axis=1)
        own_side, part_side = tile_terms(own_pred, own_true, part_pred, part_true, keep_mask)
        back_grads = back_grads.at[:, :, partners].add(part_side)
        return (back_grads, lax.optimization_barrier(jnp.sum(own_side, axis=2)))
    back_grads, own_grads = lax.scan(visit, jnp.zeros((SAMPLES, 3, NBLK, PAIR_BLK), jnp.float32), jnp.arange(NBLK, dtype=jnp.int32))
    pair_grad = jnp.moveaxis(own_grads, 0, 2) + back_grads
    pair_total = jnp.sum(pair_count.astype(jnp.float32) * (PAIR_BLK * PAIR_BLK) - PAIR_BLK)
    lddt_grad = NATOM * PAIR_BLK / pair_total * pair_grad.reshape(SAMPLES, 3, NATOM)
    coord_grad = mse_part - lddt_grad / PAIR_BLK
    return (coord_grad, lddt_grad)
```

```python
import functools
import math

import jax
import jax.numpy as jnp
from jax import lax
from jax.experimental import pallas as pl
from jax.experimental.pallas import tpu as pltpu
from jax.sharding import PartitionSpec as P

HEADS = 4
HEAD_DIM = 32
FF_ATOM = 256
LAYERS = 3
QBLK = 32
KWIN = 128
PAIR_BLK = 128
CHANNELS = 128
CHUNK = 256
HALO = 256
TOK_HALO = 48
TOK_WIN = 64
EPS = 1e-05
VMEM_LIMIT = 56 * 1024 * 1024

f32 = jnp.float32
bf16 = jnp.bfloat16


def dot(a, b, dims=((1,), (0,)), precision=None):
    return lax.dot_general(a, b, (dims, ((), ())), precision=precision, preferred_element_type=f32)


def pieces(v):
    hi = v.astype(bf16).astype(f32)
    mid = (v - hi).astype(bf16).astype(f32)
    lo = (v - hi - mid).astype(bf16).astype(f32)
    return hi, mid, lo


def rms_scale(h):
    return h * lax.rsqrt(jnp.mean(h * h, axis=1, keepdims=True) + EPS)


def atoms_kernel(
    place, scal, single, cx, tok, coord_w, wqkv, wo, wgu, wdown, gains, wout,
    pred, hid, qkv, bias,
):
    rows = single.shape[0] - 2 * HALO
    ext = single.shape[0]
    first_atom = place[0]
    total_atoms = place[1]
    first_tok = place[2]
    q_scale = math.log2(math.e) / math.sqrt(HEAD_DIM)
    lane = lax.broadcasted_iota(jnp.int32, (1, CHANNELS), 1) // HEAD_DIM

    pos = first_atom - HALO + lax.broadcasted_iota(jnp.int32, (ext, CHANNELS), 0)
    bias[...] = jnp.where((pos >= 0) & (pos < total_atoms), 0.0, -1e30)

    def project(layer, at, h):
        normed = (rms_scale(h) * gains[2 * layer : 2 * layer + 1, :]).astype(bf16)
        out = dot(normed, wqkv[layer])
        rows_at = pl.ds(at, h.shape[0])
        qkv[layer % 2, rows_at, 0:128] = (out[:, :128] * q_scale).astype(bf16)
        qkv[layer % 2, rows_at, 128:384] = out[:, 128:].astype(bf16)

    def first(k, _):
        at = pl.multiple_of(k * CHUNK, CHUNK)
        c = cx[:, pl.ds(at, CHUNK)]
        hi, mid, lo = pieces(c)
        rel = c[3:4, :].astype(jnp.int32) - (first_tok - TOK_HALO + k * (CHUNK // 8))
        hot = jnp.where(lax.broadcasted_iota(jnp.int32, (TOK_WIN, CHUNK), 0) == rel, 1.0, 0.0)
        left = jnp.concatenate([hot, hi, hi, hi, mid, mid, lo], axis=0).astype(bf16)
        tok_at = pl.ds(pl.multiple_of(k * (CHUNK // 8), CHUNK // 8), TOK_WIN)
        right = jnp.concatenate([tok[tok_at, :], coord_w[...]], axis=0)
        h = single[pl.ds(at, CHUNK), :].astype(f32) + dot(left, right, ((0,), (0,)))
        hid[pl.ds(at, CHUNK), :] = h
        project(0, at, h)
        return 0

    lax.fori_loop(0, ext // CHUNK, first, 0)

    def attend(layer, at, size):
        buf = layer % 2
        outs = []
        for w in range(size // QBLK):
            q = qkv[buf, pl.ds(at + w * QBLK, QBLK), 0:128]
            keys_at = pl.ds(at + (w * QBLK - 48), KWIN)
            keys = qkv[buf, keys_at, 128:256]
            values = qkv[buf, keys_at, 256:384]
            zero = jnp.zeros_like(q)
            spread = jnp.concatenate([jnp.where(lane == h, q, zero) for h in range(HEADS)], axis=0)
            scores = dot(keys, spread, ((1,), (1,))) + bias[keys_at, :]
            top = jnp.max(scores, axis=0, keepdims=True)
            weights = jnp.exp2(scores - top)
            weights = (weights * (1.0 / jnp.sum(weights, axis=0, keepdims=True))).astype(bf16)
            both = dot(weights, values, ((0,), (0,)))
            out = both[0:QBLK]
            for h in range(1, HEADS):
                out = jnp.where(lane == h, both[h * QBLK : (h + 1) * QBLK], out)
            outs.append(out.astype(bf16))
        return jnp.concatenate(outs, axis=0)

    def block(layer, at, size):
        h = hid[pl.ds(at, size), :]
        h = h + dot(attend(layer, at, size), wo[layer])
        normed = (rms_scale(h) * gains[2 * layer + 1 : 2 * layer + 2, :]).astype(bf16)
        gu = dot(normed, wgu[layer])
        half = 0.5 * gu[:, :FF_ATOM]
        inner = (half * (1.0 + jnp.tanh(half)) * gu[:, FF_ATOM:]).astype(bf16)
        h = h + dot(inner, wdown[layer])
        if layer + 1 < LAYERS:
            hid[pl.ds(at, size), :] = h
            project(layer + 1, at, h)
        else:
            update = dot(wout[...], rms_scale(h), ((1,), (1,)), lax.Precision.HIGHEST)
            noisy = cx[:, pl.ds(at, size)]
            pred[:, pl.ds(pl.multiple_of(at - HALO, size), size)] = scal[0] * noisy + scal[1] * update

    for layer in range(LAYERS):
        low = HALO if layer == LAYERS - 1 else HALO - 128
        span = rows if layer == LAYERS - 1 else rows + 256

        def step(k, _, layer=layer, low=low):
            block(layer, pl.multiple_of(low + k * CHUNK, 128), CHUNK)
            return 0

        lax.fori_loop(0, span // CHUNK, step, 0)


def pairs_kernel(
    scal, counts, partners, gathered_pred, gathered_true, pred, true,
    coord_grad, lddt_grad, wide_pred, wide_true,
):
    blocks = counts.shape[0]
    me = partners[0, 0] // blocks * blocks
    wide_pred[...] = gathered_pred[...].astype(f32)
    wide_true[...] = gathered_true[...].astype(f32)
    row8 = lax.broadcasted_iota(jnp.int32, (8, PAIR_BLK), 0)
    row4 = row8 & 3
    diff = lax.broadcasted_iota(jnp.int32, (PAIR_BLK, PAIR_BLK), 0) - lax.broadcasted_iota(
        jnp.int32, (PAIR_BLK, PAIR_BLK), 1
    )

    def partner_rows(wide, p):
        base = p // blocks * (3 * blocks) + p % blocks
        x, y, z = (wide[pl.ds(base + d * blocks, 1), :] for d in range(3))
        n1, n2, n3 = pieces(x * x + y * y + z * z)
        xyz = jnp.where(row4 == 0, x, jnp.where(row4 == 1, y, z))
        upper = jnp.where(row4 == 3, jnp.where(row8 == 3, n1, n2), xyz)
        ones = jnp.where(row8 < 7, 1.0, 0.0)
        lower = jnp.where(row8 < 3, xyz, jnp.where(row8 == 3, n3, ones))
        return jnp.concatenate([upper, lower], axis=0)

    def own_rows(x, y, z):
        n = x * x + y * y + z * z + 1.0
        n1, n2, n3 = pieces(0.25 * n)
        xp, yp, zp = pieces(-0.5 * x), pieces(-0.5 * y), pieces(-0.5 * z)

        def xyz(i):
            return jnp.where(row4 == 0, xp[i], jnp.where(row4 == 1, yp[i], zp[i]))

        upper = jnp.where(row4 == 3, 0.25, jnp.where(row8 < 4, xyz(0), xyz(1)))
        norms = jnp.where(row8 == 4, n1, jnp.where(row8 == 5, n2, n3))
        norms = jnp.where(row8 == 7, 0.0, norms)
        lower = jnp.where(row8 < 3, xyz(2), jnp.where(row8 == 3, 0.25, norms))
        return jnp.concatenate([upper, lower], axis=0)

    def visit(b, _):
        at = pl.ds(pl.multiple_of(b * PAIR_BLK, PAIR_BLK), PAIR_BLK)
        px, py, pz = (pred[d : d + 1, at] for d in range(3))
        tx, ty, tz = (true[d : d + 1, at] for d in range(3))
        none = jnp.zeros((16, PAIR_BLK), f32)
        own = jnp.concatenate(
            [
                jnp.concatenate([own_rows(px, py, pz), none], axis=1),
                jnp.concatenate([none, own_rows(tx, ty, tz)], axis=1),
            ],
            axis=0,
        ).astype(bf16)

        def tile(m, total):
            p = partners[b, m]
            part_pred = partner_rows(wide_pred, p)
            part = jnp.concatenate([part_pred, partner_rows(wide_true, p)], axis=0).astype(bf16)
            squares = dot(part, own, ((0,), (0,)))
            sp, st = squares[:, :PAIR_BLK], squares[:, PAIR_BLK:]
            rp = lax.rsqrt(sp)
            gap = sp * rp - st * lax.rsqrt(st)
            e2 = gap * gap + 0.0025
            re = lax.rsqrt(e2)
            err = e2 * re
            th = [jnp.tanh(0.5 * t - err) for t in (0.5, 1.0, 2.0, 4.0)]
            slope = 4.0 - (th[0] * th[0] + th[1] * th[1] + th[2] * th[2] + th[3] * th[3])
            coef = slope * gap * (re * rp)
            shut = jnp.where(m == 0, 0, 2 * PAIR_BLK)
            coef = jnp.where(diff == shut, 0.0, coef)
            sums = dot(part[0:16], coef.astype(bf16))
            return total + sums[8:16]

        total = lax.fori_loop(0, counts[b], tile, jnp.zeros((8, PAIR_BLK), f32))
        for d, (pc, tc) in enumerate(((px, tx), (py, ty), (pz, tz))):
            lg = scal[0] * (pc * total[4:5] - total[d : d + 1])
            lddt_grad[0, d : d + 1, at] = lg
            coord_grad[0, d : d + 1, at] = scal[1] * (pc - tc) - lg * (1.0 / PAIR_BLK)
        return 0

    lax.fori_loop(0, blocks, visit, 0)


def vmem(n):
    return [pl.BlockSpec(memory_space=pltpu.VMEM)] * n


def smem(n):
    return [pl.BlockSpec(memory_space=pltpu.SMEM)] * n


def run_atoms(place, scal, single, cx, tok, coord_in, w_qkv, w_o, w_gu, w_down, gains, w_out):
    ext = single.shape[0]
    rows = ext - 2 * HALO
    c3 = jnp.pad(coord_in, ((0, 5), (0, 0)))
    hi, mid, lo = (lax.reduce_precision(c3, 8, 7), None, None)
    rest = c3 - hi
    mid = lax.reduce_precision(rest, 8, 7)
    lo = rest - mid
    coord_w = jnp.concatenate([hi, mid, lo, hi, mid, hi], axis=0).astype(bf16)
    gains8 = jnp.pad(gains.reshape(2 * LAYERS, CHANNELS), ((0, 2), (0, 0)))
    wout8 = jnp.pad(w_out.T, ((0, 5), (0, 0)))
    return pl.pallas_call(
        atoms_kernel,
        name="atoms",
        out_shape=jax.ShapeDtypeStruct((8, rows), f32),
        in_specs=smem(2) + vmem(10),
        out_specs=pl.BlockSpec(memory_space=pltpu.VMEM),
        scratch_shapes=[
            pltpu.VMEM((ext, CHANNELS), f32),
            pltpu.VMEM((2, ext, 3 * CHANNELS), bf16),
            pltpu.VMEM((ext, CHANNELS), f32),
        ],
        compiler_params=pltpu.CompilerParams(vmem_limit_bytes=VMEM_LIMIT),
    )(place, scal, single, cx, tok, coord_w, w_qkv, w_o, w_gu, w_down, gains8, wout8)


def run_pairs(scal, counts, partners, gathered_pred, gathered_true, pred, true):
    rows = pred.shape[1]
    wide = pltpu.VMEM(gathered_pred.shape, f32)
    out = jax.ShapeDtypeStruct((1, 3, rows), f32)
    return pl.pallas_call(
        pairs_kernel,
        name="pairs",
        out_shape=(out, out),
        in_specs=smem(3) + vmem(4),
        out_specs=tuple(vmem(2)),
        scratch_shapes=[wide, wide],
        compiler_params=pltpu.CompilerParams(vmem_limit_bytes=VMEM_LIMIT),
    )(scal, counts, partners, gathered_pred, gathered_true, pred, true)


def extended(value, axis, dim, width):
    peers, length = (lax.axis_size(axis), value.shape[dim])
    up = [(i, (i + 1) % peers) for i in range(peers)]
    down = [(j, i) for i, j in up]
    last = lax.slice_in_dim(value, length - width, length, axis=dim)
    first = lax.slice_in_dim(value, 0, width, axis=dim)
    before = lax.ppermute(last, axis, up)
    after = lax.ppermute(first, axis, down)
    return jnp.concatenate([before, value, after], axis=dim)


def on_device(
    token_feats, proj_w, atom_single, atom_token, true_coords, noise, sigma, coord_in,
    w_qkv, w_o, w_gu, w_down, gains, w_out, pair_blocks, pair_count,
):
    rank = lax.axis_index("atoms")
    tok_rows = token_feats.shape[0]
    rows = atom_single.shape[0]
    total_atoms = rows * lax.axis_size("atoms")
    whole_feats = lax.all_gather(token_feats, "samples", axis=1, tiled=True)
    whole_proj = lax.all_gather(proj_w, "samples", axis=0, tiled=True)
    token_proj = jnp.dot(whole_feats, whole_proj, preferred_element_type=f32).astype(bf16)
    tok = extended(token_proj, "atoms", 0, TOK_HALO)
    single = extended(atom_single, "atoms", 0, HALO)
    sig = sigma[0]
    noise_total = sig * sig + 4.0
    root = jnp.sqrt(noise_total)
    scaled = (true_coords + sig * noise[0]) / root
    cx = jnp.concatenate(
        [scaled, atom_token.astype(f32)[None], jnp.zeros((4, rows), f32)], axis=0
    )
    cx = extended(cx, "atoms", 1, HALO)
    place = jnp.stack([rank * rows, jnp.int32(total_atoms), rank * tok_rows]).astype(jnp.int32)
    scal = jnp.stack([4.0 / root, 2.0 * sig / root])
    pred = run_atoms(place, scal, single, cx, tok, coord_in, w_qkv, w_o, w_gu, w_down, gains, w_out)

    def everyone(v):
        return lax.all_gather(v[:3].astype(bf16).reshape(-1, PAIR_BLK), "atoms", axis=0, tiled=True)

    total_count = lax.psum(jnp.sum(pair_count), "atoms").astype(f32)
    pair_total = total_count * (PAIR_BLK * PAIR_BLK) - PAIR_BLK * (total_atoms // PAIR_BLK)
    scal2 = jnp.stack(
        [total_atoms * PAIR_BLK / pair_total * (-0.0625), 2.0 / 3.0 * noise_total / (2.0 * sig) ** 2]
    )
    return run_pairs(
        scal2, pair_count, pair_blocks, everyone(pred), everyone(true_coords), pred, true_coords
    )


def solution(mesh):
    in_specs = (
        P("atoms", "samples"),
        P("samples", None),
        P("atoms", None),
        P("atoms"),
        P(None, "atoms"),
        P("samples", None, "atoms"),
        P("samples"),
        P(), P(), P(), P(), P(), P(), P(),
        P("atoms", None),
        P("atoms"),
    )
    out_specs = (P("samples", None, "atoms"), P("samples", None, "atoms"))
    return jax.shard_map(on_device, mesh=mesh, in_specs=in_specs, out_specs=out_specs, check_vma=False)
```

```python
import functools
import math

import jax
import jax.numpy as jnp
from jax import lax
from jax.experimental import pallas as pl
from jax.experimental.pallas import tpu as pltpu
from jax.sharding import PartitionSpec as P

HEADS = 4
HEAD_DIM = 32
FF_ATOM = 256
LAYERS = 3
QBLK = 32
KWIN = 128
PAIR_BLK = 128
CHANNELS = 128
CHUNK = 256
HALO = 256
TOK_HALO = 48
TOK_WIN = 64
EPS = 1e-05
VMEM_LIMIT = 56 * 1024 * 1024

f32 = jnp.float32
bf16 = jnp.bfloat16


def dot(a, b, dims=((1,), (0,)), precision=None):
    return lax.dot_general(a, b, (dims, ((), ())), precision=precision, preferred_element_type=f32)


def pieces(v):
    hi = v.astype(bf16).astype(f32)
    mid = (v - hi).astype(bf16).astype(f32)
    lo = (v - hi - mid).astype(bf16).astype(f32)
    return hi, mid, lo


def rms_scale(h):
    return h * lax.rsqrt(jnp.mean(h * h, axis=1, keepdims=True) + EPS)


def atoms_kernel(
    place, scal, single, cx, tok, coord_w, wqkv, wo, wgu, wdown, gains, wout,
    pred, pay, hid, qkv, bias, wide,
):
    rows = single.shape[0] - 2 * HALO
    ext = single.shape[0]
    first_atom = place[0]
    total_atoms = place[1]
    first_tok = place[2]
    q_scale = math.log2(math.e) / math.sqrt(HEAD_DIM)
    lane = lax.broadcasted_iota(jnp.int32, (1, CHANNELS), 1) // HEAD_DIM

    pos = first_atom - HALO + lax.broadcasted_iota(jnp.int32, (ext, CHANNELS), 0)
    bias[...] = jnp.where((pos >= 0) & (pos < total_atoms), 0.0, -1e30)

    def project(layer, at, h):
        normed = (rms_scale(h) * gains[2 * layer : 2 * layer + 1, :]).astype(bf16)
        out = dot(normed, wqkv[layer])
        rows_at = pl.ds(at, h.shape[0])
        qkv[layer % 2, rows_at, 0:128] = (out[:, :128] * q_scale).astype(bf16)
        qkv[layer % 2, rows_at, 128:384] = out[:, 128:].astype(bf16)

    def first(k, _):
        at = pl.multiple_of(k * CHUNK, CHUNK)
        c = cx[:, pl.ds(at, CHUNK)]
        hi, mid, lo = pieces(c)
        rel = c[3:4, :].astype(jnp.int32) - (first_tok - TOK_HALO + k * (CHUNK // 8))
        hot = jnp.where(lax.broadcasted_iota(jnp.int32, (TOK_WIN, CHUNK), 0) == rel, 1.0, 0.0)
        left = jnp.concatenate([hot, hi, hi, hi, mid, mid, lo], axis=0).astype(bf16)
        tok_at = pl.ds(pl.multiple_of(k * (CHUNK // 8), CHUNK // 8), TOK_WIN)
        right = jnp.concatenate([tok[tok_at, :], coord_w[...]], axis=0)
        h = single[pl.ds(at, CHUNK), :].astype(f32) + dot(left, right, ((0,), (0,)))
        hid[pl.ds(at, CHUNK), :] = h
        project(0, at, h)
        return 0

    lax.fori_loop(0, ext // CHUNK, first, 0)

    def attend(layer, at, size):
        buf = layer % 2
        outs = []
        for w in range(size // QBLK):
            q = qkv[buf, pl.ds(at + w * QBLK, QBLK), 0:128]
            keys_at = pl.ds(at + (w * QBLK - 48), KWIN)
            keys = qkv[buf, keys_at, 128:256]
            values = qkv[buf, keys_at, 256:384]
            zero = jnp.zeros_like(q)
            spread = jnp.concatenate([jnp.where(lane == h, q, zero) for h in range(HEADS)], axis=0)
            scores = dot(keys, spread, ((1,), (1,))) + bias[keys_at, :]
            top = jnp.max(scores, axis=0, keepdims=True)
            weights = jnp.exp2(scores - top)
            weights = (weights * (1.0 / jnp.sum(weights, axis=0, keepdims=True))).astype(bf16)
            both = dot(weights, values, ((0,), (0,)))
            out = both[0:QBLK]
            for h in range(1, HEADS):
                out = jnp.where(lane == h, both[h * QBLK : (h + 1) * QBLK], out)
            outs.append(out.astype(bf16))
        return jnp.concatenate(outs, axis=0)

    def block(layer, at, size):
        h = hid[pl.ds(at, size), :]
        h = h + dot(attend(layer, at, size), wo[layer])
        normed = (rms_scale(h) * gains[2 * layer + 1 : 2 * layer + 2, :]).astype(bf16)
        gu = dot(normed, wgu[layer])
        half = 0.5 * gu[:, :FF_ATOM]
        inner = (half * (1.0 + jnp.tanh(half)) * gu[:, FF_ATOM:]).astype(bf16)
        h = h + dot(inner, wdown[layer])
        if layer + 1 < LAYERS:
            hid[pl.ds(at, size), :] = h
            project(layer + 1, at, h)
        else:
            update = dot(wout[...], rms_scale(h), ((1,), (1,)), lax.Precision.HIGHEST)
            noisy = cx[:, pl.ds(at, size)]
            out = scal[0] * noisy + scal[1] * update
            pred[:, pl.ds(pl.multiple_of(at - HALO, size), size)] = out
            first_block = (at - HALO) // PAIR_BLK
            for i in range(size // PAIR_BLK):
                for d in range(3):
                    row = pl.ds(d * (rows // PAIR_BLK) + first_block + i, 1)
                    wide[row, :] = out[d : d + 1, i * PAIR_BLK : (i + 1) * PAIR_BLK]

    for layer in range(LAYERS):
        low = HALO if layer == LAYERS - 1 else HALO - 128
        span = rows if layer == LAYERS - 1 else rows + 256

        def step(k, _, layer=layer, low=low):
            block(layer, pl.multiple_of(low + k * CHUNK, 128), CHUNK)
            return 0

        lax.fori_loop(0, span // CHUNK, step, 0)
    pay[...] = wide[...].astype(bf16)


def pairs_kernel(
    scal, counts, partners, gathered_pred, gathered_true, pred, true,
    coord_grad, lddt_grad, wide_pred, wide_true,
):
    blocks = counts.shape[0]
    wide_pred[...] = gathered_pred[...].astype(f32)
    wide_true[...] = gathered_true[...].astype(f32)
    peers = gathered_pred.shape[0] // (3 * blocks)
    listed = jnp.zeros((blocks, PAIR_BLK), f32)
    for peer in range(peers):
        listed = listed + wide_true[peer * 4 * blocks + 3 * blocks : (peer + 1) * 4 * blocks, :]
    listed = jnp.sum(listed, axis=0, keepdims=True)
    total_pairs = listed * (PAIR_BLK * PAIR_BLK) - float(PAIR_BLK * blocks * peers)
    pair_scale = -0.0625 * (blocks * peers * PAIR_BLK * PAIR_BLK) / total_pairs
    row8 = lax.broadcasted_iota(jnp.int32, (8, PAIR_BLK), 0)
    row4 = row8 & 3
    diff = lax.broadcasted_iota(jnp.int32, (PAIR_BLK, PAIR_BLK), 0) - lax.broadcasted_iota(
        jnp.int32, (PAIR_BLK, PAIR_BLK), 1
    )

    def partner_rows(wide, p, per):
        base = p // blocks * (per * blocks) + p % blocks
        x, y, z = (wide[pl.ds(base + d * blocks, 1), :] for d in range(3))
        n1, n2, n3 = pieces(x * x + y * y + z * z)
        xyz = jnp.where(row4 == 0, x, jnp.where(row4 == 1, y, z))
        upper = jnp.where(row4 == 3, jnp.where(row8 == 3, n1, n2), xyz)
        ones = jnp.where(row8 < 7, 1.0, 0.0)
        lower = jnp.where(row8 < 3, xyz, jnp.where(row8 == 3, n3, ones))
        return jnp.concatenate([upper, lower], axis=0)

    def own_rows(x, y, z):
        n = x * x + y * y + z * z + 1.0
        n1, n2, n3 = pieces(0.25 * n)
        xp, yp, zp = pieces(-0.5 * x), pieces(-0.5 * y), pieces(-0.5 * z)

        def xyz(i):
            return jnp.where(row4 == 0, xp[i], jnp.where(row4 == 1, yp[i], zp[i]))

        upper = jnp.where(row4 == 3, 0.25, jnp.where(row8 < 4, xyz(0), xyz(1)))
        norms = jnp.where(row8 == 4, n1, jnp.where(row8 == 5, n2, n3))
        norms = jnp.where(row8 == 7, 0.0, norms)
        lower = jnp.where(row8 < 3, xyz(2), jnp.where(row8 == 3, 0.25, norms))
        return jnp.concatenate([upper, lower], axis=0)

    def visit(b, _):
        at = pl.ds(pl.multiple_of(b * PAIR_BLK, PAIR_BLK), PAIR_BLK)
        px, py, pz = (pred[d : d + 1, at] for d in range(3))
        tx, ty, tz = (true[d : d + 1, at] for d in range(3))
        none = jnp.zeros((16, PAIR_BLK), f32)
        own = jnp.concatenate(
            [
                jnp.concatenate([own_rows(px, py, pz), none], axis=1),
                jnp.concatenate([none, own_rows(tx, ty, tz)], axis=1),
            ],
            axis=0,
        ).astype(bf16)

        def tile(m, total):
            p = partners[b, m]
            part_pred = partner_rows(wide_pred, p, 3)
            part = jnp.concatenate([part_pred, partner_rows(wide_true, p, 4)], axis=0).astype(bf16)
            squares = dot(part, own, ((0,), (0,)))
            sp, st = squares[:, :PAIR_BLK], squares[:, PAIR_BLK:]
            rp = lax.rsqrt(sp)
            gap = sp * rp - st * lax.rsqrt(st)
            e2 = gap * gap + 0.0025
            re = lax.rsqrt(e2)
            err = e2 * re
            th = [jnp.tanh(0.5 * t - err) for t in (0.5, 1.0, 2.0, 4.0)]
            slope = 4.0 - (th[0] * th[0] + th[1] * th[1] + th[2] * th[2] + th[3] * th[3])
            coef = slope * gap * (re * rp)
            shut = jnp.where(m == 0, 0, 2 * PAIR_BLK)
            coef = jnp.where(diff == shut, 0.0, coef)
            sums = dot(part[0:16], coef.astype(bf16))
            return total + sums[8:16]

        total = lax.fori_loop(0, counts[b], tile, jnp.zeros((8, PAIR_BLK), f32))
        for d, (pc, tc) in enumerate(((px, tx), (py, ty), (pz, tz))):
            lg = pair_scale * (pc * total[4:5] - total[d : d + 1])
            lddt_grad[0, d : d + 1, at] = lg
            coord_grad[0, d : d + 1, at] = scal[0] * (pc - tc) - lg * (1.0 / PAIR_BLK)
        return 0

    lax.fori_loop(0, blocks, visit, 0)


MESH = pl.DeviceIdType.MESH


def remote(src, dst, send, recv, atom, sample):
    return pltpu.make_async_remote_copy(
        src_ref=src, dst_ref=dst, send_sem=send, recv_sem=recv,
        device_id=(atom, sample), device_id_type=MESH,
    )


def share_kernel(
    atom_peers, sample_peers, sigma, feats, proj, single, token, true, noise, counts,
    tok, single_ext, cx, gathered,
    partial, arrived, slab, pay, wide,
    part_send, part_recv, tok_send, tok_recv, edge_send, edge_recv, near_send, near_recv,
    all_send, all_recv, own_sem,
):
    me = lax.axis_index("atoms")
    mine = lax.axis_index("samples")
    right = lax.rem(me + 1, atom_peers)
    left = lax.rem(me + atom_peers - 1, atom_peers)
    rows = single.shape[0]
    share = feats.shape[0] // sample_peers
    pay_rows = pay.shape[0]

    barrier = pltpu.get_barrier_semaphore()

    def greet(atom, sample):
        pl.semaphore_signal(barrier, inc=1, device_id=(atom, sample), device_id_type=MESH)

    for step in range(1, sample_peers):
        greet(me, lax.rem(mine + step, sample_peers))
    for step in range(sample_peers):
        greet(left, lax.rem(mine + step, sample_peers))
        greet(right, lax.rem(mine + step, sample_peers))

    @pl.loop(2, atom_peers - 1)
    def _(step):
        greet(lax.rem(me + step, atom_peers), mine)

    own_copy = pltpu.make_async_copy(single, single_ext.at[pl.ds(HALO, rows)], own_sem)
    own_copy.start()
    partial[...] = dot(feats[...], proj[...])
    inv = lax.rsqrt(jnp.full((8, 128), sigma[0] * sigma[0] + 4.0, f32))[0:1, 0:1]
    cx[3:8, pl.ds(HALO, rows)] = jnp.concatenate(
        [token[...].astype(f32), jnp.zeros((4, rows), f32)], axis=0
    )
    cx[0:3, pl.ds(HALO, rows)] = (true[...] + sigma[0] * noise[0]) * inv
    blocks = rows // PAIR_BLK
    for d in range(3):
        for b in range(blocks):
            wide[d * blocks + b : d * blocks + b + 1, :] = true[
                d : d + 1, b * PAIR_BLK : (b + 1) * PAIR_BLK
            ]
    wide[3 * blocks : 4 * blocks, :] = jnp.broadcast_to(counts[...].astype(f32), (blocks, PAIR_BLK))
    pay[...] = wide[...].astype(bf16)
    gathered[pl.ds(pl.multiple_of(me * pay_rows, pay_rows), pay_rows), :] = pay[...]
    pl.semaphore_wait(barrier, 7 + 2 * sample_peers + atom_peers - 3)

    def part_copy(step):
        peer = lax.rem(mine + step, sample_peers)
        at = pl.multiple_of(peer * share, share)
        return remote(
            partial.at[pl.ds(at, share)], arrived.at[step], part_send.at[step], part_recv.at[step],
            me, peer,
        )

    parts = [part_copy(step) for step in range(1, sample_peers)]
    for copy in parts:
        copy.start()
    near = [
        remote(single.at[pl.ds(rows - HALO, HALO)], single_ext.at[pl.ds(0, HALO)],
               near_send.at[0], near_recv.at[0], right, mine),
        remote(single.at[pl.ds(0, HALO)], single_ext.at[pl.ds(rows + HALO, HALO)],
               near_send.at[1], near_recv.at[1], left, mine),
        remote(cx.at[:, pl.ds(rows, HALO)], cx.at[:, pl.ds(0, HALO)],
               near_send.at[2], near_recv.at[2], right, mine),
        remote(cx.at[:, pl.ds(HALO, HALO)], cx.at[:, pl.ds(rows + HALO, HALO)],
               near_send.at[3], near_recv.at[3], left, mine),
    ]
    for copy in near:
        copy.start()
    for copy in parts:
        copy.wait_recv()
    total = partial[pl.ds(pl.multiple_of(mine * share, share), share), :]
    for step in range(1, sample_peers):
        total = total + arrived[step]
    slab[...] = total.astype(bf16)
    my_rows = pl.ds(pl.multiple_of(TOK_HALO + mine * share, 16), share)
    tok[my_rows, :] = slab[...]

    def tok_copy(step):
        return remote(
            slab, tok.at[my_rows], tok_send.at[step], tok_recv.at[step],
            me, lax.rem(mine + step, sample_peers),
        )

    toks = [tok_copy(step) for step in range(1, sample_peers)]
    for copy in toks:
        copy.start()
    tokens = tok.shape[0] - 2 * TOK_HALO
    half = TOK_HALO - share
    edges = (
        (sample_peers - 1, pl.ds(0, share), pl.ds(half, share), right),
        (sample_peers - 2, pl.ds(share - half, half), pl.ds(0, half), right),
        (0, pl.ds(0, share), pl.ds(TOK_HALO + tokens, share), left),
        (1, pl.ds(0, half), pl.ds(TOK_HALO + tokens + share, half), left),
    )

    def edge_copy(i, step):
        _, src, dst, to = edges[i]
        return remote(
            slab.at[src], tok.at[dst], edge_send.at[step], edge_recv.at[i],
            to, lax.rem(mine + step, sample_peers),
        )

    for i, edge in enumerate(edges):
        @pl.when(mine == edge[0])
        def _(i=i):
            for step in range(sample_peers):
                edge_copy(i, step).start()

    def all_copy(step):
        at = pl.ds(pl.multiple_of(me * pay_rows, pay_rows), pay_rows)
        return remote(
            pay, gathered.at[at], all_send.at[step], all_recv.at[step],
            lax.rem(me + step, atom_peers), mine,
        )

    @pl.loop(1, atom_peers)
    def _(step):
        all_copy(step).start()

    for copy in parts:
        copy.wait_send()
    for copy in near:
        copy.wait()
    for copy in toks:
        copy.wait()
    for i, edge in enumerate(edges):
        edge_copy(i, 0).wait_recv()

        @pl.when(mine == edge[0])
        def _(i=i):
            for step in range(sample_peers):
                edge_copy(i, step).wait_send()

    @pl.loop(1, atom_peers)
    def _(step):
        all_copy(step).wait()

    own_copy.wait()


def spread_kernel(atom_peers, pay, gathered, send, recv):
    me = lax.axis_index("atoms")
    mine = lax.axis_index("samples")
    rows = pay.shape[0]
    barrier = pltpu.get_barrier_semaphore()

    @pl.loop(1, atom_peers)
    def _(step):
        pl.semaphore_signal(
            barrier, inc=1, device_id=(lax.rem(me + step, atom_peers), mine), device_id_type=MESH
        )

    at = pl.ds(pl.multiple_of(me * rows, rows), rows)
    gathered[at, :] = pay[...]
    pl.semaphore_wait(barrier, atom_peers - 1)

    def copy(step):
        return remote(
            pay, gathered.at[at], send.at[step], recv.at[step], lax.rem(me + step, atom_peers), mine
        )

    @pl.loop(1, atom_peers)
    def _(step):
        copy(step).start()

    @pl.loop(1, atom_peers)
    def _(step):
        copy(step).wait()


def vmem(n):
    return [pl.BlockSpec(memory_space=pltpu.VMEM)] * n


def smem(n):
    return [pl.BlockSpec(memory_space=pltpu.SMEM)] * n


def run_atoms(place, scal, single, cx, tok, coord_in, w_qkv, w_o, w_gu, w_down, gains, w_out):
    ext = single.shape[0]
    rows = ext - 2 * HALO
    c3 = jnp.pad(coord_in, ((0, 5), (0, 0)))
    hi, mid, lo = (lax.reduce_precision(c3, 8, 7), None, None)
    rest = c3 - hi
    mid = lax.reduce_precision(rest, 8, 7)
    lo = rest - mid
    coord_w = jnp.concatenate([hi, mid, lo, hi, mid, hi], axis=0).astype(bf16)
    gains8 = jnp.pad(gains.reshape(2 * LAYERS, CHANNELS), ((0, 2), (0, 0)))
    wout8 = jnp.pad(w_out.T, ((0, 5), (0, 0)))
    return pl.pallas_call(
        atoms_kernel,
        name="atoms",
        out_shape=(
            jax.ShapeDtypeStruct((8, rows), f32),
            jax.ShapeDtypeStruct((3 * (rows // PAIR_BLK), PAIR_BLK), bf16),
        ),
        in_specs=smem(2) + vmem(10),
        out_specs=tuple(vmem(2)),
        scratch_shapes=[
            pltpu.VMEM((ext, CHANNELS), f32),
            pltpu.VMEM((2, ext, 3 * CHANNELS), bf16),
            pltpu.VMEM((ext, CHANNELS), f32),
            pltpu.VMEM((3 * (rows // PAIR_BLK), PAIR_BLK), f32),
        ],
        compiler_params=pltpu.CompilerParams(vmem_limit_bytes=VMEM_LIMIT),
    )(place, scal, single, cx, tok, coord_w, w_qkv, w_o, w_gu, w_down, gains8, wout8)


def run_pairs(scal, counts, partners, gathered_pred, gathered_true, pred, true):
    rows = pred.shape[1]
    wides = [pltpu.VMEM(g.shape, f32) for g in (gathered_pred, gathered_true)]
    out = jax.ShapeDtypeStruct((1, 3, rows), f32)
    return pl.pallas_call(
        pairs_kernel,
        name="pairs",
        out_shape=(out, out),
        in_specs=smem(3) + vmem(4),
        out_specs=tuple(vmem(2)),
        scratch_shapes=wides,
        compiler_params=pltpu.CompilerParams(vmem_limit_bytes=VMEM_LIMIT),
    )(scal, counts, partners, gathered_pred, gathered_true, pred, true)


def share(sigma, feats, proj, single, token, true, noise, counts):
    atom_peers, sample_peers = lax.axis_size("atoms"), lax.axis_size("samples")
    rows, tokens = single.shape[0], feats.shape[0]
    blocks = rows // PAIR_BLK
    part = tokens // sample_peers
    dma = pltpu.SemaphoreType.DMA
    return pl.pallas_call(
        functools.partial(share_kernel, atom_peers, sample_peers),
        name="share",
        out_shape=(
            jax.ShapeDtypeStruct((tokens + 2 * TOK_HALO, CHANNELS), bf16),
            jax.ShapeDtypeStruct((rows + 2 * HALO, CHANNELS), bf16),
            jax.ShapeDtypeStruct((8, rows + 2 * HALO), f32),
            jax.ShapeDtypeStruct((atom_peers * 4 * blocks, PAIR_BLK), bf16),
        ),
        in_specs=smem(1) + vmem(7),
        out_specs=tuple(vmem(4)),
        scratch_shapes=[
            pltpu.VMEM((tokens, CHANNELS), f32),
            pltpu.VMEM((sample_peers, part, CHANNELS), f32),
            pltpu.VMEM((part, CHANNELS), bf16),
            pltpu.VMEM((4 * blocks, PAIR_BLK), bf16),
            pltpu.VMEM((4 * blocks, PAIR_BLK), f32),
            dma((sample_peers,)), dma((sample_peers,)), dma((sample_peers,)), dma((sample_peers,)),
            dma((sample_peers,)), dma((4,)), dma((4,)), dma((4,)),
            dma((atom_peers,)), dma((atom_peers,)), dma,
        ],
        compiler_params=pltpu.CompilerParams(
            collective_id=0, has_side_effects=True, vmem_limit_bytes=VMEM_LIMIT
        ),
    )(sigma, feats, proj, single, token, true, noise, counts)


def spread(pay):
    atom_peers = lax.axis_size("atoms")
    dma = pltpu.SemaphoreType.DMA
    return pl.pallas_call(
        functools.partial(spread_kernel, atom_peers),
        name="spread",
        out_shape=jax.ShapeDtypeStruct((atom_peers * pay.shape[0], pay.shape[1]), pay.dtype),
        in_specs=vmem(1),
        out_specs=vmem(1)[0],
        scratch_shapes=[dma((atom_peers,)), dma((atom_peers,))],
        compiler_params=pltpu.CompilerParams(
            collective_id=1, has_side_effects=True, vmem_limit_bytes=VMEM_LIMIT
        ),
    )(pay)


def on_device(
    token_feats, proj_w, atom_single, atom_token, true_coords, noise, sigma, coord_in,
    w_qkv, w_o, w_gu, w_down, gains, w_out, pair_blocks, pair_count,
):
    rank = lax.axis_index("atoms")
    rows = atom_single.shape[0]
    tok, single, cx, gathered_true = share(
        sigma, token_feats, proj_w, atom_single, atom_token[None], true_coords, noise,
        pair_count[:, None],
    )
    sig = sigma[0]
    noise_total = sig * sig + 4.0
    root = jnp.sqrt(noise_total)
    place = jnp.stack(
        [rank * rows, jnp.int32(rows * lax.axis_size("atoms")), rank * token_feats.shape[0]]
    ).astype(jnp.int32)
    scal = jnp.stack([4.0 / root, 2.0 * sig / root])
    pred, pay = run_atoms(
        place, scal, single, cx, tok, coord_in, w_qkv, w_o, w_gu, w_down, gains, w_out
    )
    gathered_pred = spread(pay)
    scal2 = (2.0 / 3.0 * noise_total / (2.0 * sig) ** 2)[None]
    return run_pairs(
        scal2, pair_count, pair_blocks, gathered_pred, gathered_true, pred, true_coords
    )


def solution(mesh):
    in_specs = (
        P("atoms", "samples"),
        P("samples", None),
        P("atoms", None),
        P("atoms"),
        P(None, "atoms"),
        P("samples", None, "atoms"),
        P("samples"),
        P(), P(), P(), P(), P(), P(), P(),
        P("atoms", None),
        P("atoms"),
    )
    out_specs = (P("samples", None, "atoms"), P("samples", None, "atoms"))
    return jax.shard_map(on_device, mesh=mesh, in_specs=in_specs, out_specs=out_specs, check_vma=False)
```

```python
import functools
import math

import jax
import jax.numpy as jnp
from jax import lax
from jax.experimental import pallas as pl
from jax.experimental.pallas import tpu as pltpu
from jax.sharding import PartitionSpec as P

HEADS = 4
HEAD_DIM = 32
FF_ATOM = 256
LAYERS = 3
QBLK = 32
KWIN = 128
PAIR_BLK = 128
CHANNELS = 128
CHUNK = 256
SIZE = 768
SIZE_LAST = 1024
FIRST_UNROLL = 5
UNROLL = 8
HALO = 256
TOK_HALO = 48
TOK_WIN = 64
EPS = 1e-05
VMEM_LIMIT = 56 * 1024 * 1024

f32 = jnp.float32
bf16 = jnp.bfloat16


def dot(a, b, dims=((1,), (0,)), precision=None):
    return lax.dot_general(a, b, (dims, ((), ())), precision=precision, preferred_element_type=f32)


def pieces(v):
    hi = v.astype(bf16).astype(f32)
    mid = (v - hi).astype(bf16).astype(f32)
    lo = (v - hi - mid).astype(bf16).astype(f32)
    return hi, mid, lo


def rms_scale(h):
    return h * lax.rsqrt(jnp.mean(h * h, axis=1, keepdims=True) + EPS)


def atoms_kernel(
    place, sigma, single, cx, tok, coord_in, wqkv, wo, wgu, wdown, gains, wout,
    pred, pay, hid, kv, queries, bias, wide,
):
    rows = single.shape[0] - 2 * HALO
    ext = single.shape[0]
    first_atom = place[0]
    total_atoms = place[1]
    first_tok = place[2]
    sig = sigma[0]
    inv = lax.rsqrt(jnp.full((8, CHANNELS), sig * sig + 4.0, f32))[0:1, 0:1]
    zero5 = jnp.zeros((5, CHANNELS), f32)
    hi, mid, lo = pieces(jnp.concatenate([coord_in[...], zero5], axis=0))
    coord_w = jnp.concatenate([hi, mid, lo, hi, mid, hi], axis=0).astype(bf16)
    head = jnp.concatenate([wout[...], zero5], axis=0)
    q_scale = math.log2(math.e) / math.sqrt(HEAD_DIM)
    lane = lax.broadcasted_iota(jnp.int32, (1, CHANNELS), 1) // HEAD_DIM

    pos = first_atom - HALO + lax.broadcasted_iota(jnp.int32, (ext, CHANNELS), 0)
    bias[...] = jnp.where((pos >= 0) & (pos < total_atoms), 0.0, -1e30)

    def project(layer, at, h):
        normed = (rms_scale(h) * gains[layer, 0:1, :]).astype(bf16)
        out = dot(normed, wqkv[layer])
        rows_at = pl.ds(at, h.shape[0])
        kv[layer % 2, rows_at, :] = out[:, 128:].astype(bf16)
        for t in range(h.shape[0] // CHANNELS):
            turned = (out[t * CHANNELS : (t + 1) * CHANNELS, :128] * q_scale).T
            shifted = [turned if r == 0 else pltpu.roll(turned, r * QBLK, 1) for r in range(HEADS)]
            for w in range(CHANNELS // QBLK):
                spread = jnp.concatenate(
                    [
                        jnp.where(lane == h, shifted[(h - w) % HEADS][h * QBLK : (h + 1) * QBLK], 0.0)
                        for h in range(HEADS)
                    ],
                    axis=0,
                )
                queries[layer % 2, at // QBLK + t * HEADS + w] = spread.astype(bf16)

    def first(k, _):
        at = pl.multiple_of(k * CHUNK, CHUNK)
        c = cx[:, pl.ds(at, CHUNK)]
        hi, mid, lo = pieces(c)
        rel = c[3:4, :].astype(jnp.int32) - (first_tok - TOK_HALO + k * (CHUNK // 8))
        hot = jnp.where(lax.broadcasted_iota(jnp.int32, (TOK_WIN, CHUNK), 0) == rel, 1.0, 0.0)
        left = jnp.concatenate([hot, hi, hi, hi, mid, mid, lo], axis=0).astype(bf16)
        tok_at = pl.ds(pl.multiple_of(k * (CHUNK // 8), CHUNK // 8), TOK_WIN)
        right = jnp.concatenate([tok[tok_at, :], coord_w], axis=0)
        h = single[pl.ds(at, CHUNK), :].astype(f32) + dot(left, right, ((0,), (0,)))
        hid[pl.ds(at, CHUNK), :] = h
        project(0, at, h)
        return 0

    lax.fori_loop(0, ext // CHUNK, first, 0, unroll=FIRST_UNROLL)

    def attend(layer, at, size):
        buf = layer % 2
        outs = []
        for w in range(size // QBLK):
            keys_at = pl.ds(at + (w * QBLK - 48), KWIN)
            keys = kv[buf, keys_at, 0:128]
            values = kv[buf, keys_at, 128:256]
            scores = dot(keys, queries[buf, at // QBLK + w]) + bias[keys_at, :]
            top = jnp.max(scores, axis=0, keepdims=True)
            weights = jnp.exp2(scores - top)
            weights = (weights * (1.0 / jnp.sum(weights, axis=0, keepdims=True))).astype(bf16)
            both = dot(weights, values, ((0,), (0,)))
            out = both[0:QBLK]
            for h in range(1, HEADS):
                out = jnp.where(lane == h, both[h * QBLK : (h + 1) * QBLK], out)
            outs.append(out.astype(bf16))
        return jnp.concatenate(outs, axis=0)

    def block(layer, at, size):
        h = hid[pl.ds(at, size), :]
        h = h + dot(attend(layer, at, size), wo[layer])
        normed = (rms_scale(h) * gains[layer, 1:2, :]).astype(bf16)
        gu = dot(normed, wgu[layer])
        half = 0.5 * gu[:, :FF_ATOM]
        inner = (half * (1.0 + jnp.tanh(half)) * gu[:, FF_ATOM:]).astype(bf16)
        h = h + dot(inner, wdown[layer])
        if layer + 1 < LAYERS:
            hid[pl.ds(at, size), :] = h
            project(layer + 1, at, h)
        else:
            update = dot(head, rms_scale(h), ((1,), (1,)), lax.Precision.HIGHEST)
            noisy = cx[:, pl.ds(at, size)]
            out = inv * (4.0 * noisy + (2.0 * sig) * update)
            pred[:, pl.ds(pl.multiple_of(at - HALO, 128), size)] = out
            first_block = (at - HALO) // PAIR_BLK
            for i in range(size // PAIR_BLK):
                for d in range(3):
                    row = pl.ds(d * (rows // PAIR_BLK) + first_block + i, 1)
                    wide[row, :] = out[d : d + 1, i * PAIR_BLK : (i + 1) * PAIR_BLK]

    for layer in range(LAYERS):
        low = HALO if layer == LAYERS - 1 else HALO - 128
        span = rows if layer == LAYERS - 1 else rows + 256
        size = SIZE_LAST if layer == LAYERS - 1 else SIZE

        def step(k, _, layer=layer, low=low, size=size):
            block(layer, pl.multiple_of(low + k * size, 128), size)
            return 0

        lax.fori_loop(0, span // size, step, 0)
    pay[...] = wide[...].astype(bf16)


def pairs_kernel(
    sigma, counts, partners, gathered_pred, gathered_true, pred, true,
    coord_grad, lddt_grad, wide_pred, wide_true, owns, totals,
):
    blocks = counts.shape[0]
    wide_pred[...] = gathered_pred[...].astype(f32)
    wide_true[...] = gathered_true[...].astype(f32)
    peers = gathered_pred.shape[0] // (3 * blocks)
    listed = jnp.zeros((blocks, PAIR_BLK), f32)
    for peer in range(peers):
        listed = listed + wide_true[peer * 4 * blocks + 3 * blocks : (peer + 1) * 4 * blocks, :]
    listed = jnp.sum(listed, axis=0, keepdims=True)
    total_pairs = listed * (PAIR_BLK * PAIR_BLK) - float(PAIR_BLK * blocks * peers)
    pair_scale = -0.0625 * (blocks * peers * PAIR_BLK * PAIR_BLK) / total_pairs
    row8 = lax.broadcasted_iota(jnp.int32, (8, PAIR_BLK), 0)
    row4 = row8 & 3
    diff = lax.broadcasted_iota(jnp.int32, (PAIR_BLK, PAIR_BLK), 0) - lax.broadcasted_iota(
        jnp.int32, (PAIR_BLK, PAIR_BLK), 1
    )

    def partner_rows(p):
        base = p // blocks * (4 * blocks) + p % blocks
        x, y, z = (wide_true[pl.ds(base + d * blocks, 1), :] for d in range(3))
        n1, n2, n3 = pieces(x * x + y * y + z * z)
        xyz = jnp.where(row4 == 0, x, jnp.where(row4 == 1, y, z))
        upper = jnp.where(row4 == 3, jnp.where(row8 == 3, n1, n2), xyz)
        ones = jnp.where(row8 < 7, 1.0, 0.0)
        lower = jnp.where(row8 < 3, xyz, jnp.where(row8 == 3, n3, ones))
        base = p // blocks * (3 * blocks) + p % blocks
        x, y, z = (wide_pred[pl.ds(base + d * blocks, 1), :] for d in range(3))
        xyz = jnp.where(row8 == 0, x, jnp.where(row8 == 1, y, jnp.where(row8 == 2, z, 0.0)))
        return jnp.concatenate([upper, lower, xyz, jnp.zeros_like(xyz)], axis=0).astype(bf16)

    def own_square(x, y, z):
        n1, n2, n3 = pieces(0.25 * (x * x + y * y + z * z + 1.0))
        xp, yp, zp = pieces(-0.5 * x), pieces(-0.5 * y), pieces(-0.5 * z)

        def xyz(i):
            return jnp.where(row4 == 0, xp[i], jnp.where(row4 == 1, yp[i], zp[i]))

        upper = jnp.where(row4 == 3, 0.25, jnp.where(row8 < 4, xyz(0), xyz(1)))
        norms = jnp.where(row8 == 4, n1, jnp.where(row8 == 5, n2, n3))
        norms = jnp.where(row8 == 7, 0.0, norms)
        lower = jnp.where(row8 < 3, xyz(2), jnp.where(row8 == 3, 0.25, norms))
        zero = jnp.zeros_like(lower)
        return jnp.concatenate([upper, lower, zero, zero], axis=0)

    def own_gap(d, x):
        hi, mid, lo = pieces(-0.5 * x)
        zero = jnp.zeros((8, PAIR_BLK), f32)
        lower = jnp.where(row8 == 4, hi, jnp.where(row8 == 5, mid, jnp.where(row8 == 6, lo, 0.0)))
        pick = jnp.where(row8 == d, 0.5, 0.0)
        return jnp.concatenate([zero, lower, pick, zero], axis=0)

    square = sigma[0] * sigma[0]
    mse_scale = jnp.full((1, PAIR_BLK), square + 4.0, f32) / jnp.full((1, PAIR_BLK), 6.0 * square, f32)
    totals[...] = jnp.zeros_like(totals)
    owns[blocks] = jnp.zeros(owns.shape[1:], bf16) + 1.0
    for b in range(blocks):
        at = slice(b * PAIR_BLK, (b + 1) * PAIR_BLK)
        owns[b] = jnp.concatenate(
            [own_square(*(true[d : d + 1, at] for d in range(3)))]
            + [own_gap(d, pred[d : d + 1, at]) for d in range(3)],
            axis=1,
        ).astype(bf16)

    def tile(b, m):
        known = jnp.minimum(b, blocks - 1)
        p = partners[known, m]
        found = dot(partner_rows(p), owns[b], ((0,), (0,)))
        st, gx, gy, gz = (found[:, i * PAIR_BLK : (i + 1) * PAIR_BLK] for i in range(4))
        sp = gx * gx + gy * gy + gz * gz + 0.25
        rp = lax.rsqrt(sp)
        gap = sp * rp - st * lax.rsqrt(st)
        e2 = gap * gap + 0.0025
        re = lax.rsqrt(e2)
        err = e2 * re
        th = [jnp.tanh(0.5 * t - err) for t in (0.5, 1.0, 2.0, 4.0)]
        slope = 4.0 - (th[0] * th[0] + th[1] * th[1] + th[2] * th[2] + th[3] * th[3])
        coef = slope * gap * (re * rp)
        shut = jnp.where(m == 0, 0, 2 * PAIR_BLK)
        coef = jnp.where(diff == shut, 0.0, coef)
        sums = jnp.concatenate(
            [jnp.sum((coef * g).reshape(16, 8, PAIR_BLK), axis=0) for g in (gx, gy, gz)], axis=0
        )
        last = m + 1 >= counts[known]
        return sums, jnp.where(last, jnp.minimum(b + 1, blocks), b), jnp.where(last, 0, m + 1)

    def visit(_, place):
        b, m = place
        found = []
        for _ in range(UNROLL):
            sums, after, then = tile(b, m)
            found.append((b, sums))
            b, m = after, then
        for at, sums in found:
            totals[at] = totals[at] + sums
        return b, m

    live = counts[0]
    for b in range(1, blocks):
        live = live + counts[b]
    lax.fori_loop(0, (live + UNROLL - 1) // UNROLL, visit, (jnp.int32(0), jnp.int32(0)))

    for b in range(blocks):
        at = slice(b * PAIR_BLK, (b + 1) * PAIR_BLK)
        total = totals[b]
        for d in range(3):
            pc, tc = pred[d : d + 1, at], true[d : d + 1, at]
            lg = (-2.0 * pair_scale) * jnp.sum(total[8 * d : 8 * d + 8], axis=0, keepdims=True)
            lddt_grad[d, :, at] = lg
            coord_grad[d, :, at] = mse_scale * (pc - tc) - lg * (1.0 / PAIR_BLK)


MESH = pl.DeviceIdType.MESH


def remote(src, dst, send, recv, atom, sample):
    return pltpu.make_async_remote_copy(
        src_ref=src, dst_ref=dst, send_sem=send, recv_sem=recv,
        device_id=(atom, sample), device_id_type=MESH,
    )


def share_kernel(
    atom_peers, sample_peers, sigma, counts, feats, proj, single, token, true, noise,
    tok, single_ext, cx, gathered,
    partial, arrived, slab, pay, wide,
    part_send, part_recv, tok_send, tok_recv, edge_send, edge_recv, near_send, near_recv,
    all_send, all_recv, own_sem,
):
    me = lax.axis_index("atoms")
    mine = lax.axis_index("samples")
    right = lax.rem(me + 1, atom_peers)
    left = lax.rem(me + atom_peers - 1, atom_peers)
    rows = single.shape[0]
    share = feats.shape[1] // sample_peers
    pay_rows = pay.shape[0]

    barrier = pltpu.get_barrier_semaphore()

    def greet(atom, sample):
        pl.semaphore_signal(barrier, inc=1, device_id=(atom, sample), device_id_type=MESH)

    for step in range(1, sample_peers):
        greet(me, lax.rem(mine + step, sample_peers))
    for step in range(sample_peers):
        greet(left, lax.rem(mine + step, sample_peers))
        greet(right, lax.rem(mine + step, sample_peers))

    @pl.loop(2, atom_peers - 1)
    def _(step):
        greet(lax.rem(me + step, atom_peers), mine)

    own_copy = pltpu.make_async_copy(single, single_ext.at[pl.ds(HALO, rows)], own_sem)
    own_copy.start()
    partial[...] = dot(feats[...], proj[...], ((0,), (0,)))
    inv = lax.rsqrt(jnp.full((8, 128), sigma[0] * sigma[0] + 4.0, f32))[0:1, 0:1]
    cx[3:8, pl.ds(HALO, rows)] = jnp.concatenate(
        [token[...].astype(f32), jnp.zeros((4, rows), f32)], axis=0
    )
    for d in range(3):
        cx[d : d + 1, pl.ds(HALO, rows)] = (true[d : d + 1, :] + sigma[0] * noise[d]) * inv
    blocks = rows // PAIR_BLK
    for d in range(3):
        for b in range(blocks):
            wide[d * blocks + b : d * blocks + b + 1, :] = true[
                d : d + 1, b * PAIR_BLK : (b + 1) * PAIR_BLK
            ]
    for b in range(blocks):
        wide[3 * blocks + b : 3 * blocks + b + 1, :] = jnp.full((1, PAIR_BLK), counts[b], jnp.int32).astype(f32)
    pay[...] = wide[...].astype(bf16)
    gathered[pl.ds(pl.multiple_of(me * pay_rows, pay_rows), pay_rows), :] = pay[...]
    pl.semaphore_wait(barrier, 7 + 2 * sample_peers + atom_peers - 3)

    def part_copy(step):
        peer = lax.rem(mine + step, sample_peers)
        at = pl.multiple_of(peer * share, share)
        return remote(
            partial.at[pl.ds(at, share)], arrived.at[step], part_send.at[step], part_recv.at[step],
            me, peer,
        )

    parts = [part_copy(step) for step in range(1, sample_peers)]
    for copy in parts:
        copy.start()
    near = [
        remote(single.at[pl.ds(rows - HALO, HALO)], single_ext.at[pl.ds(0, HALO)],
               near_send.at[0], near_recv.at[0], right, mine),
        remote(single.at[pl.ds(0, HALO)], single_ext.at[pl.ds(rows + HALO, HALO)],
               near_send.at[1], near_recv.at[1], left, mine),
        remote(cx.at[:, pl.ds(rows, HALO)], cx.at[:, pl.ds(0, HALO)],
               near_send.at[2], near_recv.at[2], right, mine),
        remote(cx.at[:, pl.ds(HALO, HALO)], cx.at[:, pl.ds(rows + HALO, HALO)],
               near_send.at[3], near_recv.at[3], left, mine),
    ]
    for copy in near:
        copy.start()
    for copy in parts:
        copy.wait_recv()
    total = partial[pl.ds(pl.multiple_of(mine * share, share), share), :]
    for step in range(1, sample_peers):
        total = total + arrived[step]
    slab[...] = total.astype(bf16)
    my_rows = pl.ds(pl.multiple_of(TOK_HALO + mine * share, 16), share)
    tok[my_rows, :] = slab[...]

    def tok_copy(step):
        return remote(
            slab, tok.at[my_rows], tok_send.at[step], tok_recv.at[step],
            me, lax.rem(mine + step, sample_peers),
        )

    toks = [tok_copy(step) for step in range(1, sample_peers)]
    for copy in toks:
        copy.start()
    tokens = tok.shape[0] - 2 * TOK_HALO
    half = TOK_HALO - share
    edges = (
        (sample_peers - 1, pl.ds(0, share), pl.ds(half, share), right),
        (sample_peers - 2, pl.ds(share - half, half), pl.ds(0, half), right),
        (0, pl.ds(0, share), pl.ds(TOK_HALO + tokens, share), left),
        (1, pl.ds(0, half), pl.ds(TOK_HALO + tokens + share, half), left),
    )

    def edge_copy(i, step):
        _, src, dst, to = edges[i]
        return remote(
            slab.at[src], tok.at[dst], edge_send.at[step], edge_recv.at[i],
            to, lax.rem(mine + step, sample_peers),
        )

    for i, edge in enumerate(edges):
        @pl.when(mine == edge[0])
        def _(i=i):
            for step in range(sample_peers):
                edge_copy(i, step).start()

    def all_copy(step):
        at = pl.ds(pl.multiple_of(me * pay_rows, pay_rows), pay_rows)
        return remote(
            pay, gathered.at[at], all_send.at[step], all_recv.at[step],
            lax.rem(me + step, atom_peers), mine,
        )

    @pl.loop(1, atom_peers)
    def _(step):
        all_copy(step).start()

    for copy in parts:
        copy.wait_send()
    for copy in near:
        copy.wait()
    for copy in toks:
        copy.wait()
    for i, edge in enumerate(edges):
        edge_copy(i, 0).wait_recv()

        @pl.when(mine == edge[0])
        def _(i=i):
            for step in range(sample_peers):
                edge_copy(i, step).wait_send()

    @pl.loop(1, atom_peers)
    def _(step):
        all_copy(step).wait()

    own_copy.wait()


def spread_kernel(atom_peers, pay, gathered, send, recv):
    me = lax.axis_index("atoms")
    mine = lax.axis_index("samples")
    rows = pay.shape[0]
    barrier = pltpu.get_barrier_semaphore()

    @pl.loop(1, atom_peers)
    def _(step):
        pl.semaphore_signal(
            barrier, inc=1, device_id=(lax.rem(me + step, atom_peers), mine), device_id_type=MESH
        )

    at = pl.ds(pl.multiple_of(me * rows, rows), rows)
    gathered[at, :] = pay[...]
    pl.semaphore_wait(barrier, atom_peers - 1)

    def copy(step):
        return remote(
            pay, gathered.at[at], send.at[step], recv.at[step], lax.rem(me + step, atom_peers), mine
        )

    @pl.loop(1, atom_peers)
    def _(step):
        copy(step).start()

    @pl.loop(1, atom_peers)
    def _(step):
        copy(step).wait()


def vmem(n):
    return [pl.BlockSpec(memory_space=pltpu.VMEM)] * n


def smem(n):
    return [pl.BlockSpec(memory_space=pltpu.SMEM)] * n


def run_atoms(place, sigma, single, cx, tok, coord_in, w_qkv, w_o, w_gu, w_down, gains, w_out):
    ext = single.shape[0]
    rows = ext - 2 * HALO
    return pl.pallas_call(
        atoms_kernel,
        name="atoms",
        out_shape=(
            jax.ShapeDtypeStruct((8, rows), f32),
            jax.ShapeDtypeStruct((3 * (rows // PAIR_BLK), PAIR_BLK), bf16),
        ),
        in_specs=smem(2) + vmem(10),
        out_specs=tuple(vmem(2)),
        scratch_shapes=[
            pltpu.VMEM((ext, CHANNELS), f32),
            pltpu.VMEM((2, ext, 2 * CHANNELS), bf16),
            pltpu.VMEM((2, ext // QBLK, CHANNELS, CHANNELS), bf16),
            pltpu.VMEM((ext, CHANNELS), f32),
            pltpu.VMEM((3 * (rows // PAIR_BLK), PAIR_BLK), f32),
        ],
        compiler_params=pltpu.CompilerParams(vmem_limit_bytes=VMEM_LIMIT),
    )(place, sigma, single, cx, tok, coord_in, w_qkv, w_o, w_gu, w_down, gains, w_out.T)


def run_pairs(sigma, counts, partners, gathered_pred, gathered_true, pred, true):
    rows = pred.shape[1]
    wides = [pltpu.VMEM(g.shape, f32) for g in (gathered_pred, gathered_true)]
    out = jax.ShapeDtypeStruct((3, 1, rows), f32)
    coord_grad, lddt_grad = pl.pallas_call(
        pairs_kernel,
        name="pairs",
        out_shape=(out, out),
        in_specs=smem(3) + vmem(4),
        out_specs=tuple(vmem(2)),
        scratch_shapes=wides
        + [
            pltpu.VMEM((rows // PAIR_BLK + 1, 32, 4 * PAIR_BLK), bf16),
            pltpu.VMEM((rows // PAIR_BLK + 1, 24, PAIR_BLK), f32),
        ],
        compiler_params=pltpu.CompilerParams(vmem_limit_bytes=VMEM_LIMIT),
    )(sigma, counts, partners, gathered_pred, gathered_true, pred, true)
    return jnp.swapaxes(coord_grad, 0, 1), jnp.swapaxes(lddt_grad, 0, 1)


def share(sigma, feats, proj, single, token, true, noise, counts):
    atom_peers, sample_peers = lax.axis_size("atoms"), lax.axis_size("samples")
    rows, tokens = single.shape[0], feats.shape[1]
    blocks = rows // PAIR_BLK
    part = tokens // sample_peers
    dma = pltpu.SemaphoreType.DMA
    return pl.pallas_call(
        functools.partial(share_kernel, atom_peers, sample_peers),
        name="share",
        out_shape=(
            jax.ShapeDtypeStruct((tokens + 2 * TOK_HALO, CHANNELS), bf16),
            jax.ShapeDtypeStruct((rows + 2 * HALO, CHANNELS), bf16),
            jax.ShapeDtypeStruct((8, rows + 2 * HALO), f32),
            jax.ShapeDtypeStruct((atom_peers * 4 * blocks, PAIR_BLK), bf16),
        ),
        in_specs=smem(2) + vmem(6),
        out_specs=tuple(vmem(4)),
        scratch_shapes=[
            pltpu.VMEM((tokens, CHANNELS), f32),
            pltpu.VMEM((sample_peers, part, CHANNELS), f32),
            pltpu.VMEM((part, CHANNELS), bf16),
            pltpu.VMEM((4 * blocks, PAIR_BLK), bf16),
            pltpu.VMEM((4 * blocks, PAIR_BLK), f32),
            dma((sample_peers,)), dma((sample_peers,)), dma((sample_peers,)), dma((sample_peers,)),
            dma((sample_peers,)), dma((4,)), dma((4,)), dma((4,)),
            dma((atom_peers,)), dma((atom_peers,)), dma,
        ],
        compiler_params=pltpu.CompilerParams(
            collective_id=0, has_side_effects=True, vmem_limit_bytes=VMEM_LIMIT
        ),
    )(sigma, counts, feats, proj, single, token, true, noise)


def spread(pay):
    atom_peers = lax.axis_size("atoms")
    dma = pltpu.SemaphoreType.DMA
    return pl.pallas_call(
        functools.partial(spread_kernel, atom_peers),
        name="spread",
        out_shape=jax.ShapeDtypeStruct((atom_peers * pay.shape[0], pay.shape[1]), pay.dtype),
        in_specs=vmem(1),
        out_specs=vmem(1)[0],
        scratch_shapes=[dma((atom_peers,)), dma((atom_peers,))],
        compiler_params=pltpu.CompilerParams(
            collective_id=1, has_side_effects=True, vmem_limit_bytes=VMEM_LIMIT
        ),
    )(pay)


def on_device(
    token_feats, proj_w, atom_single, atom_token, true_coords, noise, sigma, coord_in,
    w_qkv, w_o, w_gu, w_down, gains, w_out, pair_blocks, pair_count,
):
    rank = lax.axis_index("atoms")
    rows = atom_single.shape[0]
    tok, single, cx, gathered_true = share(
        sigma, token_feats.T, proj_w, atom_single, atom_token[None], true_coords,
        jnp.swapaxes(noise, 0, 1), pair_count,
    )
    place = jnp.stack(
        [rank * rows, jnp.int32(rows * lax.axis_size("atoms")), rank * token_feats.shape[0]]
    ).astype(jnp.int32)
    pred, pay = run_atoms(
        place, sigma, single, cx, tok, coord_in, w_qkv, w_o, w_gu, w_down, gains, w_out
    )
    gathered_pred = spread(pay)
    return run_pairs(
        sigma, pair_count, pair_blocks, gathered_pred, gathered_true, pred, true_coords
    )


def solution(mesh):
    in_specs = (
        P("atoms", "samples"),
        P("samples", None),
        P("atoms", None),
        P("atoms"),
        P(None, "atoms"),
        P("samples", None, "atoms"),
        P("samples"),
        P(), P(), P(), P(), P(), P(), P(),
        P("atoms", None),
        P("atoms"),
    )
    out_specs = (P("samples", None, "atoms"), P("samples", None, "atoms"))
    return jax.shard_map(on_device, mesh=mesh, in_specs=in_specs, out_specs=out_specs, check_vma=False)
```

```python
import functools
import math

import jax
import jax.numpy as jnp
from jax import lax
from jax.experimental import pallas as pl
from jax.experimental.pallas import tpu as pltpu
from jax.sharding import PartitionSpec as P

HEADS = 4
HEAD_DIM = 32
FF_ATOM = 256
LAYERS = 3
QBLK = 32
KWIN = 128
PAIR_BLK = 128
CHANNELS = 128
CHUNK = 256
SIZE = 768
SIZE_LAST = 1024
FIRST_UNROLL = 5
UNROLL = 8
HALO = 256
TOK_HALO = 48
TOK_WIN = 64
EPS = 1e-05
DEPTH = 8
VMEM_LIMIT = 56 * 1024 * 1024

f32 = jnp.float32
bf16 = jnp.bfloat16


def dot(a, b, dims=((1,), (0,)), precision=None):
    return lax.dot_general(a, b, (dims, ((), ())), precision=precision, preferred_element_type=f32)


def pieces(v):
    hi = v.astype(bf16).astype(f32)
    mid = (v - hi).astype(bf16).astype(f32)
    lo = (v - hi - mid).astype(bf16).astype(f32)
    return hi, mid, lo


def rms_scale(h):
    return h * lax.rsqrt(jnp.mean(h * h, axis=1, keepdims=True) + EPS)


MESH = pl.DeviceIdType.MESH


def remote(src, dst, send, recv, atom, sample):
    return pltpu.make_async_remote_copy(
        src_ref=src, dst_ref=dst, send_sem=send, recv_sem=recv,
        device_id=(atom, sample), device_id_type=MESH,
    )

def gather_plan(atom_peers):
    nz = DEPTH
    nx = atom_peers // nz
    me = lax.axis_index("atoms")
    x, z = me // nz, lax.rem(me, nz)

    def along_z(dz):
        return x * nz + lax.rem(z + dz + nz, nz)

    def along_x(dx):
        return lax.rem(x + dx, nx) * nz + z

    return nz, nx, me, along_z, along_x


class Gather:
    def __init__(self, atom_peers, pay, whole, sems):
        self.nz, self.nx, self.me, self.along_z, self.along_x = gather_plan(atom_peers)
        self.mine = lax.axis_index("samples")
        self.pay, self.whole = pay, whole
        self.z_send, self.z_recv, self.x_send, self.x_recv = sems
        self.order = [0]
        for step in range(1, self.nz // 2 + 1):
            self.order += [step, self.nz - step] if 2 * step != self.nz else [step]

    def rows(self, owner):
        size = self.pay.shape[0]
        return pl.ds(pl.multiple_of(owner * size, size), size)

    def z_copy(self, dz):
        return remote(
            self.pay, self.whole.at[self.rows(self.me)], self.z_send.at[dz], self.z_recv.at[dz],
            self.along_z(dz), self.mine,
        )

    def x_copy(self, dz, dx):
        at = self.rows(self.along_z(-dz))
        src = self.pay if dz == 0 else self.whole.at[at]
        slot = dz * self.nx + dx
        return remote(
            src, self.whole.at[at], self.x_send.at[slot], self.x_recv.at[slot],
            self.along_x(dx), self.mine,
        )

    def start(self):
        for dz in self.order[1:]:
            self.z_copy(dz).start()
        for dx in range(1, self.nx):
            self.x_copy(0, dx).start()
        self.whole[self.rows(self.me), :] = self.pay[...]

    def forward(self):
        for dz in self.order[1:]:
            self.z_copy(dz).wait_recv()
            for dx in range(1, self.nx):
                self.x_copy(dz, dx).start()

    def finish(self):
        for dz in self.order[1:]:
            self.z_copy(dz).wait_send()
        for dz in self.order:
            for dx in range(1, self.nx):
                self.x_copy(dz, dx).wait()


def atoms_kernel(
    atom_peers, sigma, counts, true, single, cx, tok, coord_in, wqkv, wo, wgu, wdown, gains, wout,
    pred, gathered_pred, gathered_true, hid, kv, queries, bias, pay, true_pay, wide, *sems,
):
    rows = single.shape[0] - 2 * HALO
    ext = single.shape[0]
    nz, nx, me, along_z, along_x = gather_plan(atom_peers)
    mine = lax.axis_index("samples")
    barrier = pltpu.get_barrier_semaphore()
    for dz in range(1, nz):
        pl.semaphore_signal(barrier, inc=1, device_id=(along_z(dz), mine), device_id_type=MESH)
    for dx in range(1, nx):
        pl.semaphore_signal(barrier, inc=1, device_id=(along_x(dx), mine), device_id_type=MESH)
    first_atom = me * rows
    total_atoms = rows * atom_peers
    first_tok = me * (tok.shape[0] - 2 * TOK_HALO)
    blocks = rows // PAIR_BLK
    for d in range(3):
        for b in range(blocks):
            wide[d * blocks + b : d * blocks + b + 1, :] = true[
                d : d + 1, b * PAIR_BLK : (b + 1) * PAIR_BLK
            ]
    for b in range(blocks):
        wide[3 * blocks + b : 3 * blocks + b + 1, :] = jnp.full((1, PAIR_BLK), counts[b], jnp.int32).astype(f32)
    true_pay[...] = wide[...].astype(bf16)
    pl.semaphore_wait(barrier, nz + nx - 2)
    true_gather = Gather(atom_peers, true_pay, gathered_true, sems[:4])
    pred_gather = Gather(atom_peers, pay, gathered_pred, sems[4:])
    true_gather.start()
    sig = sigma[0]
    inv = lax.rsqrt(jnp.full((8, CHANNELS), sig * sig + 4.0, f32))[0:1, 0:1]
    zero5 = jnp.zeros((5, CHANNELS), f32)
    hi, mid, lo = pieces(jnp.concatenate([coord_in[...], zero5], axis=0))
    coord_w = jnp.concatenate([hi, mid, lo, hi, mid, hi], axis=0).astype(bf16)
    head = jnp.concatenate([wout[...], zero5], axis=0)
    q_scale = math.log2(math.e) / math.sqrt(HEAD_DIM)
    lane = lax.broadcasted_iota(jnp.int32, (1, CHANNELS), 1) // HEAD_DIM

    pos = first_atom - HALO + lax.broadcasted_iota(jnp.int32, (ext, CHANNELS), 0)
    bias[...] = jnp.where((pos >= 0) & (pos < total_atoms), 0.0, -1e30)

    def project(layer, at, h):
        normed = (rms_scale(h) * gains[layer, 0:1, :]).astype(bf16)
        out = dot(normed, wqkv[layer])
        rows_at = pl.ds(at, h.shape[0])
        kv[layer % 2, rows_at, :] = out[:, 128:].astype(bf16)
        for t in range(h.shape[0] // CHANNELS):
            turned = (out[t * CHANNELS : (t + 1) * CHANNELS, :128] * q_scale).T
            shifted = [turned if r == 0 else pltpu.roll(turned, r * QBLK, 1) for r in range(HEADS)]
            for w in range(CHANNELS // QBLK):
                spread = jnp.concatenate(
                    [
                        jnp.where(lane == h, shifted[(h - w) % HEADS][h * QBLK : (h + 1) * QBLK], 0.0)
                        for h in range(HEADS)
                    ],
                    axis=0,
                )
                queries[layer % 2, at // QBLK + t * HEADS + w] = spread.astype(bf16)

    def first(k, _):
        at = pl.multiple_of(k * CHUNK, CHUNK)
        c = cx[:, pl.ds(at, CHUNK)]
        hi, mid, lo = pieces(c)
        rel = c[3:4, :].astype(jnp.int32) - (first_tok - TOK_HALO + k * (CHUNK // 8))
        hot = jnp.where(lax.broadcasted_iota(jnp.int32, (TOK_WIN, CHUNK), 0) == rel, 1.0, 0.0)
        left = jnp.concatenate([hot, hi, hi, hi, mid, mid, lo], axis=0).astype(bf16)
        tok_at = pl.ds(pl.multiple_of(k * (CHUNK // 8), CHUNK // 8), TOK_WIN)
        right = jnp.concatenate([tok[tok_at, :], coord_w], axis=0)
        h = single[pl.ds(at, CHUNK), :].astype(f32) + dot(left, right, ((0,), (0,)))
        hid[pl.ds(at, CHUNK), :] = h
        project(0, at, h)
        return 0

    lax.fori_loop(0, ext // CHUNK, first, 0, unroll=FIRST_UNROLL)

    true_gather.forward()

    def attend(layer, at, size):
        buf = layer % 2
        outs = []
        for w in range(size // QBLK):
            keys_at = pl.ds(at + (w * QBLK - 48), KWIN)
            keys = kv[buf, keys_at, 0:128]
            values = kv[buf, keys_at, 128:256]
            scores = dot(keys, queries[buf, at // QBLK + w]) + bias[keys_at, :]
            top = jnp.max(scores, axis=0, keepdims=True)
            weights = jnp.exp2(scores - top)
            weights = (weights * (1.0 / jnp.sum(weights, axis=0, keepdims=True))).astype(bf16)
            both = dot(weights, values, ((0,), (0,)))
            out = both[0:QBLK]
            for h in range(1, HEADS):
                out = jnp.where(lane == h, both[h * QBLK : (h + 1) * QBLK], out)
            outs.append(out.astype(bf16))
        return jnp.concatenate(outs, axis=0)

    def block(layer, at, size):
        h = hid[pl.ds(at, size), :]
        h = h + dot(attend(layer, at, size), wo[layer])
        normed = (rms_scale(h) * gains[layer, 1:2, :]).astype(bf16)
        gu = dot(normed, wgu[layer])
        half = 0.5 * gu[:, :FF_ATOM]
        inner = (half * (1.0 + jnp.tanh(half)) * gu[:, FF_ATOM:]).astype(bf16)
        h = h + dot(inner, wdown[layer])
        if layer + 1 < LAYERS:
            hid[pl.ds(at, size), :] = h
            project(layer + 1, at, h)
        else:
            update = dot(head, rms_scale(h), ((1,), (1,)), lax.Precision.HIGHEST)
            noisy = cx[:, pl.ds(at, size)]
            out = inv * (4.0 * noisy + (2.0 * sig) * update)
            pred[:, pl.ds(pl.multiple_of(at - HALO, 128), size)] = out
            first_block = (at - HALO) // PAIR_BLK
            for i in range(size // PAIR_BLK):
                for d in range(3):
                    row = pl.ds(d * (rows // PAIR_BLK) + first_block + i, 1)
                    wide[row, :] = out[d : d + 1, i * PAIR_BLK : (i + 1) * PAIR_BLK]

    for layer in range(LAYERS):
        low = HALO if layer == LAYERS - 1 else HALO - 128
        span = rows if layer == LAYERS - 1 else rows + 256
        size = SIZE_LAST if layer == LAYERS - 1 else SIZE

        def step(k, _, layer=layer, low=low, size=size):
            block(layer, pl.multiple_of(low + k * size, 128), size)
            return 0

        lax.fori_loop(0, span // size, step, 0)
    pay[...] = wide[0 : 3 * blocks, :].astype(bf16)
    pred_gather.start()
    pred_gather.forward()
    true_gather.finish()
    pred_gather.finish()


def pairs_kernel(
    sigma, counts, partners, gathered_pred, gathered_true, pred, true,
    coord_grad, lddt_grad, wide_pred, wide_true, owns, totals,
):
    blocks = counts.shape[0]
    wide_pred[...] = gathered_pred[...].astype(f32)
    wide_true[...] = gathered_true[...].astype(f32)
    peers = gathered_pred.shape[0] // (3 * blocks)
    listed = jnp.zeros((blocks, PAIR_BLK), f32)
    for peer in range(peers):
        listed = listed + wide_true[peer * 4 * blocks + 3 * blocks : (peer + 1) * 4 * blocks, :]
    listed = jnp.sum(listed, axis=0, keepdims=True)
    total_pairs = listed * (PAIR_BLK * PAIR_BLK) - float(PAIR_BLK * blocks * peers)
    pair_scale = -0.0625 * (blocks * peers * PAIR_BLK * PAIR_BLK) / total_pairs
    row8 = lax.broadcasted_iota(jnp.int32, (8, PAIR_BLK), 0)
    row4 = row8 & 3
    diff = lax.broadcasted_iota(jnp.int32, (PAIR_BLK, PAIR_BLK), 0) - lax.broadcasted_iota(
        jnp.int32, (PAIR_BLK, PAIR_BLK), 1
    )

    def partner_rows(p):
        base = p // blocks * (4 * blocks) + p % blocks
        x, y, z = (wide_true[pl.ds(base + d * blocks, 1), :] for d in range(3))
        n1, n2, n3 = pieces(x * x + y * y + z * z)
        xyz = jnp.where(row4 == 0, x, jnp.where(row4 == 1, y, z))
        upper = jnp.where(row4 == 3, jnp.where(row8 == 3, n1, n2), xyz)
        ones = jnp.where(row8 < 7, 1.0, 0.0)
        lower = jnp.where(row8 < 3, xyz, jnp.where(row8 == 3, n3, ones))
        base = p // blocks * (3 * blocks) + p % blocks
        x, y, z = (wide_pred[pl.ds(base + d * blocks, 1), :] for d in range(3))
        xyz = jnp.where(row8 == 0, x, jnp.where(row8 == 1, y, jnp.where(row8 == 2, z, 0.0)))
        return jnp.concatenate([upper, lower, xyz, jnp.zeros_like(xyz)], axis=0).astype(bf16)

    def own_square(x, y, z):
        n1, n2, n3 = pieces(0.25 * (x * x + y * y + z * z + 1.0))
        xp, yp, zp = pieces(-0.5 * x), pieces(-0.5 * y), pieces(-0.5 * z)

        def xyz(i):
            return jnp.where(row4 == 0, xp[i], jnp.where(row4 == 1, yp[i], zp[i]))

        upper = jnp.where(row4 == 3, 0.25, jnp.where(row8 < 4, xyz(0), xyz(1)))
        norms = jnp.where(row8 == 4, n1, jnp.where(row8 == 5, n2, n3))
        norms = jnp.where(row8 == 7, 0.0, norms)
        lower = jnp.where(row8 < 3, xyz(2), jnp.where(row8 == 3, 0.25, norms))
        zero = jnp.zeros_like(lower)
        return jnp.concatenate([upper, lower, zero, zero], axis=0)

    def own_gap(d, x):
        hi, mid, lo = pieces(-0.5 * x)
        zero = jnp.zeros((8, PAIR_BLK), f32)
        lower = jnp.where(row8 == 4, hi, jnp.where(row8 == 5, mid, jnp.where(row8 == 6, lo, 0.0)))
        pick = jnp.where(row8 == d, 0.5, 0.0)
        return jnp.concatenate([zero, lower, pick, zero], axis=0)

    square = sigma[0] * sigma[0]
    mse_scale = jnp.full((1, PAIR_BLK), square + 4.0, f32) / jnp.full((1, PAIR_BLK), 6.0 * square, f32)
    totals[...] = jnp.zeros_like(totals)
    owns[blocks] = jnp.zeros(owns.shape[1:], bf16) + 1.0
    for b in range(blocks):
        at = slice(b * PAIR_BLK, (b + 1) * PAIR_BLK)
        owns[b] = jnp.concatenate(
            [own_square(*(true[d : d + 1, at] for d in range(3)))]
            + [own_gap(d, pred[d : d + 1, at]) for d in range(3)],
            axis=1,
        ).astype(bf16)

    def tile(b, m):
        known = jnp.minimum(b, blocks - 1)
        p = partners[known, m]
        found = dot(partner_rows(p), owns[b], ((0,), (0,)))
        st, gx, gy, gz = (found[:, i * PAIR_BLK : (i + 1) * PAIR_BLK] for i in range(4))
        sp = gx * gx + gy * gy + gz * gz + 0.25
        rp = lax.rsqrt(sp)
        gap = sp * rp - st * lax.rsqrt(st)
        e2 = gap * gap + 0.0025
        re = lax.rsqrt(e2)
        err = e2 * re
        th = [jnp.tanh(0.5 * t - err) for t in (0.5, 1.0, 2.0, 4.0)]
        slope = 4.0 - (th[0] * th[0] + th[1] * th[1] + th[2] * th[2] + th[3] * th[3])
        coef = slope * gap * (re * rp)
        shut = jnp.where(m == 0, 0, 2 * PAIR_BLK)
        coef = jnp.where(diff == shut, 0.0, coef)
        sums = jnp.concatenate(
            [jnp.sum((coef * g).reshape(16, 8, PAIR_BLK), axis=0) for g in (gx, gy, gz)], axis=0
        )
        last = m + 1 >= counts[known]
        return sums, jnp.where(last, jnp.minimum(b + 1, blocks), b), jnp.where(last, 0, m + 1)

    def visit(_, place):
        b, m = place
        found = []
        for _ in range(UNROLL):
            sums, after, then = tile(b, m)
            found.append((b, sums))
            b, m = after, then
        for at, sums in found:
            totals[at] = totals[at] + sums
        return b, m

    live = counts[0]
    for b in range(1, blocks):
        live = live + counts[b]
    lax.fori_loop(0, (live + UNROLL - 1) // UNROLL, visit, (jnp.int32(0), jnp.int32(0)))

    for b in range(blocks):
        at = slice(b * PAIR_BLK, (b + 1) * PAIR_BLK)
        total = totals[b]
        for d in range(3):
            pc, tc = pred[d : d + 1, at], true[d : d + 1, at]
            lg = (-2.0 * pair_scale) * jnp.sum(total[8 * d : 8 * d + 8], axis=0, keepdims=True)
            lddt_grad[d, :, at] = lg
            coord_grad[d, :, at] = mse_scale * (pc - tc) - lg * (1.0 / PAIR_BLK)


def share_kernel(
    atom_peers, sample_peers, sigma, feats, proj, single, token, true, noise,
    tok, single_ext, cx,
    partial, arrived, slab,
    part_send, part_recv, tok_send, tok_recv, edge_send, edge_recv, near_send, near_recv, own_sem,
):
    me = lax.axis_index("atoms")
    mine = lax.axis_index("samples")
    right = lax.rem(me + 1, atom_peers)
    left = lax.rem(me + atom_peers - 1, atom_peers)
    rows = single.shape[0]
    share = feats.shape[1] // sample_peers

    barrier = pltpu.get_barrier_semaphore()

    def greet(atom, sample):
        pl.semaphore_signal(barrier, inc=1, device_id=(atom, sample), device_id_type=MESH)

    for step in range(1, sample_peers):
        greet(me, lax.rem(mine + step, sample_peers))
    for step in range(sample_peers):
        greet(left, lax.rem(mine + step, sample_peers))
        greet(right, lax.rem(mine + step, sample_peers))

    own_copy = pltpu.make_async_copy(single, single_ext.at[pl.ds(HALO, rows)], own_sem)
    own_copy.start()
    partial[...] = dot(feats[...], proj[...], ((0,), (0,)))
    inv = lax.rsqrt(jnp.full((8, 128), sigma[0] * sigma[0] + 4.0, f32))[0:1, 0:1]
    cx[3:8, pl.ds(HALO, rows)] = jnp.concatenate(
        [token[...].astype(f32), jnp.zeros((4, rows), f32)], axis=0
    )
    for d in range(3):
        cx[d : d + 1, pl.ds(HALO, rows)] = (true[d : d + 1, :] + sigma[0] * noise[d]) * inv
    pl.semaphore_wait(barrier, 3 * sample_peers - 1)

    def part_copy(step):
        peer = lax.rem(mine + step, sample_peers)
        at = pl.multiple_of(peer * share, share)
        return remote(
            partial.at[pl.ds(at, share)], arrived.at[step], part_send.at[step], part_recv.at[step],
            me, peer,
        )

    parts = [part_copy(step) for step in range(1, sample_peers)]
    for copy in parts:
        copy.start()
    near = [
        remote(single.at[pl.ds(rows - HALO, HALO)], single_ext.at[pl.ds(0, HALO)],
               near_send.at[0], near_recv.at[0], right, mine),
        remote(single.at[pl.ds(0, HALO)], single_ext.at[pl.ds(rows + HALO, HALO)],
               near_send.at[1], near_recv.at[1], left, mine),
        remote(cx.at[:, pl.ds(rows, HALO)], cx.at[:, pl.ds(0, HALO)],
               near_send.at[2], near_recv.at[2], right, mine),
        remote(cx.at[:, pl.ds(HALO, HALO)], cx.at[:, pl.ds(rows + HALO, HALO)],
               near_send.at[3], near_recv.at[3], left, mine),
    ]
    for copy in near:
        copy.start()
    for copy in parts:
        copy.wait_recv()
    total = partial[pl.ds(pl.multiple_of(mine * share, share), share), :]
    for step in range(1, sample_peers):
        total = total + arrived[step]
    slab[...] = total.astype(bf16)
    my_rows = pl.ds(pl.multiple_of(TOK_HALO + mine * share, 16), share)
    tok[my_rows, :] = slab[...]

    def tok_copy(step):
        return remote(
            slab, tok.at[my_rows], tok_send.at[step], tok_recv.at[step],
            me, lax.rem(mine + step, sample_peers),
        )

    toks = [tok_copy(step) for step in range(1, sample_peers)]
    for copy in toks:
        copy.start()
    tokens = tok.shape[0] - 2 * TOK_HALO
    half = TOK_HALO - share
    edges = (
        (sample_peers - 1, pl.ds(0, share), pl.ds(half, share), right),
        (sample_peers - 2, pl.ds(share - half, half), pl.ds(0, half), right),
        (0, pl.ds(0, share), pl.ds(TOK_HALO + tokens, share), left),
        (1, pl.ds(0, half), pl.ds(TOK_HALO + tokens + share, half), left),
    )

    def edge_copy(i, step):
        _, src, dst, to = edges[i]
        return remote(
            slab.at[src], tok.at[dst], edge_send.at[step], edge_recv.at[i],
            to, lax.rem(mine + step, sample_peers),
        )

    for i, edge in enumerate(edges):
        @pl.when(mine == edge[0])
        def _(i=i):
            for step in range(sample_peers):
                edge_copy(i, step).start()

    for copy in parts:
        copy.wait_send()
    for copy in near:
        copy.wait()
    for copy in toks:
        copy.wait()
    for i, edge in enumerate(edges):
        edge_copy(i, 0).wait_recv()

        @pl.when(mine == edge[0])
        def _(i=i):
            for step in range(sample_peers):
                edge_copy(i, step).wait_send()

    own_copy.wait()


def vmem(n):
    return [pl.BlockSpec(memory_space=pltpu.VMEM)] * n


def smem(n):
    return [pl.BlockSpec(memory_space=pltpu.SMEM)] * n


def run_atoms(sigma, counts, true, single, cx, tok, coord_in, w_qkv, w_o, w_gu, w_down, gains, w_out):
    ext = single.shape[0]
    rows = ext - 2 * HALO
    blocks = rows // PAIR_BLK
    atom_peers = lax.axis_size("atoms")
    dma = pltpu.SemaphoreType.DMA
    one_gather = [dma((DEPTH,)), dma((DEPTH,)), dma((atom_peers,)), dma((atom_peers,))]
    return pl.pallas_call(
        functools.partial(atoms_kernel, atom_peers),
        name="atoms",
        out_shape=(
            jax.ShapeDtypeStruct((8, rows), f32),
            jax.ShapeDtypeStruct((atom_peers * 3 * blocks, PAIR_BLK), bf16),
            jax.ShapeDtypeStruct((atom_peers * 4 * blocks, PAIR_BLK), bf16),
        ),
        in_specs=smem(2) + vmem(11),
        out_specs=tuple(vmem(3)),
        scratch_shapes=[
            pltpu.VMEM((ext, CHANNELS), f32),
            pltpu.VMEM((2, ext, 2 * CHANNELS), bf16),
            pltpu.VMEM((2, ext // QBLK, CHANNELS, CHANNELS), bf16),
            pltpu.VMEM((ext, CHANNELS), f32),
            pltpu.VMEM((3 * blocks, PAIR_BLK), bf16),
            pltpu.VMEM((4 * blocks, PAIR_BLK), bf16),
            pltpu.VMEM((4 * blocks, PAIR_BLK), f32),
        ]
        + one_gather
        + one_gather,
        compiler_params=pltpu.CompilerParams(
            collective_id=1, has_side_effects=True, vmem_limit_bytes=VMEM_LIMIT
        ),
    )(sigma, counts, true, single, cx, tok, coord_in, w_qkv, w_o, w_gu, w_down, gains, w_out.T)


def run_pairs(sigma, counts, partners, gathered_pred, gathered_true, pred, true):
    rows = pred.shape[1]
    wides = [pltpu.VMEM(g.shape, f32) for g in (gathered_pred, gathered_true)]
    out = jax.ShapeDtypeStruct((3, 1, rows), f32)
    coord_grad, lddt_grad = pl.pallas_call(
        pairs_kernel,
        name="pairs",
        out_shape=(out, out),
        in_specs=smem(3) + vmem(4),
        out_specs=tuple(vmem(2)),
        scratch_shapes=wides
        + [
            pltpu.VMEM((rows // PAIR_BLK + 1, 32, 4 * PAIR_BLK), bf16),
            pltpu.VMEM((rows // PAIR_BLK + 1, 24, PAIR_BLK), f32),
        ],
        compiler_params=pltpu.CompilerParams(vmem_limit_bytes=VMEM_LIMIT),
    )(sigma, counts, partners, gathered_pred, gathered_true, pred, true)
    return jnp.swapaxes(coord_grad, 0, 1), jnp.swapaxes(lddt_grad, 0, 1)


def share(sigma, feats, proj, single, token, true, noise):
    atom_peers, sample_peers = lax.axis_size("atoms"), lax.axis_size("samples")
    rows, tokens = single.shape[0], feats.shape[1]
    part = tokens // sample_peers
    dma = pltpu.SemaphoreType.DMA
    return pl.pallas_call(
        functools.partial(share_kernel, atom_peers, sample_peers),
        name="share",
        out_shape=(
            jax.ShapeDtypeStruct((tokens + 2 * TOK_HALO, CHANNELS), bf16),
            jax.ShapeDtypeStruct((rows + 2 * HALO, CHANNELS), bf16),
            jax.ShapeDtypeStruct((8, rows + 2 * HALO), f32),
        ),
        in_specs=smem(1) + vmem(6),
        out_specs=tuple(vmem(3)),
        scratch_shapes=[
            pltpu.VMEM((tokens, CHANNELS), f32),
            pltpu.VMEM((sample_peers, part, CHANNELS), f32),
            pltpu.VMEM((part, CHANNELS), bf16),
            dma((sample_peers,)), dma((sample_peers,)), dma((sample_peers,)), dma((sample_peers,)),
            dma((sample_peers,)), dma((4,)), dma((4,)), dma((4,)),
            dma,
        ],
        compiler_params=pltpu.CompilerParams(
            collective_id=0, has_side_effects=True, vmem_limit_bytes=VMEM_LIMIT
        ),
    )(sigma, feats, proj, single, token, true, noise)


def on_device(
    token_feats, proj_w, atom_single, atom_token, true_coords, noise, sigma, coord_in,
    w_qkv, w_o, w_gu, w_down, gains, w_out, pair_blocks, pair_count,
):
    tok, single, cx = share(
        sigma, token_feats.T, proj_w, atom_single, atom_token[None], true_coords,
        jnp.swapaxes(noise, 0, 1),
    )
    pred, gathered_pred, gathered_true = run_atoms(
        sigma, pair_count, true_coords, single, cx, tok,
        coord_in, w_qkv, w_o, w_gu, w_down, gains, w_out,
    )
    return run_pairs(
        sigma, pair_count, pair_blocks, gathered_pred, gathered_true, pred, true_coords
    )


def solution(mesh):
    in_specs = (
        P("atoms", "samples"),
        P("samples", None),
        P("atoms", None),
        P("atoms"),
        P(None, "atoms"),
        P("samples", None, "atoms"),
        P("samples"),
        P(), P(), P(), P(), P(), P(), P(),
        P("atoms", None),
        P("atoms"),
    )
    out_specs = (P("samples", None, "atoms"), P("samples", None, "atoms"))
    return jax.shard_map(on_device, mesh=mesh, in_specs=in_specs, out_specs=out_specs, check_vma=False)
```

```python
import functools
import math

import jax
import jax.numpy as jnp
from jax import lax
from jax.experimental import pallas as pl
from jax.experimental.pallas import tpu as pltpu
from jax.sharding import PartitionSpec as P

HEADS = 4
HEAD_DIM = 32
FF_ATOM = 256
LAYERS = 3
QBLK = 32
KWIN = 128
PAIR_BLK = 128
CHANNELS = 128
CHUNK = 256
FIRST_UNROLL = 5
UNROLL = 4
HALO = 256
TOK_HALO = 48
TOK_WIN = 64
EPS = 1e-05
DEPTH = 8
VMEM_LIMIT = 56 * 1024 * 1024

f32 = jnp.float32
bf16 = jnp.bfloat16


def dot(a, b, dims=((1,), (0,)), precision=None):
    return lax.dot_general(a, b, (dims, ((), ())), precision=precision, preferred_element_type=f32)


def pieces(v):
    hi = v.astype(bf16).astype(f32)
    mid = (v - hi).astype(bf16).astype(f32)
    lo = (v - hi - mid).astype(bf16).astype(f32)
    return hi, mid, lo


def rms_scale(h):
    return h * lax.rsqrt(jnp.mean(h * h, axis=1, keepdims=True) + EPS)


MESH = pl.DeviceIdType.MESH


def remote(src, dst, send, recv, atom, sample):
    return pltpu.make_async_remote_copy(
        src_ref=src, dst_ref=dst, send_sem=send, recv_sem=recv,
        device_id=(atom, sample), device_id_type=MESH,
    )

def gather_plan(atom_peers):
    nz = DEPTH
    nx = atom_peers // nz
    me = lax.axis_index("atoms")
    x, z = me // nz, lax.rem(me, nz)

    def along_z(dz):
        return x * nz + lax.rem(z + dz + nz, nz)

    def along_x(dx):
        return lax.rem(x + dx, nx) * nz + z

    return nz, nx, me, along_z, along_x


class Gather:
    def __init__(self, atom_peers, pay, whole, sems):
        self.nz, self.nx, self.me, self.along_z, self.along_x = gather_plan(atom_peers)
        self.mine = lax.axis_index("samples")
        self.pay, self.whole = pay, whole
        self.z_send, self.z_recv, self.x_send, self.x_recv = sems
        self.order = [0]
        for step in range(1, self.nz // 2 + 1):
            self.order += [step, self.nz - step] if 2 * step != self.nz else [step]

    def rows(self, owner):
        size = self.pay.shape[0]
        return pl.ds(pl.multiple_of(owner * size, size), size)

    def z_copy(self, dz):
        return remote(
            self.pay, self.whole.at[self.rows(self.me)], self.z_send.at[dz], self.z_recv.at[dz],
            self.along_z(dz), self.mine,
        )

    def x_copy(self, dz, dx):
        at = self.rows(self.along_z(-dz))
        src = self.pay if dz == 0 else self.whole.at[at]
        slot = dz * self.nx + dx
        return remote(
            src, self.whole.at[at], self.x_send.at[slot], self.x_recv.at[slot],
            self.along_x(dx), self.mine,
        )

    def start(self):
        for dz in self.order[1:]:
            self.z_copy(dz).start()
        for dx in range(1, self.nx):
            self.x_copy(0, dx).start()
        self.whole[self.rows(self.me), :] = self.pay[...]

    def forward(self):
        for dz in self.order[1:]:
            self.z_copy(dz).wait_recv()
            for dx in range(1, self.nx):
                self.x_copy(dz, dx).start()

    def finish(self):
        for dz in self.order[1:]:
            self.z_copy(dz).wait_send()
        for dz in self.order:
            for dx in range(1, self.nx):
                self.x_copy(dz, dx).wait()


def atoms_kernel(
    atom_peers, sample_peers, sigma, counts, feats, proj, own_single, token, true, noise,
    coord_in, wqkv, wo, wgu, wdown, gains, wout,
    pred, gathered_pred, gathered_true,
    hid, kv, queries, bias, pay, true_pay, wide, tok, single, cx, partial, arrived, slab, *sems,
):
    rows = own_single.shape[0]
    ext = single.shape[0]
    blocks = rows // PAIR_BLK
    half = blocks // 2
    nz, nx, me, along_z, along_x = gather_plan(atom_peers)
    mine = lax.axis_index("samples")
    barrier = pltpu.get_barrier_semaphore()
    right = lax.rem(me + 1, atom_peers)
    left = lax.rem(me + atom_peers - 1, atom_peers)
    share = feats.shape[1] // sample_peers
    (part_send, part_recv, tok_send, tok_recv, edge_send, edge_recv, near_send, near_recv,
     own_sem) = sems[:9]

    def greet(atom, sample):
        pl.semaphore_signal(barrier, inc=1, device_id=(atom, sample), device_id_type=MESH)

    for step in range(1, sample_peers):
        greet(me, lax.rem(mine + step, sample_peers))
    for step in range(sample_peers):
        greet(left, lax.rem(mine + step, sample_peers))
        greet(right, lax.rem(mine + step, sample_peers))

    for dz in range(1, nz):
        greet(along_z(dz), mine)
    for dx in range(1, nx):
        greet(along_x(dx), mine)
    first_atom = me * rows
    total_atoms = rows * atom_peers
    first_tok = me * (tok.shape[0] - 2 * TOK_HALO)
    sig = sigma[0]
    inv = lax.rsqrt(jnp.full((8, CHANNELS), sig * sig + 4.0, f32))[0:1, 0:1]
    zero5 = jnp.zeros((5, CHANNELS), f32)
    hi, mid, lo = pieces(jnp.concatenate([coord_in[...], zero5], axis=0))
    coord_w = jnp.concatenate([hi, mid, lo, hi, mid, hi], axis=0).astype(bf16)
    head = jnp.concatenate([wout[...], jnp.zeros((CHANNELS - 3, CHANNELS), f32)], axis=0).T
    hi, mid, lo = pieces(head)
    head = jnp.concatenate([hi, hi, mid], axis=0).astype(bf16)
    q_scale = math.log2(math.e) / math.sqrt(HEAD_DIM)
    lane = lax.broadcasted_iota(jnp.int32, (1, CHANNELS), 1) // HEAD_DIM

    pos = first_atom - HALO + lax.broadcasted_iota(jnp.int32, (ext, CHANNELS), 0)
    own_copy = pltpu.make_async_copy(own_single, single.at[pl.ds(HALO, rows)], own_sem)
    own_copy.start()
    partial[...] = dot(feats[...], proj[...], ((0,), (0,)))
    cx[3:8, pl.ds(HALO, rows)] = jnp.concatenate(
        [token[...].astype(f32), jnp.zeros((4, rows), f32)], axis=0
    )
    for d in range(3):
        cx[d : d + 1, pl.ds(HALO, rows)] = (true[d : d + 1, :] + sig * noise[d]) * inv
    for d in range(3):
        for b in range(blocks):
            wide[d * blocks + b : d * blocks + b + 1, :] = true[
                d : d + 1, b * PAIR_BLK : (b + 1) * PAIR_BLK
            ]
    for b in range(blocks):
        wide[3 * blocks + b : 3 * blocks + b + 1, :] = jnp.full((1, PAIR_BLK), counts[b], jnp.int32).astype(f32)
    true_pay[...] = wide[...].astype(bf16)
    bias[...] = jnp.where((pos >= 0) & (pos < total_atoms), 0.0, -1e30)
    pl.semaphore_wait(barrier, 3 * sample_peers - 1 + nz + nx - 2)
    true_gather = Gather(atom_peers, true_pay, gathered_true, sems[9:13])
    pred_gathers = [
        Gather(
            atom_peers, pay.at[i], gathered_pred.at[pl.ds(i * (atom_peers * 4 * half), atom_peers * 4 * half)],
            sems[13 + 4 * i : 17 + 4 * i],
        )
        for i in range(2)
    ]

    def part_copy(step):
        peer = lax.rem(mine + step, sample_peers)
        at = pl.multiple_of(peer * share, share)
        return remote(
            partial.at[pl.ds(at, share)], arrived.at[step], part_send.at[step], part_recv.at[step],
            me, peer,
        )

    parts = [part_copy(step) for step in range(1, sample_peers)]
    for copy in parts:
        copy.start()
    near = [
        remote(own_single.at[pl.ds(rows - HALO, HALO)], single.at[pl.ds(0, HALO)],
               near_send.at[0], near_recv.at[0], right, mine),
        remote(own_single.at[pl.ds(0, HALO)], single.at[pl.ds(rows + HALO, HALO)],
               near_send.at[1], near_recv.at[1], left, mine),
        remote(cx.at[:, pl.ds(rows, HALO)], cx.at[:, pl.ds(0, HALO)],
               near_send.at[2], near_recv.at[2], right, mine),
        remote(cx.at[:, pl.ds(HALO, HALO)], cx.at[:, pl.ds(rows + HALO, HALO)],
               near_send.at[3], near_recv.at[3], left, mine),
    ]
    for copy in near:
        copy.start()
    for copy in parts:
        copy.wait_recv()
    total = partial[pl.ds(pl.multiple_of(mine * share, share), share), :]
    for step in range(1, sample_peers):
        total = total + arrived[step]
    slab[...] = total.astype(bf16)
    my_rows = pl.ds(pl.multiple_of(TOK_HALO + mine * share, 16), share)
    tok[my_rows, :] = slab[...]

    def tok_copy(step):
        return remote(
            slab, tok.at[my_rows], tok_send.at[step], tok_recv.at[step],
            me, lax.rem(mine + step, sample_peers),
        )

    toks = [tok_copy(step) for step in range(1, sample_peers)]
    for copy in toks:
        copy.start()
    tokens = tok.shape[0] - 2 * TOK_HALO
    rest = TOK_HALO - share
    edges = (
        (sample_peers - 1, pl.ds(0, share), pl.ds(rest, share), right),
        (sample_peers - 2, pl.ds(share - rest, rest), pl.ds(0, rest), right),
        (0, pl.ds(0, share), pl.ds(TOK_HALO + tokens, share), left),
        (1, pl.ds(0, rest), pl.ds(TOK_HALO + tokens + share, rest), left),
    )

    def edge_copy(i, step):
        _, src, dst, to = edges[i]
        return remote(
            slab.at[src], tok.at[dst], edge_send.at[step], edge_recv.at[i],
            to, lax.rem(mine + step, sample_peers),
        )

    for i, edge in enumerate(edges):
        @pl.when(mine == edge[0])
        def _(i=i):
            for step in range(sample_peers):
                edge_copy(i, step).start()

    for copy in parts:
        copy.wait_send()
    for copy in near:
        copy.wait()
    for copy in toks:
        copy.wait()
    for i, edge in enumerate(edges):
        edge_copy(i, 0).wait_recv()

        @pl.when(mine == edge[0])
        def _(i=i):
            for step in range(sample_peers):
                edge_copy(i, step).wait_send()

    own_copy.wait()
    true_gather.start()

    def project(layer, at, h):
        normed = (rms_scale(h) * gains[layer, 0:1, :]).astype(bf16)
        out = dot(normed, wqkv[layer])
        rows_at = pl.ds(at, h.shape[0])
        kv[layer % 2, rows_at, :] = out[:, 128:].astype(bf16)
        for t in range(h.shape[0] // CHANNELS):
            turned = (out[t * CHANNELS : (t + 1) * CHANNELS, :128] * q_scale).T
            shifted = [turned if r == 0 else pltpu.roll(turned, r * QBLK, 1) for r in range(HEADS)]
            for w in range(CHANNELS // QBLK):
                spread = jnp.concatenate(
                    [
                        jnp.where(lane == h, shifted[(h - w) % HEADS][h * QBLK : (h + 1) * QBLK], 0.0)
                        for h in range(HEADS)
                    ],
                    axis=0,
                )
                queries[layer % 2, at // QBLK + t * HEADS + w] = spread.astype(bf16)

    def first(k, _):
        at = pl.multiple_of(k * CHUNK, CHUNK)
        c = cx[:, pl.ds(at, CHUNK)]
        hi, mid, lo = pieces(c)
        rel = c[3:4, :].astype(jnp.int32) - (first_tok - TOK_HALO + k * (CHUNK // 8))
        hot = jnp.where(lax.broadcasted_iota(jnp.int32, (TOK_WIN, CHUNK), 0) == rel, 1.0, 0.0)
        left = jnp.concatenate([hot, hi, hi, hi, mid, mid, lo], axis=0).astype(bf16)
        tok_at = pl.ds(pl.multiple_of(k * (CHUNK // 8), CHUNK // 8), TOK_WIN)
        right = jnp.concatenate([tok[tok_at, :], coord_w], axis=0)
        h = single[pl.ds(at, CHUNK), :].astype(f32) + dot(left, right, ((0,), (0,)))
        hid[pl.ds(at, CHUNK), :] = h
        project(0, at, h)
        return 0

    lax.fori_loop(0, ext // CHUNK, first, 0, unroll=FIRST_UNROLL)

    true_gather.forward()

    def attend(layer, at, size):
        buf = layer % 2
        outs = []
        for w in range(size // QBLK):
            keys_at = pl.ds(at + (w * QBLK - 48), KWIN)
            keys = kv[buf, keys_at, 0:128]
            values = kv[buf, keys_at, 128:256]
            scores = dot(keys, queries[buf, at // QBLK + w]) + bias[keys_at, :]
            top = jnp.max(scores, axis=0, keepdims=True)
            weights = jnp.exp2(scores - top)
            weights = (weights * (1.0 / jnp.sum(weights, axis=0, keepdims=True))).astype(bf16)
            both = dot(weights, values, ((0,), (0,)))
            out = both[0:QBLK]
            for h in range(1, HEADS):
                out = jnp.where(lane == h, both[h * QBLK : (h + 1) * QBLK], out)
            outs.append(out.astype(bf16))
        return jnp.concatenate(outs, axis=0)

    def block(layer, at, size):
        h = hid[pl.ds(at, size), :]
        h = h + dot(attend(layer, at, size), wo[layer])
        normed = (rms_scale(h) * gains[layer, 1:2, :]).astype(bf16)
        gu = dot(normed, wgu[layer])
        gate = 0.5 * gu[:, :FF_ATOM]
        inner = (gate * (1.0 + jnp.tanh(gate)) * gu[:, FF_ATOM:]).astype(bf16)
        h = h + dot(inner, wdown[layer])
        if layer + 1 < LAYERS:
            hid[pl.ds(at, size), :] = h
            project(layer + 1, at, h)
        else:
            normed = rms_scale(h)
            hi = normed.astype(bf16)
            mid = (normed - hi.astype(f32)).astype(bf16)
            update = dot(jnp.concatenate([hi, mid, hi], axis=1), head)
            update = jnp.concatenate(
                [update[t * CHANNELS : (t + 1) * CHANNELS].T[0:8] for t in range(size // CHANNELS)],
                axis=1,
            )
            noisy = cx[:, pl.ds(at, size)]
            out = inv * (4.0 * noisy + (2.0 * sig) * update)
            pred[:, pl.ds(pl.multiple_of(at - HALO, 128), size)] = out
            part = (at - HALO) // (half * PAIR_BLK)
            for d in range(3):
                for i in range(half):
                    wide[d * half + i : d * half + i + 1, :] = out[
                        d : d + 1, i * PAIR_BLK : (i + 1) * PAIR_BLK
                    ]
            pay[part] = wide[0 : 4 * half, :].astype(bf16)

    middle = HALO + rows // 2
    start = HALO - 128
    end = HALO + rows + 128
    block(0, start, middle + 256 - start)
    block(1, start, middle + 128 - start)
    block(2, HALO, rows // 2)
    pred_gathers[0].start()
    block(0, middle + 256, end - middle - 256)
    pred_gathers[0].forward()
    block(1, middle + 128, end - middle - 128)
    block(2, middle, rows // 2)
    pred_gathers[1].start()
    pred_gathers[1].forward()
    true_gather.finish()
    pred_gathers[0].finish()
    pred_gathers[1].finish()


def pairs_kernel(
    sigma, counts, partners, gathered_pred, gathered_true, pred, true,
    coord_grad, lddt_grad, wide_pred, wide_true, owns, totals, held, parts,
):
    blocks = counts.shape[0]
    wide_pred[...] = gathered_pred[...].astype(f32)
    wide_true[...] = gathered_true[...].astype(f32)
    peers = gathered_true.shape[0] // (4 * blocks)
    listed = jnp.zeros((blocks, PAIR_BLK), f32)
    for peer in range(peers):
        listed = listed + wide_true[peer * 4 * blocks + 3 * blocks : (peer + 1) * 4 * blocks, :]
    listed = jnp.sum(listed, axis=0, keepdims=True)
    total_pairs = listed * (PAIR_BLK * PAIR_BLK) - float(PAIR_BLK * blocks * peers)
    pair_scale = -0.0625 * (blocks * peers * PAIR_BLK * PAIR_BLK) / total_pairs
    row8 = lax.broadcasted_iota(jnp.int32, (8, PAIR_BLK), 0)
    row4 = row8 & 3
    diff = lax.broadcasted_iota(jnp.int32, (PAIR_BLK, PAIR_BLK), 0) - lax.broadcasted_iota(
        jnp.int32, (PAIR_BLK, PAIR_BLK), 1
    )

    half = blocks // 2

    def partner_rows(wide, base, stride):
        x, y, z = (wide[pl.ds(base + d * stride, 1), :] for d in range(3))
        n1, n2, n3 = pieces(x * x + y * y + z * z)
        xyz = jnp.where(row4 == 0, x, jnp.where(row4 == 1, y, z))
        upper = jnp.where(row4 == 3, jnp.where(row8 == 3, n1, n2), xyz)
        ones = jnp.where(row8 < 7, 1.0, 0.0)
        lower = jnp.where(row8 < 3, xyz, jnp.where(row8 == 3, n3, ones))
        return jnp.concatenate([upper, lower], axis=0)

    def own_rows(x, y, z):
        n = x * x + y * y + z * z + 1.0
        n1, n2, n3 = pieces(0.25 * n)
        xp, yp, zp = pieces(-0.5 * x), pieces(-0.5 * y), pieces(-0.5 * z)

        def xyz(i):
            return jnp.where(row4 == 0, xp[i], jnp.where(row4 == 1, yp[i], zp[i]))

        upper = jnp.where(row4 == 3, 0.25, jnp.where(row8 < 4, xyz(0), xyz(1)))
        norms = jnp.where(row8 == 4, n1, jnp.where(row8 == 5, n2, n3))
        norms = jnp.where(row8 == 7, 0.0, norms)
        lower = jnp.where(row8 < 3, xyz(2), jnp.where(row8 == 3, 0.25, norms))
        return jnp.concatenate([upper, lower], axis=0)

    none = jnp.zeros((16, PAIR_BLK), f32)
    square = sigma[0] * sigma[0]
    mse_scale = jnp.full((1, PAIR_BLK), square + 4.0, f32) / jnp.full((1, PAIR_BLK), 6.0 * square, f32)
    totals[...] = jnp.zeros_like(totals)
    owns[blocks] = jnp.zeros(owns.shape[1:], bf16) + 1.0
    for b in range(blocks):
        at = slice(b * PAIR_BLK, (b + 1) * PAIR_BLK)
        own_pred = own_rows(*(pred[d : d + 1, at] for d in range(3)))
        own_true = own_rows(*(true[d : d + 1, at] for d in range(3)))
        owns[b] = jnp.concatenate(
            [
                jnp.concatenate([own_pred, none], axis=1),
                jnp.concatenate([none, own_true], axis=1),
            ],
            axis=0,
        ).astype(bf16)

    def begin(b, m):
        known = jnp.minimum(b, blocks - 1)
        p = partners[known, m]
        owner, place = p // blocks, p % blocks
        at = place // half * (peers * 4 * half) + owner * (4 * half) + place % half
        part_pred = partner_rows(wide_pred, at, half)
        part_true = partner_rows(wide_true, owner * (4 * blocks) + place, blocks)
        part = jnp.concatenate([part_pred, part_true], axis=0).astype(bf16)
        squares = dot(part, owns[b], ((0,), (0,)))
        last = m + 1 >= counts[known]
        after = jnp.where(last, jnp.minimum(b + 1, blocks), b), jnp.where(last, 0, m + 1)
        return part, squares, after

    def middle(squares, m):
        sp, st = squares[:, :PAIR_BLK], squares[:, PAIR_BLK:]
        rp = lax.rsqrt(sp)
        gap = sp * rp - st * lax.rsqrt(st)
        e2 = gap * gap + 0.0025
        re = lax.rsqrt(e2)
        err = e2 * re
        th = [jnp.tanh(0.5 * t - err) for t in (0.5, 1.0, 2.0, 4.0)]
        slope = 4.0 - (th[0] * th[0] + th[1] * th[1] + th[2] * th[2] + th[3] * th[3])
        coef = slope * gap * (re * rp)
        shut = jnp.where(m == 0, 0, 2 * PAIR_BLK)
        return jnp.where(diff == shut, 0.0, coef).astype(bf16)

    def start(slot, b, m):
        begun = []
        for i in range(UNROLL):
            part, squares, after = begin(b, m)
            parts[slot, i] = part[0:16]
            held[slot, i] = squares
            begun.append((b, m))
            b, m = after
        return begun, (b, m)

    def end(slot, begun):
        coefs = [middle(held[slot, i], m) for i, (_, m) in enumerate(begun)]
        found = [(b, dot(parts[slot, i], coef)[8:16]) for i, ((b, _), coef) in enumerate(zip(begun, coefs))]
        for at, sums in found:
            totals[at] = totals[at] + sums

    def visit(_, carry):
        begun, place = carry
        more, place = start(1, *place)
        end(0, begun)
        begun, place = start(0, *place)
        end(1, more)
        return begun, place

    live = counts[0]
    for b in range(1, blocks):
        live = live + counts[b]
    lax.fori_loop(0, (live + 2 * UNROLL - 1) // (2 * UNROLL), visit, start(0, jnp.int32(0), jnp.int32(0)))

    for b in range(blocks):
        at = slice(b * PAIR_BLK, (b + 1) * PAIR_BLK)
        total = totals[b]
        for d in range(3):
            pc, tc = pred[d : d + 1, at], true[d : d + 1, at]
            lg = pair_scale[:, 0:PAIR_BLK] * (pc * total[4:5] - total[d : d + 1])
            lddt_grad[d, :, at] = lg
            coord_grad[d, :, at] = mse_scale * (pc - tc) - lg * (1.0 / PAIR_BLK)


def vmem(n):
    return [pl.BlockSpec(memory_space=pltpu.VMEM)] * n


def smem(n):
    return [pl.BlockSpec(memory_space=pltpu.SMEM)] * n


def run_atoms(
    sigma, counts, feats, proj, single, token, true, noise,
    coord_in, w_qkv, w_o, w_gu, w_down, gains, w_out,
):
    rows, tokens = single.shape[0], feats.shape[1]
    ext = rows + 2 * HALO
    blocks = rows // PAIR_BLK
    atom_peers, sample_peers = lax.axis_size("atoms"), lax.axis_size("samples")
    part = tokens // sample_peers
    dma = pltpu.SemaphoreType.DMA
    one_gather = [dma((DEPTH,)), dma((DEPTH,)), dma((atom_peers,)), dma((atom_peers,))]
    return pl.pallas_call(
        functools.partial(atoms_kernel, atom_peers, sample_peers),
        name="atoms",
        out_shape=(
            jax.ShapeDtypeStruct((8, rows), f32),
            jax.ShapeDtypeStruct((atom_peers * 4 * blocks, PAIR_BLK), bf16),
            jax.ShapeDtypeStruct((atom_peers * 4 * blocks, PAIR_BLK), bf16),
        ),
        in_specs=smem(2) + vmem(13),
        out_specs=tuple(vmem(3)),
        scratch_shapes=[
            pltpu.VMEM((ext, CHANNELS), f32),
            pltpu.VMEM((2, ext, 2 * CHANNELS), bf16),
            pltpu.VMEM((2, ext // QBLK, CHANNELS, CHANNELS), bf16),
            pltpu.VMEM((ext, CHANNELS), f32),
            pltpu.VMEM((2, 2 * blocks, PAIR_BLK), bf16),
            pltpu.VMEM((4 * blocks, PAIR_BLK), bf16),
            pltpu.VMEM((4 * blocks, PAIR_BLK), f32),
            pltpu.VMEM((tokens + 2 * TOK_HALO, CHANNELS), bf16),
            pltpu.VMEM((ext, CHANNELS), bf16),
            pltpu.VMEM((8, ext), f32),
            pltpu.VMEM((tokens, CHANNELS), f32),
            pltpu.VMEM((sample_peers, part, CHANNELS), f32),
            pltpu.VMEM((part, CHANNELS), bf16),
            dma((sample_peers,)), dma((sample_peers,)), dma((sample_peers,)), dma((sample_peers,)),
            dma((sample_peers,)), dma((4,)), dma((4,)), dma((4,)), dma,
        ]
        + 3 * one_gather,
        compiler_params=pltpu.CompilerParams(
            collective_id=0, has_side_effects=True, vmem_limit_bytes=VMEM_LIMIT
        ),
    )(
        sigma, counts, feats, proj, single, token, true, noise,
        coord_in, w_qkv, w_o, w_gu, w_down, gains, w_out.T,
    )


def run_pairs(sigma, counts, partners, gathered_pred, gathered_true, pred, true):
    rows = pred.shape[1]
    wides = [pltpu.VMEM(g.shape, f32) for g in (gathered_pred, gathered_true)]
    out = jax.ShapeDtypeStruct((3, 1, rows), f32)
    coord_grad, lddt_grad = pl.pallas_call(
        pairs_kernel,
        name="pairs",
        out_shape=(out, out),
        in_specs=smem(3) + vmem(4),
        out_specs=tuple(vmem(2)),
        scratch_shapes=wides
        + [
            pltpu.VMEM((rows // PAIR_BLK + 1, 32, 2 * PAIR_BLK), bf16),
            pltpu.VMEM((rows // PAIR_BLK + 1, 8, PAIR_BLK), f32),
            pltpu.VMEM((2, UNROLL, PAIR_BLK, 2 * PAIR_BLK), f32),
            pltpu.VMEM((2, UNROLL, 16, PAIR_BLK), bf16),
        ],
        compiler_params=pltpu.CompilerParams(vmem_limit_bytes=VMEM_LIMIT),
    )(sigma, counts, partners, gathered_pred, gathered_true, pred, true)
    return jnp.swapaxes(coord_grad, 0, 1), jnp.swapaxes(lddt_grad, 0, 1)


def on_device(
    token_feats, proj_w, atom_single, atom_token, true_coords, noise, sigma, coord_in,
    w_qkv, w_o, w_gu, w_down, gains, w_out, pair_blocks, pair_count,
):
    pred, gathered_pred, gathered_true = run_atoms(
        sigma, pair_count, token_feats.T, proj_w, atom_single, atom_token[None], true_coords,
        jnp.swapaxes(noise, 0, 1), coord_in, w_qkv, w_o, w_gu, w_down, gains, w_out,
    )
    return run_pairs(
        sigma, pair_count, pair_blocks, gathered_pred, gathered_true, pred, true_coords
    )


def solution(mesh):
    in_specs = (
        P("atoms", "samples"),
        P("samples", None),
        P("atoms", None),
        P("atoms"),
        P(None, "atoms"),
        P("samples", None, "atoms"),
        P("samples"),
        P(), P(), P(), P(), P(), P(), P(),
        P("atoms", None),
        P("atoms"),
    )
    out_specs = (P("samples", None, "atoms"), P("samples", None, "atoms"))
    return jax.shard_map(on_device, mesh=mesh, in_specs=in_specs, out_specs=out_specs, check_vma=False)
```

```python
import functools
import math

import jax
import jax.numpy as jnp
from jax import lax
from jax.experimental import pallas as pl
from jax.experimental.pallas import tpu as pltpu
from jax.sharding import PartitionSpec as P

HEADS = 4
HEAD_DIM = 32
FF_ATOM = 256
LAYERS = 3
QBLK = 32
KWIN = 128
PAIR_BLK = 128
CHANNELS = 128
CHUNK = 256
FIRST_UNROLL = 5
UNROLL = 8
HALO = 256
TOK_HALO = 48
TOK_WIN = 64
EPS = 1e-05
DEPTH = 8
VMEM_LIMIT = 56 * 1024 * 1024

f32 = jnp.float32
bf16 = jnp.bfloat16


def dot(a, b, dims=((1,), (0,)), precision=None):
    return lax.dot_general(a, b, (dims, ((), ())), precision=precision, preferred_element_type=f32)


def pieces(v):
    hi = v.astype(bf16).astype(f32)
    mid = (v - hi).astype(bf16).astype(f32)
    lo = (v - hi - mid).astype(bf16).astype(f32)
    return hi, mid, lo


def rms_scale(h):
    return h * lax.rsqrt(jnp.mean(h * h, axis=1, keepdims=True) + EPS)


MESH = pl.DeviceIdType.MESH


def remote(src, dst, send, recv, atom, sample):
    return pltpu.make_async_remote_copy(
        src_ref=src, dst_ref=dst, send_sem=send, recv_sem=recv,
        device_id=(atom, sample), device_id_type=MESH,
    )

def gather_plan(atom_peers):
    nz = DEPTH
    nx = atom_peers // nz
    me = lax.axis_index("atoms")
    x, z = me // nz, lax.rem(me, nz)

    def along_z(dz):
        return x * nz + lax.rem(z + dz + nz, nz)

    def along_x(dx):
        return lax.rem(x + dx, nx) * nz + z

    return nz, nx, me, along_z, along_x


class Gather:
    def __init__(self, atom_peers, pay, whole, sems):
        self.nz, self.nx, self.me, self.along_z, self.along_x = gather_plan(atom_peers)
        self.mine = lax.axis_index("samples")
        self.pay, self.whole = pay, whole
        self.z_send, self.z_recv, self.x_send, self.x_recv = sems
        self.order = [0]
        for step in range(1, self.nz // 2 + 1):
            self.order += [step, self.nz - step] if 2 * step != self.nz else [step]

    def rows(self, owner):
        size = self.pay.shape[0]
        return pl.ds(pl.multiple_of(owner * size, size), size)

    def z_copy(self, dz):
        return remote(
            self.pay, self.whole.at[self.rows(self.me)], self.z_send.at[dz], self.z_recv.at[dz],
            self.along_z(dz), self.mine,
        )

    def x_copy(self, dz, dx):
        at = self.rows(self.along_z(-dz))
        src = self.pay if dz == 0 else self.whole.at[at]
        slot = dz * self.nx + dx
        return remote(
            src, self.whole.at[at], self.x_send.at[slot], self.x_recv.at[slot],
            self.along_x(dx), self.mine,
        )

    def start(self):
        for dz in self.order[1:]:
            self.z_copy(dz).start()
        for dx in range(1, self.nx):
            self.x_copy(0, dx).start()
        self.whole[self.rows(self.me), :] = self.pay[...]

    def forward(self):
        for dz in self.order[1:]:
            self.z_copy(dz).wait_recv()
            for dx in range(1, self.nx):
                self.x_copy(dz, dx).start()

    def finish(self):
        for dz in self.order[1:]:
            self.z_copy(dz).wait_send()
        for dz in self.order:
            for dx in range(1, self.nx):
                self.x_copy(dz, dx).wait()


def partner_features(x, y, z):
    row8 = lax.broadcasted_iota(jnp.int32, (8, PAIR_BLK), 0)
    row4 = row8 & 3
    n1, n2, n3 = pieces(x * x + y * y + z * z)
    xyz = jnp.where(row4 == 0, x, jnp.where(row4 == 1, y, z))
    upper = jnp.where(row4 == 3, jnp.where(row8 == 3, n1, n2), xyz)
    ones = jnp.where(row8 < 7, 1.0, 0.0)
    lower = jnp.where(row8 < 3, xyz, jnp.where(row8 == 3, n3, ones))
    return jnp.concatenate([upper, lower], axis=0)


def own_features(x, y, z):
    row8 = lax.broadcasted_iota(jnp.int32, (8, PAIR_BLK), 0)
    row4 = row8 & 3
    n1, n2, n3 = pieces(0.25 * (x * x + y * y + z * z + 1.0))
    xp, yp, zp = pieces(-0.5 * x), pieces(-0.5 * y), pieces(-0.5 * z)

    def xyz(i):
        return jnp.where(row4 == 0, xp[i], jnp.where(row4 == 1, yp[i], zp[i]))

    upper = jnp.where(row4 == 3, 0.25, jnp.where(row8 < 4, xyz(0), xyz(1)))
    norms = jnp.where(row8 == 4, n1, jnp.where(row8 == 5, n2, n3))
    norms = jnp.where(row8 == 7, 0.0, norms)
    lower = jnp.where(row8 < 3, xyz(2), jnp.where(row8 == 3, 0.25, norms))
    return jnp.concatenate([upper, lower], axis=0)


def pair_coef(squares):
    sp, st = squares[:, :PAIR_BLK], squares[:, PAIR_BLK:]
    rp = lax.rsqrt(sp)
    gap = sp * rp - st * lax.rsqrt(st)
    e2 = gap * gap + 0.0025
    re = lax.rsqrt(e2)
    err = e2 * re
    th = [jnp.tanh(0.5 * t - err) for t in (0.5, 1.0, 2.0, 4.0)]
    slope = 4.0 - (th[0] * th[0] + th[1] * th[1] + th[2] * th[2] + th[3] * th[3])
    return slope * gap * (re * rp)


def atoms_kernel(
    atom_peers, sample_peers, sigma, counts, feats, proj, own_single, token, true, noise,
    coord_in, wqkv, wo, wgu, wdown, gains, wout,
    pred, gathered_pred, gathered_true, owns, selves,
    hid, kv, queries, bias, pay, true_pay, wide, tok, near_single, cx, hots, partial, arrived, slab, *sems,
):
    rows = own_single.shape[0]
    ext = rows + 2 * HALO
    blocks = rows // PAIR_BLK
    nz, nx, me, along_z, along_x = gather_plan(atom_peers)
    mine = lax.axis_index("samples")
    barrier = pltpu.get_barrier_semaphore()
    right = lax.rem(me + 1, atom_peers)
    left = lax.rem(me + atom_peers - 1, atom_peers)
    share = feats.shape[1] // sample_peers
    (part_send, part_recv, tok_send, tok_recv, edge_send, edge_recv, near_send, near_recv) = sems[:8]

    def greet(atom, sample):
        pl.semaphore_signal(barrier, inc=1, device_id=(atom, sample), device_id_type=MESH)

    for step in range(1, sample_peers):
        greet(me, lax.rem(mine + step, sample_peers))
    for step in range(sample_peers):
        greet(left, lax.rem(mine + step, sample_peers))
        greet(right, lax.rem(mine + step, sample_peers))

    for dz in range(1, nz):
        greet(along_z(dz), mine)
    for dx in range(1, nx):
        greet(along_x(dx), mine)
    first_atom = me * rows
    total_atoms = rows * atom_peers
    first_tok = me * (tok.shape[0] - 2 * TOK_HALO)
    sig = sigma[0]
    inv = lax.rsqrt(jnp.full((8, CHANNELS), sig * sig + 4.0, f32))[0:1, 0:1]
    zero5 = jnp.zeros((5, CHANNELS), f32)
    hi, mid, lo = pieces(jnp.concatenate([coord_in[...], zero5], axis=0))
    coord_w = jnp.concatenate([hi, mid, lo, hi, mid, hi], axis=0).astype(bf16)
    head = jnp.concatenate([wout[...], jnp.zeros((CHANNELS - 3, CHANNELS), f32)], axis=0).T
    hi, mid, lo = pieces(head)
    head = jnp.concatenate([hi, hi, mid], axis=0).astype(bf16)
    q_scale = math.log2(math.e) / math.sqrt(HEAD_DIM)
    lane = lax.broadcasted_iota(jnp.int32, (1, CHANNELS), 1) // HEAD_DIM

    pos = first_atom - HALO + lax.broadcasted_iota(jnp.int32, (ext, CHANNELS), 0)
    partial[...] = dot(feats[...], proj[...], ((0,), (0,)))
    cx[3:8, pl.ds(HALO, rows)] = jnp.concatenate(
        [token[...].astype(f32), jnp.zeros((4, rows), f32)], axis=0
    )
    for d in range(3):
        cx[d : d + 1, pl.ds(HALO, rows)] = (true[d : d + 1, :] + sig * noise[d]) * inv
    for d in range(3):
        for b in range(blocks):
            wide[d * blocks + b : d * blocks + b + 1, :] = true[
                d : d + 1, b * PAIR_BLK : (b + 1) * PAIR_BLK
            ]
    for b in range(blocks):
        wide[3 * blocks + b : 3 * blocks + b + 1, :] = jnp.full((1, PAIR_BLK), counts[b], jnp.int32).astype(f32)
    true_pay[...] = wide[...].astype(bf16)
    bias[...] = jnp.where((pos >= 0) & (pos < total_atoms), 0.0, -1e30)
    pl.semaphore_wait(barrier, 3 * sample_peers - 1 + nz + nx - 2)
    true_gather = Gather(atom_peers, true_pay, gathered_true, sems[8:12])
    pred_gather = Gather(atom_peers, pay, gathered_pred, sems[12:16])

    def part_copy(step):
        peer = lax.rem(mine + step, sample_peers)
        at = pl.multiple_of(peer * share, share)
        return remote(
            partial.at[pl.ds(at, share)], arrived.at[step], part_send.at[step], part_recv.at[step],
            me, peer,
        )

    parts = [part_copy(step) for step in range(1, sample_peers)]
    for copy in parts:
        copy.start()
    near = [
        remote(own_single.at[pl.ds(rows - HALO, HALO)], near_single.at[0],
               near_send.at[0], near_recv.at[0], right, mine),
        remote(own_single.at[pl.ds(0, HALO)], near_single.at[1],
               near_send.at[1], near_recv.at[1], left, mine),
        remote(cx.at[:, pl.ds(rows, HALO)], cx.at[:, pl.ds(0, HALO)],
               near_send.at[2], near_recv.at[2], right, mine),
        remote(cx.at[:, pl.ds(HALO, HALO)], cx.at[:, pl.ds(rows + HALO, HALO)],
               near_send.at[3], near_recv.at[3], left, mine),
    ]
    for copy in near:
        copy.start()

    def prepare(k, alone):
        at = pl.multiple_of(k * CHUNK, CHUNK)
        c = cx[:, pl.ds(at, CHUNK)]
        hi, mid, lo = pieces(c)
        coords = jnp.concatenate([hi, hi, hi, mid, mid, lo], axis=0).astype(bf16)
        hid[pl.ds(at, CHUNK), :] = alone.astype(f32) + dot(coords, coord_w, ((0,), (0,)))
        rel = c[3:4, :].astype(jnp.int32) - (first_tok - TOK_HALO + k * (CHUNK // 8))
        hot = jnp.where(lax.broadcasted_iota(jnp.int32, (CHANNELS, CHUNK), 0) == rel, 1.0, 0.0)
        hots[pl.ds(at, CHUNK), :] = hot.T.astype(bf16)

    def prepare_own(k, _):
        prepare(k, own_single[pl.ds(pl.multiple_of((k - 1) * CHUNK, CHUNK), CHUNK), :])
        return 0

    lax.fori_loop(1, 1 + rows // CHUNK, prepare_own, 0, unroll=4)
    for copy in parts:
        copy.wait_recv()
    total = partial[pl.ds(pl.multiple_of(mine * share, share), share), :]
    for step in range(1, sample_peers):
        total = total + arrived[step]
    slab[...] = total.astype(bf16)
    my_rows = pl.ds(pl.multiple_of(TOK_HALO + mine * share, 16), share)
    tok[my_rows, :] = slab[...]

    def tok_copy(step):
        return remote(
            slab, tok.at[my_rows], tok_send.at[step], tok_recv.at[step],
            me, lax.rem(mine + step, sample_peers),
        )

    toks = [tok_copy(step) for step in range(1, sample_peers)]
    for copy in toks:
        copy.start()
    tokens = tok.shape[0] - 2 * TOK_HALO
    rest = TOK_HALO - share
    edges = (
        (sample_peers - 1, pl.ds(0, share), pl.ds(rest, share), right),
        (sample_peers - 2, pl.ds(share - rest, rest), pl.ds(0, rest), right),
        (0, pl.ds(0, share), pl.ds(TOK_HALO + tokens, share), left),
        (1, pl.ds(0, rest), pl.ds(TOK_HALO + tokens + share, rest), left),
    )

    def edge_copy(i, step):
        _, src, dst, to = edges[i]
        return remote(
            slab.at[src], tok.at[dst], edge_send.at[step], edge_recv.at[i],
            to, lax.rem(mine + step, sample_peers),
        )

    for i, edge in enumerate(edges):
        @pl.when(mine == edge[0])
        def _(i=i):
            for step in range(sample_peers):
                edge_copy(i, step).start()

    for copy in near:
        copy.wait_recv()
    prepare(0, near_single[0])
    prepare(ext // CHUNK - 1, near_single[1])
    for copy in toks:
        copy.wait_recv()
    for i in range(len(edges)):
        edge_copy(i, 0).wait_recv()
    true_gather.start()

    def project(layer, at, h):
        normed = (rms_scale(h) * gains[layer, 0:1, :]).astype(bf16)
        out = dot(normed, wqkv[layer])
        rows_at = pl.ds(at, h.shape[0])
        kv[layer % 2, rows_at, :] = out[:, 128:].astype(bf16)
        for t in range(h.shape[0] // CHANNELS):
            turned = (out[t * CHANNELS : (t + 1) * CHANNELS, :128] * q_scale).T
            shifted = [turned if r == 0 else pltpu.roll(turned, r * QBLK, 1) for r in range(HEADS)]
            for w in range(CHANNELS // QBLK):
                spread = jnp.concatenate(
                    [
                        jnp.where(lane == h, shifted[(h - w) % HEADS][h * QBLK : (h + 1) * QBLK], 0.0)
                        for h in range(HEADS)
                    ],
                    axis=0,
                )
                queries[layer % 2, at // QBLK + t * HEADS + w] = spread.astype(bf16)

    def first(k, _):
        at = pl.multiple_of(k * CHUNK, CHUNK)
        tok_at = pl.ds(pl.multiple_of(k * (CHUNK // 8), CHUNK // 8), TOK_WIN)
        h = hid[pl.ds(at, CHUNK), :] + dot(hots[pl.ds(at, CHUNK), 0:TOK_WIN], tok[tok_at, :])
        hid[pl.ds(at, CHUNK), :] = h
        project(0, at, h)
        return 0

    lax.fori_loop(0, ext // CHUNK, first, 0, unroll=FIRST_UNROLL)

    true_gather.forward()

    def attend(layer, at, size):
        buf = layer % 2
        outs = []
        for w in range(size // QBLK):
            keys_at = pl.ds(at + (w * QBLK - 48), KWIN)
            keys = kv[buf, keys_at, 0:128]
            values = kv[buf, keys_at, 128:256]
            scores = dot(keys, queries[buf, at // QBLK + w]) + bias[keys_at, :]
            top = jnp.max(scores, axis=0, keepdims=True)
            weights = jnp.exp2(scores - top)
            weights = (weights * (1.0 / jnp.sum(weights, axis=0, keepdims=True))).astype(bf16)
            both = dot(weights, values, ((0,), (0,)))
            out = both[0:QBLK]
            for h in range(1, HEADS):
                out = jnp.where(lane == h, both[h * QBLK : (h + 1) * QBLK], out)
            outs.append(out.astype(bf16))
        return jnp.concatenate(outs, axis=0)

    def block(layer, at, size):
        h = hid[pl.ds(at, size), :]
        h = h + dot(attend(layer, at, size), wo[layer])
        normed = (rms_scale(h) * gains[layer, 1:2, :]).astype(bf16)
        gu = dot(normed, wgu[layer])
        gate = 0.5 * gu[:, :FF_ATOM]
        inner = (gate * (1.0 + jnp.tanh(gate)) * gu[:, FF_ATOM:]).astype(bf16)
        h = h + dot(inner, wdown[layer])
        if layer + 1 < LAYERS:
            hid[pl.ds(at, size), :] = h
            project(layer + 1, at, h)
        else:
            normed = rms_scale(h)
            hi = normed.astype(bf16)
            mid = (normed - hi.astype(f32)).astype(bf16)
            update = dot(jnp.concatenate([hi, mid, hi], axis=1), head)
            update = jnp.concatenate(
                [update[t * CHANNELS : (t + 1) * CHANNELS].T[0:8] for t in range(size // CHANNELS)],
                axis=1,
            )
            noisy = cx[:, pl.ds(at, size)]
            out = inv * (4.0 * noisy + (2.0 * sig) * update)
            pred[:, pl.ds(pl.multiple_of(at - HALO, 128), size)] = out
            first_block = (at - HALO) // PAIR_BLK
            for d in range(3):
                for i in range(size // PAIR_BLK):
                    wide[pl.ds(d * blocks + first_block + i, 1), :] = out[
                        d : d + 1, i * PAIR_BLK : (i + 1) * PAIR_BLK
                    ]

    for layer in range(LAYERS):
        low = HALO if layer == LAYERS - 1 else HALO - 128
        size = (rows if layer == LAYERS - 1 else rows + 256) // 2

        @pl.loop(0, 2)
        def _(k, layer=layer, low=low, size=size):
            block(layer, pl.multiple_of(low + k * size, 128), size)

    pay[...] = wide[0 : 3 * blocks, :].astype(bf16)
    pred_gather.start()

    diagonal = lax.broadcasted_iota(jnp.int32, (PAIR_BLK, PAIR_BLK), 0) == lax.broadcasted_iota(
        jnp.int32, (PAIR_BLK, PAIR_BLK), 1
    )
    none = jnp.zeros((16, PAIR_BLK), f32)

    def within(group):
        begun = []
        for b in group:
            at = slice(b * PAIR_BLK, (b + 1) * PAIR_BLK)
            ours = [pred[d : d + 1, at] for d in range(3)]
            known = [true[d : d + 1, at] for d in range(3)]
            own = jnp.concatenate(
                [
                    jnp.concatenate([own_features(*ours), none], axis=1),
                    jnp.concatenate([none, own_features(*known)], axis=1),
                ],
                axis=0,
            ).astype(bf16)
            owns[b] = own
            part = jnp.concatenate(
                [partner_features(*(v.astype(bf16).astype(f32) for v in vs)) for vs in (ours, known)],
                axis=0,
            ).astype(bf16)
            begun.append((part[0:16], dot(part, own, ((0,), (0,)))))
        coefs = [jnp.where(diagonal, 0.0, pair_coef(squares)).astype(bf16) for _, squares in begun]
        for b, (part, _), coef in zip(group, begun, coefs):
            selves[b] = dot(part, coef)[8:16]

    within(range(blocks // 2))
    pred_gather.forward()
    within(range(blocks // 2, blocks))
    for copy in parts + near + toks:
        copy.wait_send()
    for i, edge in enumerate(edges):
        @pl.when(mine == edge[0])
        def _(i=i):
            for step in range(sample_peers):
                edge_copy(i, step).wait_send()

    true_gather.finish()
    pred_gather.finish()


def pairs_kernel(
    sigma, counts, partners, gathered_pred, gathered_true, owns, selves, pred, true,
    coord_grad, lddt_grad, wide_pred, wide_true, totals, held, parts,
):
    blocks = counts.shape[0]
    wide_pred[...] = gathered_pred[...].astype(f32)
    wide_true[...] = gathered_true[...].astype(f32)
    totals[0:blocks] = selves[...]
    totals[blocks] = jnp.zeros((8, PAIR_BLK), f32)

    def rows_of(wide, base):
        return partner_features(*(wide[pl.ds(base + d * blocks, 1), :] for d in range(3)))

    def begin(b, m):
        known = jnp.minimum(b, blocks - 1)
        p = partners[known, m]
        owner, place = p // blocks, p % blocks
        part_pred = rows_of(wide_pred, owner * (3 * blocks) + place)
        part_true = rows_of(wide_true, owner * (4 * blocks) + place)
        part = jnp.concatenate([part_pred, part_true], axis=0).astype(bf16)
        squares = dot(part, owns[known], ((0,), (0,)))
        count = counts[known]
        row = jnp.where(m < count, b, blocks)
        last = m + 1 >= count
        return part, squares, row, (jnp.where(last, jnp.minimum(b + 1, blocks), b), jnp.where(last, 1, m + 1))

    def start(slot, b, m):
        rows = []
        for i in range(UNROLL):
            part, squares, row, (b, m) = begin(b, m)
            parts[slot, i] = part[0:16]
            held[slot, i] = squares
            rows.append(row)
        return rows, (b, m)

    def end(slot, rows):
        coefs = [pair_coef(held[slot, i]).astype(bf16) for i in range(UNROLL)]
        found = [dot(parts[slot, i], coef)[8:16] for i, coef in enumerate(coefs)]
        for row, sums in zip(rows, found):
            totals[row] = totals[row] + sums

    def visit(_, carry):
        rows, place = carry
        more, place = start(1, *place)
        end(0, rows)
        rows, place = start(0, *place)
        end(1, more)
        return rows, place

    live = jnp.maximum(counts[0] - 1, 1)
    for b in range(1, blocks):
        live = live + jnp.maximum(counts[b] - 1, 1)
    groups = (live + UNROLL - 1) // UNROLL
    rows, _ = lax.fori_loop(0, groups // 2, visit, start(0, jnp.int32(0), jnp.int32(1)))

    @pl.when(groups % 2 == 1)
    def _():
        end(0, rows)

    square = sigma[0] * sigma[0]
    mse_scale = jnp.full((1, PAIR_BLK), square + 4.0, f32) / jnp.full((1, PAIR_BLK), 6.0 * square, f32)
    peers = gathered_true.shape[0] // (4 * blocks)
    listed = jnp.zeros((blocks, PAIR_BLK), f32)
    for peer in range(peers):
        listed = listed + wide_true[peer * 4 * blocks + 3 * blocks : (peer + 1) * 4 * blocks, :]
    listed = jnp.sum(listed, axis=0, keepdims=True)
    total_pairs = listed * (PAIR_BLK * PAIR_BLK) - float(PAIR_BLK * blocks * peers)
    pair_scale = -0.0625 * (blocks * peers * PAIR_BLK * PAIR_BLK) / total_pairs
    for b in range(blocks):
        at = slice(b * PAIR_BLK, (b + 1) * PAIR_BLK)
        total = totals[b]
        for d in range(3):
            pc, tc = pred[d : d + 1, at], true[d : d + 1, at]
            lg = pair_scale * (pc * total[4:5] - total[d : d + 1])
            lddt_grad[d, :, at] = lg
            coord_grad[d, :, at] = mse_scale * (pc - tc) - lg * (1.0 / PAIR_BLK)


def vmem(n):
    return [pl.BlockSpec(memory_space=pltpu.VMEM)] * n


def smem(n):
    return [pl.BlockSpec(memory_space=pltpu.SMEM)] * n


def run_atoms(
    sigma, counts, feats, proj, single, token, true, noise,
    coord_in, w_qkv, w_o, w_gu, w_down, gains, w_out,
):
    rows, tokens = single.shape[0], feats.shape[1]
    ext = rows + 2 * HALO
    blocks = rows // PAIR_BLK
    atom_peers, sample_peers = lax.axis_size("atoms"), lax.axis_size("samples")
    part = tokens // sample_peers
    dma = pltpu.SemaphoreType.DMA
    one_gather = [dma((DEPTH,)), dma((DEPTH,)), dma((atom_peers,)), dma((atom_peers,))]
    return pl.pallas_call(
        functools.partial(atoms_kernel, atom_peers, sample_peers),
        name="atoms",
        out_shape=(
            jax.ShapeDtypeStruct((8, rows), f32),
            jax.ShapeDtypeStruct((atom_peers * 3 * blocks, PAIR_BLK), bf16),
            jax.ShapeDtypeStruct((atom_peers * 4 * blocks, PAIR_BLK), bf16),
            jax.ShapeDtypeStruct((blocks, 32, 2 * PAIR_BLK), bf16),
            jax.ShapeDtypeStruct((blocks, 8, PAIR_BLK), f32),
        ),
        in_specs=smem(2) + vmem(13),
        out_specs=tuple(vmem(5)),
        scratch_shapes=[
            pltpu.VMEM((ext, CHANNELS), f32),
            pltpu.VMEM((2, ext, 2 * CHANNELS), bf16),
            pltpu.VMEM((2, ext // QBLK, CHANNELS, CHANNELS), bf16),
            pltpu.VMEM((ext, CHANNELS), f32),
            pltpu.VMEM((3 * blocks, PAIR_BLK), bf16),
            pltpu.VMEM((4 * blocks, PAIR_BLK), bf16),
            pltpu.VMEM((4 * blocks, PAIR_BLK), f32),
            pltpu.VMEM((tokens + 2 * TOK_HALO, CHANNELS), bf16),
            pltpu.VMEM((2, HALO, CHANNELS), bf16),
            pltpu.VMEM((8, ext), f32),
            pltpu.VMEM((ext, CHANNELS), bf16),
            pltpu.VMEM((tokens, CHANNELS), f32),
            pltpu.VMEM((sample_peers, part, CHANNELS), f32),
            pltpu.VMEM((part, CHANNELS), bf16),
            dma((sample_peers,)), dma((sample_peers,)), dma((sample_peers,)), dma((sample_peers,)),
            dma((sample_peers,)), dma((4,)), dma((4,)), dma((4,)),
        ]
        + 2 * one_gather,
        compiler_params=pltpu.CompilerParams(
            collective_id=0, has_side_effects=True, vmem_limit_bytes=VMEM_LIMIT
        ),
    )(
        sigma, counts, feats, proj, single, token, true, noise,
        coord_in, w_qkv, w_o, w_gu, w_down, gains, w_out.T,
    )


def run_pairs(sigma, counts, partners, gathered_pred, gathered_true, owns, selves, pred, true):
    rows = pred.shape[1]
    out = jax.ShapeDtypeStruct((3, 1, rows), f32)
    coord_grad, lddt_grad = pl.pallas_call(
        pairs_kernel,
        name="pairs",
        out_shape=(out, out),
        in_specs=smem(3) + vmem(6),
        out_specs=tuple(vmem(2)),
        scratch_shapes=[pltpu.VMEM(g.shape, f32) for g in (gathered_pred, gathered_true)]
        + [
            pltpu.VMEM((rows // PAIR_BLK + 1, 8, PAIR_BLK), f32),
            pltpu.VMEM((2, UNROLL, PAIR_BLK, 2 * PAIR_BLK), f32),
            pltpu.VMEM((2, UNROLL, 16, PAIR_BLK), bf16),
        ],
        compiler_params=pltpu.CompilerParams(vmem_limit_bytes=VMEM_LIMIT),
    )(sigma, counts, partners, gathered_pred, gathered_true, owns, selves, pred, true)
    return jnp.swapaxes(coord_grad, 0, 1), jnp.swapaxes(lddt_grad, 0, 1)


def on_device(
    token_feats, proj_w, atom_single, atom_token, true_coords, noise, sigma, coord_in,
    w_qkv, w_o, w_gu, w_down, gains, w_out, pair_blocks, pair_count,
):
    pred, gathered_pred, gathered_true, owns, selves = run_atoms(
        sigma, pair_count, token_feats.T, proj_w, atom_single, atom_token[None], true_coords,
        jnp.swapaxes(noise, 0, 1), coord_in, w_qkv, w_o, w_gu, w_down, gains, w_out,
    )
    return run_pairs(
        sigma, pair_count, pair_blocks, gathered_pred, gathered_true, owns, selves, pred, true_coords
    )


def solution(mesh):
    in_specs = (
        P("atoms", "samples"),
        P("samples", None),
        P("atoms", None),
        P("atoms"),
        P(None, "atoms"),
        P("samples", None, "atoms"),
        P("samples"),
        P(), P(), P(), P(), P(), P(), P(),
        P("atoms", None),
        P("atoms"),
    )
    out_specs = (P("samples", None, "atoms"), P("samples", None, "atoms"))
    return jax.shard_map(on_device, mesh=mesh, in_specs=in_specs, out_specs=out_specs, check_vma=False)
```

```python
import functools
import math

import jax
import jax.numpy as jnp
from jax import lax
from jax.experimental import pallas as pl
from jax.experimental.pallas import tpu as pltpu
from jax.sharding import PartitionSpec as P

HEADS = 4
HEAD_DIM = 32
FF_ATOM = 256
LAYERS = 3
QBLK = 32
KWIN = 128
PAIR_BLK = 128
CHANNELS = 128
CHUNK = 256
FIRST_UNROLL = 5
UNROLL = 8
HALO = 256
TOK_HALO = 48
TOK_WIN = 64
EPS = 1e-05
DEPTH = 8
VMEM_LIMIT = 56 * 1024 * 1024

f32 = jnp.float32
bf16 = jnp.bfloat16


def dot(a, b, dims=((1,), (0,)), precision=None):
    return lax.dot_general(a, b, (dims, ((), ())), precision=precision, preferred_element_type=f32)


def pieces(v):
    hi = v.astype(bf16).astype(f32)
    mid = (v - hi).astype(bf16).astype(f32)
    lo = (v - hi - mid).astype(bf16).astype(f32)
    return hi, mid, lo


def rms_scale(h):
    return h * lax.rsqrt(jnp.mean(h * h, axis=1, keepdims=True) + EPS)


MESH = pl.DeviceIdType.MESH


def remote(src, dst, send, recv, atom, sample):
    return pltpu.make_async_remote_copy(
        src_ref=src, dst_ref=dst, send_sem=send, recv_sem=recv,
        device_id=(atom, sample), device_id_type=MESH,
    )

def gather_plan(atom_peers):
    nz = DEPTH
    nx = atom_peers // nz
    me = lax.axis_index("atoms")
    x, z = me // nz, lax.rem(me, nz)

    def along_z(dz):
        return x * nz + lax.rem(z + dz + nz, nz)

    def along_x(dx):
        return lax.rem(x + dx, nx) * nz + z

    return nz, nx, me, along_z, along_x


class Gather:
    def __init__(self, atom_peers, pay, whole, sems):
        self.nz, self.nx, self.me, self.along_z, self.along_x = gather_plan(atom_peers)
        self.mine = lax.axis_index("samples")
        self.pay, self.whole = pay, whole
        self.z_send, self.z_recv, self.x_send, self.x_recv = sems
        self.order = [0]
        for step in range(1, self.nz // 2 + 1):
            self.order += [step, self.nz - step] if 2 * step != self.nz else [step]

    def rows(self, owner):
        size = self.pay.shape[0]
        return pl.ds(pl.multiple_of(owner * size, size), size)

    def z_copy(self, dz):
        return remote(
            self.pay, self.whole.at[self.rows(self.me)], self.z_send.at[dz], self.z_recv.at[dz],
            self.along_z(dz), self.mine,
        )

    def x_copy(self, dz, dx):
        at = self.rows(self.along_z(-dz))
        src = self.pay if dz == 0 else self.whole.at[at]
        slot = dz * self.nx + dx
        return remote(
            src, self.whole.at[at], self.x_send.at[slot], self.x_recv.at[slot],
            self.along_x(dx), self.mine,
        )

    def line_copy(self, dx):
        size = self.pay.shape[0] * self.nz
        at = pl.ds(pl.multiple_of(self.me // self.nz * size, size), size)
        line = self.whole.at[at]
        return remote(line, line, self.x_send.at[dx], self.x_recv.at[dx], self.along_x(dx), self.mine)

    def start_lines(self):
        self.whole[self.rows(self.me), :] = self.pay[...]
        for dz in self.order[1:]:
            self.z_copy(dz).start()

    def forward_lines(self):
        for dz in self.order[1:]:
            self.z_copy(dz).wait_recv()
        for dx in range(1, self.nx):
            self.line_copy(dx).start()

    def finish_lines(self):
        for dz in self.order[1:]:
            self.z_copy(dz).wait_send()
        for dx in range(1, self.nx):
            self.line_copy(dx).wait()

    def start(self):
        for dz in self.order[1:]:
            self.z_copy(dz).start()
        for dx in range(1, self.nx):
            self.x_copy(0, dx).start()
        self.whole[self.rows(self.me), :] = self.pay[...]

    def forward(self):
        for dz in self.order[1:]:
            self.z_copy(dz).wait_recv()
            for dx in range(1, self.nx):
                self.x_copy(dz, dx).start()

    def finish(self):
        for dz in self.order[1:]:
            self.z_copy(dz).wait_send()
        for dz in self.order:
            for dx in range(1, self.nx):
                self.x_copy(dz, dx).wait()


def partner_features(x, y, z):
    row8 = lax.broadcasted_iota(jnp.int32, (8, PAIR_BLK), 0)
    row4 = row8 & 3
    n1, n2, n3 = pieces(x * x + y * y + z * z)
    xyz = jnp.where(row4 == 0, x, jnp.where(row4 == 1, y, z))
    upper = jnp.where(row4 == 3, jnp.where(row8 == 3, n1, n2), xyz)
    ones = jnp.where(row8 < 7, 1.0, 0.0)
    lower = jnp.where(row8 < 3, xyz, jnp.where(row8 == 3, n3, ones))
    return jnp.concatenate([upper, lower], axis=0)


def own_features(x, y, z):
    row8 = lax.broadcasted_iota(jnp.int32, (8, PAIR_BLK), 0)
    row4 = row8 & 3
    n1, n2, n3 = pieces(0.25 * (x * x + y * y + z * z + 1.0))
    xp, yp, zp = pieces(-0.5 * x), pieces(-0.5 * y), pieces(-0.5 * z)

    def xyz(i):
        return jnp.where(row4 == 0, xp[i], jnp.where(row4 == 1, yp[i], zp[i]))

    upper = jnp.where(row4 == 3, 0.25, jnp.where(row8 < 4, xyz(0), xyz(1)))
    norms = jnp.where(row8 == 4, n1, jnp.where(row8 == 5, n2, n3))
    norms = jnp.where(row8 == 7, 0.0, norms)
    lower = jnp.where(row8 < 3, xyz(2), jnp.where(row8 == 3, 0.25, norms))
    return jnp.concatenate([upper, lower], axis=0)


def pair_coef(squares):
    sp, st = squares[:, :PAIR_BLK], squares[:, PAIR_BLK:]
    rp = lax.rsqrt(sp)
    gap = sp * rp - st * lax.rsqrt(st)
    e2 = gap * gap + 0.0025
    re = lax.rsqrt(e2)
    err = e2 * re
    th = [jnp.tanh(0.5 * t - err) for t in (0.5, 1.0, 2.0, 4.0)]
    slope = 4.0 - (th[0] * th[0] + th[1] * th[1] + th[2] * th[2] + th[3] * th[3])
    return slope * gap * (re * rp)


def atoms_kernel(
    atom_peers, sample_peers, sigma, counts, feats, proj, own_single, token, true, noise,
    coord_in, wqkv, wo, wgu, wdown, gains, wout,
    pred, gathered_pred, gathered_true, owns, selves,
    hid, kv, queries, bias, pay, true_pay, wide, tok, near_single, cx, hots, partial, arrived, slab, *sems,
):
    rows = own_single.shape[0]
    ext = rows + 2 * HALO
    blocks = rows // PAIR_BLK
    nz, nx, me, along_z, along_x = gather_plan(atom_peers)
    mine = lax.axis_index("samples")
    barrier = pltpu.get_barrier_semaphore()
    right = lax.rem(me + 1, atom_peers)
    left = lax.rem(me + atom_peers - 1, atom_peers)
    share = feats.shape[1] // sample_peers
    (part_send, part_recv, tok_send, tok_recv, edge_send, edge_recv, near_send, near_recv) = sems[:8]

    def greet(atom, sample):
        pl.semaphore_signal(barrier, inc=1, device_id=(atom, sample), device_id_type=MESH)

    for step in range(1, sample_peers):
        greet(me, lax.rem(mine + step, sample_peers))
    for step in range(sample_peers):
        greet(left, lax.rem(mine + step, sample_peers))
        greet(right, lax.rem(mine + step, sample_peers))

    for dz in range(1, nz):
        greet(along_z(dz), mine)
    for dx in range(1, nx):
        greet(along_x(dx), mine)
    first_atom = me * rows
    total_atoms = rows * atom_peers
    first_tok = me * (tok.shape[0] - 2 * TOK_HALO)
    sig = sigma[0]
    inv = lax.rsqrt(jnp.full((8, CHANNELS), sig * sig + 4.0, f32))[0:1, 0:1]
    zero5 = jnp.zeros((5, CHANNELS), f32)
    hi, mid, lo = pieces(jnp.concatenate([coord_in[...], zero5], axis=0))
    coord_w = jnp.concatenate([hi, mid, lo, hi, mid, hi], axis=0).astype(bf16)
    head = jnp.concatenate([wout[...], jnp.zeros((CHANNELS - 3, CHANNELS), f32)], axis=0).T
    hi, mid, lo = pieces(head)
    head = jnp.concatenate([hi, hi, mid], axis=0).astype(bf16)
    q_scale = math.log2(math.e) / math.sqrt(HEAD_DIM)
    lane = lax.broadcasted_iota(jnp.int32, (1, CHANNELS), 1) // HEAD_DIM

    pos = first_atom - HALO + lax.broadcasted_iota(jnp.int32, (ext, CHANNELS), 0)
    partial[...] = dot(feats[...], proj[...], ((0,), (0,)))
    cx[3:8, pl.ds(HALO, rows)] = jnp.concatenate(
        [token[...].astype(f32), jnp.zeros((4, rows), f32)], axis=0
    )
    for d in range(3):
        cx[d : d + 1, pl.ds(HALO, rows)] = (true[d : d + 1, :] + sig * noise[d]) * inv
    for d in range(3):
        for b in range(blocks):
            wide[d * blocks + b : d * blocks + b + 1, :] = true[
                d : d + 1, b * PAIR_BLK : (b + 1) * PAIR_BLK
            ]
    for b in range(blocks):
        wide[3 * blocks + b : 3 * blocks + b + 1, :] = jnp.full((1, PAIR_BLK), counts[b], jnp.int32).astype(f32)
    true_pay[...] = wide[...].astype(bf16)
    bias[...] = jnp.where((pos >= 0) & (pos < total_atoms), 0.0, -1e30)
    pl.semaphore_wait(barrier, 3 * sample_peers - 1 + nz + nx - 2)
    true_gather = Gather(atom_peers, true_pay, gathered_true, sems[8:12])
    pred_gather = Gather(atom_peers, pay, gathered_pred, sems[12:16])

    def part_copy(step):
        peer = lax.rem(mine + step, sample_peers)
        at = pl.multiple_of(peer * share, share)
        return remote(
            partial.at[pl.ds(at, share)], arrived.at[step], part_send.at[step], part_recv.at[step],
            me, peer,
        )

    parts = [part_copy(step) for step in range(1, sample_peers)]
    for copy in parts:
        copy.start()
    near = [
        remote(own_single.at[pl.ds(rows - HALO, HALO)], near_single.at[0],
               near_send.at[0], near_recv.at[0], right, mine),
        remote(own_single.at[pl.ds(0, HALO)], near_single.at[1],
               near_send.at[1], near_recv.at[1], left, mine),
        remote(cx.at[:, pl.ds(rows, HALO)], cx.at[:, pl.ds(0, HALO)],
               near_send.at[2], near_recv.at[2], right, mine),
        remote(cx.at[:, pl.ds(HALO, HALO)], cx.at[:, pl.ds(rows + HALO, HALO)],
               near_send.at[3], near_recv.at[3], left, mine),
    ]
    for copy in near:
        copy.start()

    def prepare(k, alone):
        at = pl.multiple_of(k * CHUNK, CHUNK)
        c = cx[:, pl.ds(at, CHUNK)]
        hi, mid, lo = pieces(c)
        coords = jnp.concatenate([hi, hi, hi, mid, mid, lo], axis=0).astype(bf16)
        hid[pl.ds(at, CHUNK), :] = alone.astype(f32) + dot(coords, coord_w, ((0,), (0,)))
        rel = c[3:4, :].astype(jnp.int32) - (first_tok - TOK_HALO + k * (CHUNK // 8))
        hot = jnp.where(lax.broadcasted_iota(jnp.int32, (CHANNELS, CHUNK), 0) == rel, 1.0, 0.0)
        hots[pl.ds(at, CHUNK), :] = hot.T.astype(bf16)

    def prepare_own(k, _):
        prepare(k, own_single[pl.ds(pl.multiple_of((k - 1) * CHUNK, CHUNK), CHUNK), :])
        return 0

    lax.fori_loop(1, 1 + rows // CHUNK, prepare_own, 0, unroll=4)
    for copy in parts:
        copy.wait_recv()
    total = partial[pl.ds(pl.multiple_of(mine * share, share), share), :]
    for step in range(1, sample_peers):
        total = total + arrived[step]
    slab[...] = total.astype(bf16)
    my_rows = pl.ds(pl.multiple_of(TOK_HALO + mine * share, 16), share)
    tok[my_rows, :] = slab[...]

    def tok_copy(step):
        return remote(
            slab, tok.at[my_rows], tok_send.at[step], tok_recv.at[step],
            me, lax.rem(mine + step, sample_peers),
        )

    toks = [tok_copy(step) for step in range(1, sample_peers)]
    for copy in toks:
        copy.start()
    tokens = tok.shape[0] - 2 * TOK_HALO
    rest = TOK_HALO - share
    edges = (
        (sample_peers - 1, pl.ds(0, share), pl.ds(rest, share), right),
        (sample_peers - 2, pl.ds(share - rest, rest), pl.ds(0, rest), right),
        (0, pl.ds(0, share), pl.ds(TOK_HALO + tokens, share), left),
        (1, pl.ds(0, rest), pl.ds(TOK_HALO + tokens + share, rest), left),
    )

    def edge_copy(i, step):
        _, src, dst, to = edges[i]
        return remote(
            slab.at[src], tok.at[dst], edge_send.at[step], edge_recv.at[i],
            to, lax.rem(mine + step, sample_peers),
        )

    for i, edge in enumerate(edges):
        @pl.when(mine == edge[0])
        def _(i=i):
            for step in range(sample_peers):
                edge_copy(i, step).start()

    true_gather.start_lines()
    for copy in near:
        copy.wait_recv()
    prepare(0, near_single[0])
    prepare(ext // CHUNK - 1, near_single[1])
    for copy in toks:
        copy.wait_recv()
    for i in range(len(edges)):
        edge_copy(i, 0).wait_recv()

    def project(layer, at, h):
        normed = (rms_scale(h) * gains[layer, 0:1, :]).astype(bf16)
        out = dot(normed, wqkv[layer])
        rows_at = pl.ds(at, h.shape[0])
        kv[layer % 2, rows_at, :] = out[:, 128:].astype(bf16)
        for t in range(h.shape[0] // CHANNELS):
            turned = (out[t * CHANNELS : (t + 1) * CHANNELS, :128] * q_scale).T
            shifted = [turned if r == 0 else pltpu.roll(turned, r * QBLK, 1) for r in range(HEADS)]
            for w in range(CHANNELS // QBLK):
                spread = jnp.concatenate(
                    [
                        jnp.where(lane == h, shifted[(h - w) % HEADS][h * QBLK : (h + 1) * QBLK], 0.0)
                        for h in range(HEADS)
                    ],
                    axis=0,
                )
                queries[layer % 2, at // QBLK + t * HEADS + w] = spread.astype(bf16)

    def first(k, _):
        at = pl.multiple_of(k * CHUNK, CHUNK)
        tok_at = pl.ds(pl.multiple_of(k * (CHUNK // 8), CHUNK // 8), TOK_WIN)
        h = hid[pl.ds(at, CHUNK), :] + dot(hots[pl.ds(at, CHUNK), 0:TOK_WIN], tok[tok_at, :])
        hid[pl.ds(at, CHUNK), :] = h
        project(0, at, h)
        return 0

    lax.fori_loop(0, ext // CHUNK, first, 0, unroll=FIRST_UNROLL)

    true_gather.forward_lines()

    def attend(layer, at, size):
        buf = layer % 2
        outs = []
        for w in range(size // QBLK):
            keys_at = pl.ds(at + (w * QBLK - 48), KWIN)
            keys = kv[buf, keys_at, 0:128]
            values = kv[buf, keys_at, 128:256]
            scores = dot(keys, queries[buf, at // QBLK + w]) + bias[keys_at, :]
            top = jnp.max(scores, axis=0, keepdims=True)
            weights = jnp.exp2(scores - top)
            weights = (weights * (1.0 / jnp.sum(weights, axis=0, keepdims=True))).astype(bf16)
            both = dot(weights, values, ((0,), (0,)))
            out = both[0:QBLK]
            for h in range(1, HEADS):
                out = jnp.where(lane == h, both[h * QBLK : (h + 1) * QBLK], out)
            outs.append(out.astype(bf16))
        return jnp.concatenate(outs, axis=0)

    def block(layer, at, size):
        h = hid[pl.ds(at, size), :]
        h = h + dot(attend(layer, at, size), wo[layer])
        normed = (rms_scale(h) * gains[layer, 1:2, :]).astype(bf16)
        gu = dot(normed, wgu[layer])
        gate = 0.5 * gu[:, :FF_ATOM]
        inner = (gate * (1.0 + jnp.tanh(gate)) * gu[:, FF_ATOM:]).astype(bf16)
        h = h + dot(inner, wdown[layer])
        if layer + 1 < LAYERS:
            hid[pl.ds(at, size), :] = h
            project(layer + 1, at, h)
        else:
            normed = rms_scale(h)
            hi = normed.astype(bf16)
            mid = (normed - hi.astype(f32)).astype(bf16)
            update = dot(jnp.concatenate([hi, mid, hi], axis=1), head)
            update = jnp.concatenate(
                [update[t * CHANNELS : (t + 1) * CHANNELS].T[0:8] for t in range(size // CHANNELS)],
                axis=1,
            )
            noisy = cx[:, pl.ds(at, size)]
            out = inv * (4.0 * noisy + (2.0 * sig) * update)
            pred[:, pl.ds(pl.multiple_of(at - HALO, 128), size)] = out
            first_block = (at - HALO) // PAIR_BLK
            for d in range(3):
                for i in range(size // PAIR_BLK):
                    wide[pl.ds(d * blocks + first_block + i, 1), :] = out[
                        d : d + 1, i * PAIR_BLK : (i + 1) * PAIR_BLK
                    ]

    for layer in range(LAYERS):
        low = HALO if layer == LAYERS - 1 else HALO - 128
        size = (rows if layer == LAYERS - 1 else rows + 256) // 2

        @pl.loop(0, 2)
        def _(k, layer=layer, low=low, size=size):
            block(layer, pl.multiple_of(low + k * size, 128), size)

    pay[...] = wide[0 : 3 * blocks, :].astype(bf16)
    pred_gather.start()

    diagonal = lax.broadcasted_iota(jnp.int32, (PAIR_BLK, PAIR_BLK), 0) == lax.broadcasted_iota(
        jnp.int32, (PAIR_BLK, PAIR_BLK), 1
    )
    none = jnp.zeros((16, PAIR_BLK), f32)

    def within(group):
        begun = []
        for b in group:
            at = slice(b * PAIR_BLK, (b + 1) * PAIR_BLK)
            ours = [pred[d : d + 1, at] for d in range(3)]
            known = [true[d : d + 1, at] for d in range(3)]
            own = jnp.concatenate(
                [
                    jnp.concatenate([own_features(*ours), none], axis=1),
                    jnp.concatenate([none, own_features(*known)], axis=1),
                ],
                axis=0,
            ).astype(bf16)
            owns[b] = own
            part = jnp.concatenate(
                [partner_features(*(v.astype(bf16).astype(f32) for v in vs)) for vs in (ours, known)],
                axis=0,
            ).astype(bf16)
            begun.append((part[0:16], dot(part, own, ((0,), (0,)))))
        coefs = [jnp.where(diagonal, 0.0, pair_coef(squares)).astype(bf16) for _, squares in begun]
        for b, (part, _), coef in zip(group, begun, coefs):
            selves[b] = dot(part, coef)[8:16]

    within(range(blocks // 2))
    pred_gather.forward()
    within(range(blocks // 2, blocks))
    for copy in parts + near + toks:
        copy.wait_send()
    for i, edge in enumerate(edges):
        @pl.when(mine == edge[0])
        def _(i=i):
            for step in range(sample_peers):
                edge_copy(i, step).wait_send()

    true_gather.finish_lines()
    pred_gather.finish()


def pairs_kernel(
    sigma, counts, partners, gathered_pred, gathered_true, owns, selves, pred, true,
    coord_grad, lddt_grad, wide_pred, wide_true, totals, held, parts,
):
    blocks = counts.shape[0]
    wide_pred[...] = gathered_pred[...].astype(f32)
    wide_true[...] = gathered_true[...].astype(f32)
    totals[0:blocks] = selves[...]
    totals[blocks] = jnp.zeros((8, PAIR_BLK), f32)

    def rows_of(wide, base):
        return partner_features(*(wide[pl.ds(base + d * blocks, 1), :] for d in range(3)))

    def begin(b, m):
        known = jnp.minimum(b, blocks - 1)
        p = partners[known, m]
        owner, place = p // blocks, p % blocks
        part_pred = rows_of(wide_pred, owner * (3 * blocks) + place)
        part_true = rows_of(wide_true, owner * (4 * blocks) + place)
        part = jnp.concatenate([part_pred, part_true], axis=0).astype(bf16)
        squares = dot(part, owns[known], ((0,), (0,)))
        count = counts[known]
        row = jnp.where(m < count, b, blocks)
        last = m + 1 >= count
        return part, squares, row, (jnp.where(last, jnp.minimum(b + 1, blocks), b), jnp.where(last, 1, m + 1))

    def start(slot, b, m):
        rows = []
        for i in range(UNROLL):
            part, squares, row, (b, m) = begin(b, m)
            parts[slot, i] = part[0:16]
            held[slot, i] = squares
            rows.append(row)
        return rows, (b, m)

    def end(slot, rows):
        coefs = [pair_coef(held[slot, i]).astype(bf16) for i in range(UNROLL)]
        found = [dot(parts[slot, i], coef)[8:16] for i, coef in enumerate(coefs)]
        for row, sums in zip(rows, found):
            totals[row] = totals[row] + sums

    def visit(_, carry):
        rows, place = carry
        more, place = start(1, *place)
        end(0, rows)
        rows, place = start(0, *place)
        end(1, more)
        return rows, place

    live = jnp.maximum(counts[0] - 1, 1)
    for b in range(1, blocks):
        live = live + jnp.maximum(counts[b] - 1, 1)
    groups = (live + UNROLL - 1) // UNROLL
    rows, _ = lax.fori_loop(0, groups // 2, visit, start(0, jnp.int32(0), jnp.int32(1)))

    @pl.when(groups % 2 == 1)
    def _():
        end(0, rows)

    square = sigma[0] * sigma[0]
    mse_scale = jnp.full((1, PAIR_BLK), square + 4.0, f32) / jnp.full((1, PAIR_BLK), 6.0 * square, f32)
    peers = gathered_true.shape[0] // (4 * blocks)
    listed = jnp.zeros((blocks, PAIR_BLK), f32)
    for peer in range(peers):
        listed = listed + wide_true[peer * 4 * blocks + 3 * blocks : (peer + 1) * 4 * blocks, :]
    listed = jnp.sum(listed, axis=0, keepdims=True)
    total_pairs = listed * (PAIR_BLK * PAIR_BLK) - float(PAIR_BLK * blocks * peers)
    pair_scale = -0.0625 * (blocks * peers * PAIR_BLK * PAIR_BLK) / total_pairs
    for b in range(blocks):
        at = slice(b * PAIR_BLK, (b + 1) * PAIR_BLK)
        total = totals[b]
        for d in range(3):
            pc, tc = pred[d : d + 1, at], true[d : d + 1, at]
            lg = pair_scale * (pc * total[4:5] - total[d : d + 1])
            lddt_grad[d, :, at] = lg
            coord_grad[d, :, at] = mse_scale * (pc - tc) - lg * (1.0 / PAIR_BLK)


def vmem(n):
    return [pl.BlockSpec(memory_space=pltpu.VMEM)] * n


def smem(n):
    return [pl.BlockSpec(memory_space=pltpu.SMEM)] * n


def run_atoms(
    sigma, counts, feats, proj, single, token, true, noise,
    coord_in, w_qkv, w_o, w_gu, w_down, gains, w_out,
):
    rows, tokens = single.shape[0], feats.shape[1]
    ext = rows + 2 * HALO
    blocks = rows // PAIR_BLK
    atom_peers, sample_peers = lax.axis_size("atoms"), lax.axis_size("samples")
    part = tokens // sample_peers
    dma = pltpu.SemaphoreType.DMA
    one_gather = [dma((DEPTH,)), dma((DEPTH,)), dma((atom_peers,)), dma((atom_peers,))]
    return pl.pallas_call(
        functools.partial(atoms_kernel, atom_peers, sample_peers),
        name="atoms",
        out_shape=(
            jax.ShapeDtypeStruct((8, rows), f32),
            jax.ShapeDtypeStruct((atom_peers * 3 * blocks, PAIR_BLK), bf16),
            jax.ShapeDtypeStruct((atom_peers * 4 * blocks, PAIR_BLK), bf16),
            jax.ShapeDtypeStruct((blocks, 32, 2 * PAIR_BLK), bf16),
            jax.ShapeDtypeStruct((blocks, 8, PAIR_BLK), f32),
        ),
        in_specs=smem(2) + vmem(13),
        out_specs=tuple(vmem(5)),
        scratch_shapes=[
            pltpu.VMEM((ext, CHANNELS), f32),
            pltpu.VMEM((2, ext, 2 * CHANNELS), bf16),
            pltpu.VMEM((2, ext // QBLK, CHANNELS, CHANNELS), bf16),
            pltpu.VMEM((ext, CHANNELS), f32),
            pltpu.VMEM((3 * blocks, PAIR_BLK), bf16),
            pltpu.VMEM((4 * blocks, PAIR_BLK), bf16),
            pltpu.VMEM((4 * blocks, PAIR_BLK), f32),
            pltpu.VMEM((tokens + 2 * TOK_HALO, CHANNELS), bf16),
            pltpu.VMEM((2, HALO, CHANNELS), bf16),
            pltpu.VMEM((8, ext), f32),
            pltpu.VMEM((ext, CHANNELS), bf16),
            pltpu.VMEM((tokens, CHANNELS), f32),
            pltpu.VMEM((sample_peers, part, CHANNELS), f32),
            pltpu.VMEM((part, CHANNELS), bf16),
            dma((sample_peers,)), dma((sample_peers,)), dma((sample_peers,)), dma((sample_peers,)),
            dma((sample_peers,)), dma((4,)), dma((4,)), dma((4,)),
        ]
        + 2 * one_gather,
        compiler_params=pltpu.CompilerParams(
            collective_id=0, has_side_effects=True, vmem_limit_bytes=VMEM_LIMIT
        ),
    )(
        sigma, counts, feats, proj, single, token, true, noise,
        coord_in, w_qkv, w_o, w_gu, w_down, gains, w_out.T,
    )


def run_pairs(sigma, counts, partners, gathered_pred, gathered_true, owns, selves, pred, true):
    rows = pred.shape[1]
    out = jax.ShapeDtypeStruct((3, 1, rows), f32)
    coord_grad, lddt_grad = pl.pallas_call(
        pairs_kernel,
        name="pairs",
        out_shape=(out, out),
        in_specs=smem(3) + vmem(6),
        out_specs=tuple(vmem(2)),
        scratch_shapes=[pltpu.VMEM(g.shape, f32) for g in (gathered_pred, gathered_true)]
        + [
            pltpu.VMEM((rows // PAIR_BLK + 1, 8, PAIR_BLK), f32),
            pltpu.VMEM((2, UNROLL, PAIR_BLK, 2 * PAIR_BLK), f32),
            pltpu.VMEM((2, UNROLL, 16, PAIR_BLK), bf16),
        ],
        compiler_params=pltpu.CompilerParams(vmem_limit_bytes=VMEM_LIMIT),
    )(sigma, counts, partners, gathered_pred, gathered_true, owns, selves, pred, true)
    return jnp.swapaxes(coord_grad, 0, 1), jnp.swapaxes(lddt_grad, 0, 1)


def on_device(
    token_feats, proj_w, atom_single, atom_token, true_coords, noise, sigma, coord_in,
    w_qkv, w_o, w_gu, w_down, gains, w_out, pair_blocks, pair_count,
):
    pred, gathered_pred, gathered_true, owns, selves = run_atoms(
        sigma, pair_count, token_feats.T, proj_w, atom_single, atom_token[None], true_coords,
        jnp.swapaxes(noise, 0, 1), coord_in, w_qkv, w_o, w_gu, w_down, gains, w_out,
    )
    return run_pairs(
        sigma, pair_count, pair_blocks, gathered_pred, gathered_true, owns, selves, pred, true_coords
    )


def solution(mesh):
    in_specs = (
        P("atoms", "samples"),
        P("samples", None),
        P("atoms", None),
        P("atoms"),
        P(None, "atoms"),
        P("samples", None, "atoms"),
        P("samples"),
        P(), P(), P(), P(), P(), P(), P(),
        P("atoms", None),
        P("atoms"),
    )
    out_specs = (P("samples", None, "atoms"), P("samples", None, "atoms"))
    return jax.shard_map(on_device, mesh=mesh, in_specs=in_specs, out_specs=out_specs, check_vma=False)
```

```python
import functools
import math

import jax
import jax.numpy as jnp
from jax import lax
from jax.experimental import pallas as pl
from jax.experimental.pallas import tpu as pltpu
from jax.sharding import PartitionSpec as P

HEADS = 4
HEAD_DIM = 32
FF_ATOM = 256
LAYERS = 3
QBLK = 32
KWIN = 128
PAIR_BLK = 128
CHANNELS = 128
CHUNK = 256
FIRST_UNROLL = 5
UNROLL = 8
HALO = 256
TOK_HALO = 48
TOK_WIN = 64
EPS = 1e-05
DEPTH = 8
VMEM_LIMIT = 56 * 1024 * 1024

f32 = jnp.float32
bf16 = jnp.bfloat16


def dot(a, b, dims=((1,), (0,)), precision=None):
    return lax.dot_general(a, b, (dims, ((), ())), precision=precision, preferred_element_type=f32)


def pieces(v):
    hi = v.astype(bf16).astype(f32)
    mid = (v - hi).astype(bf16).astype(f32)
    lo = (v - hi - mid).astype(bf16).astype(f32)
    return hi, mid, lo


def rms_scale(h):
    return h * lax.rsqrt(jnp.mean(h * h, axis=1, keepdims=True) + EPS)


MESH = pl.DeviceIdType.MESH


def remote(src, dst, send, recv, atom, sample):
    return pltpu.make_async_remote_copy(
        src_ref=src, dst_ref=dst, send_sem=send, recv_sem=recv,
        device_id=(atom, sample), device_id_type=MESH,
    )

def gather_plan(atom_peers):
    nz = DEPTH
    nx = atom_peers // nz
    me = lax.axis_index("atoms")
    x, z = me // nz, lax.rem(me, nz)

    def along_z(dz):
        return x * nz + lax.rem(z + dz + nz, nz)

    def along_x(dx):
        return lax.rem(x + dx, nx) * nz + z

    return nz, nx, me, along_z, along_x


class Gather:
    def __init__(self, atom_peers, pay, whole, sems):
        self.nz, self.nx, self.me, self.along_z, self.along_x = gather_plan(atom_peers)
        self.mine = lax.axis_index("samples")
        self.pay, self.whole = pay, whole
        self.z_send, self.z_recv, self.x_send, self.x_recv = sems
        self.order = [0]
        for step in range(1, self.nz // 2 + 1):
            self.order += [step, self.nz - step] if 2 * step != self.nz else [step]

    def rows(self, owner):
        size = self.pay.shape[0]
        return pl.ds(pl.multiple_of(owner * size, size), size)

    def z_copy(self, dz):
        return remote(
            self.pay, self.whole.at[self.rows(self.me)], self.z_send.at[dz], self.z_recv.at[dz],
            self.along_z(dz), self.mine,
        )

    def line_copy(self, dx):
        size = self.pay.shape[0] * self.nz
        at = pl.ds(pl.multiple_of(self.me // self.nz * size, size), size)
        line = self.whole.at[at]
        return remote(line, line, self.x_send.at[dx], self.x_recv.at[dx], self.along_x(dx), self.mine)

    def start_lines(self):
        self.whole[self.rows(self.me), :] = self.pay[...]
        for dz in self.order[1:]:
            self.z_copy(dz).start()

    def forward_lines(self):
        for dz in self.order[1:]:
            self.z_copy(dz).wait_recv()
        for dx in range(1, self.nx):
            self.line_copy(dx).start()

    def finish_lines(self):
        for dz in self.order[1:]:
            self.z_copy(dz).wait_send()
        for dx in range(1, self.nx):
            self.line_copy(dx).wait()

    groups = ((0, 1), (1, 2), (3, 2), (5, 3))

    def places(self, first, count):
        size = self.pay.shape[0]
        at = pl.multiple_of((self.me // self.nz * self.nz + first) * size, size)
        return self.whole.at[pl.ds(at, count * size)]

    def near_copy(self, i):
        return remote(
            self.pay, self.places(i, 1), self.z_send.at[i], self.z_recv.at[i],
            self.along_z(self.order[i]), self.mine,
        )

    def group_copy(self, j, dx):
        part = self.places(*self.groups[j])
        slot = j * self.nx + dx
        return remote(
            part, part, self.x_send.at[slot], self.x_recv.at[slot], self.along_x(dx), self.mine
        )

    def start(self):
        size = self.pay.shape[0]
        at = pl.multiple_of(self.me // self.nz * self.nz * size, size)
        self.whole[pl.ds(at, size), :] = self.pay[...]
        for i in range(1, self.nz):
            self.near_copy(i).start()
        for dx in range(1, self.nx):
            self.group_copy(0, dx).start()

    def forward(self):
        for j, (first, count) in enumerate(self.groups[1:], 1):
            for i in range(first, first + count):
                self.near_copy(i).wait_recv()
            for dx in range(1, self.nx):
                self.group_copy(j, dx).start()

    def finish(self):
        for i in range(1, self.nz):
            self.near_copy(i).wait_send()
        for j in range(len(self.groups)):
            for dx in range(1, self.nx):
                self.group_copy(j, dx).wait()


def partner_features(x, y, z):
    row8 = lax.broadcasted_iota(jnp.int32, (8, PAIR_BLK), 0)
    row4 = row8 & 3
    n1, n2, n3 = pieces(x * x + y * y + z * z)
    xyz = jnp.where(row4 == 0, x, jnp.where(row4 == 1, y, z))
    upper = jnp.where(row4 == 3, jnp.where(row8 == 3, n1, n2), xyz)
    ones = jnp.where(row8 < 7, 1.0, 0.0)
    lower = jnp.where(row8 < 3, xyz, jnp.where(row8 == 3, n3, ones))
    return jnp.concatenate([upper, lower], axis=0)


def own_features(x, y, z):
    row8 = lax.broadcasted_iota(jnp.int32, (8, PAIR_BLK), 0)
    row4 = row8 & 3
    n1, n2, n3 = pieces(0.25 * (x * x + y * y + z * z + 1.0))
    xp, yp, zp = pieces(-0.5 * x), pieces(-0.5 * y), pieces(-0.5 * z)

    def xyz(i):
        return jnp.where(row4 == 0, xp[i], jnp.where(row4 == 1, yp[i], zp[i]))

    upper = jnp.where(row4 == 3, 0.25, jnp.where(row8 < 4, xyz(0), xyz(1)))
    norms = jnp.where(row8 == 4, n1, jnp.where(row8 == 5, n2, n3))
    norms = jnp.where(row8 == 7, 0.0, norms)
    lower = jnp.where(row8 < 3, xyz(2), jnp.where(row8 == 3, 0.25, norms))
    return jnp.concatenate([upper, lower], axis=0)


def pair_coef(squares):
    sp, st = squares[:, :PAIR_BLK], squares[:, PAIR_BLK:]
    rp = lax.rsqrt(sp)
    gap = sp * rp - st * lax.rsqrt(st)
    e2 = gap * gap + 0.0025
    re = lax.rsqrt(e2)
    err = e2 * re
    th = [jnp.tanh(0.5 * t - err) for t in (0.5, 1.0, 2.0, 4.0)]
    slope = 4.0 - (th[0] * th[0] + th[1] * th[1] + th[2] * th[2] + th[3] * th[3])
    return slope * gap * (re * rp)


def atoms_kernel(
    atom_peers, sample_peers, sigma, counts, feats, proj, own_single, token, true, noise,
    coord_in, wqkv, wo, wgu, wdown, gains, wout,
    pred, gathered_pred, gathered_true, owns, selves,
    hid, kv, queries, bias, pay, true_pay, wide, tok, near_single, cx, hots, partial, arrived, slab, *sems,
):
    rows = own_single.shape[0]
    ext = rows + 2 * HALO
    blocks = rows // PAIR_BLK
    nz, nx, me, along_z, along_x = gather_plan(atom_peers)
    mine = lax.axis_index("samples")
    barrier = pltpu.get_barrier_semaphore()
    right = lax.rem(me + 1, atom_peers)
    left = lax.rem(me + atom_peers - 1, atom_peers)
    share = feats.shape[1] // sample_peers
    (part_send, part_recv, tok_send, tok_recv, edge_send, edge_recv, near_send, near_recv) = sems[:8]

    def greet(atom, sample):
        pl.semaphore_signal(barrier, inc=1, device_id=(atom, sample), device_id_type=MESH)

    for step in range(1, sample_peers):
        greet(me, lax.rem(mine + step, sample_peers))
    greet(left, mine)
    greet(right, mine)
    for owner in (0, 1):
        greet(right, owner)
        greet(left, sample_peers - 1 - owner)
    for dz in range(1, nz):
        greet(along_z(dz), mine)
    for dx in range(1, nx):
        greet(along_x(dx), mine)
    first_atom = me * rows
    total_atoms = rows * atom_peers
    first_tok = me * (tok.shape[0] - 2 * TOK_HALO)
    sig = sigma[0]
    inv = lax.rsqrt(jnp.full((8, CHANNELS), sig * sig + 4.0, f32))[0:1, 0:1]
    zero5 = jnp.zeros((5, CHANNELS), f32)
    hi, mid, lo = pieces(jnp.concatenate([coord_in[...], zero5], axis=0))
    coord_w = jnp.concatenate([hi, mid, lo, hi, mid, hi], axis=0).astype(bf16)
    head = jnp.concatenate([wout[...], jnp.zeros((CHANNELS - 3, CHANNELS), f32)], axis=0).T
    hi, mid, lo = pieces(head)
    head = jnp.concatenate([hi, hi, mid], axis=0).astype(bf16)
    q_scale = math.log2(math.e) / math.sqrt(HEAD_DIM)
    lane = lax.broadcasted_iota(jnp.int32, (1, CHANNELS), 1) // HEAD_DIM

    pos = first_atom - HALO + lax.broadcasted_iota(jnp.int32, (ext, CHANNELS), 0)
    partial[...] = dot(feats[...], proj[...], ((0,), (0,)))
    cx[3:8, pl.ds(HALO, rows)] = jnp.concatenate(
        [token[...].astype(f32), jnp.zeros((4, rows), f32)], axis=0
    )
    for d in range(3):
        cx[d : d + 1, pl.ds(HALO, rows)] = (true[d : d + 1, :] + sig * noise[d]) * inv
    for d in range(3):
        for b in range(blocks):
            wide[d * blocks + b : d * blocks + b + 1, :] = true[
                d : d + 1, b * PAIR_BLK : (b + 1) * PAIR_BLK
            ]
    for b in range(blocks):
        wide[3 * blocks + b : 3 * blocks + b + 1, :] = jnp.full((1, PAIR_BLK), counts[b], jnp.int32).astype(f32)
    true_pay[...] = wide[...].astype(bf16)
    bias[...] = jnp.where((pos >= 0) & (pos < total_atoms), 0.0, -1e30)
    expected = sample_peers + 1 + nz + nx - 2
    on_edge = (mine < 2) | (mine >= sample_peers - 2)
    pl.semaphore_wait(barrier, expected + jnp.where(on_edge, sample_peers, 0))
    true_gather = Gather(atom_peers, true_pay, gathered_true, sems[8:12])
    pred_gather = Gather(atom_peers, pay, gathered_pred, sems[12:16])

    def part_copy(step):
        peer = lax.rem(mine + step, sample_peers)
        at = pl.multiple_of(peer * share, share)
        return remote(
            partial.at[pl.ds(at, share)], arrived.at[step], part_send.at[step], part_recv.at[step],
            me, peer,
        )

    parts = [part_copy(step) for step in range(1, sample_peers)]
    for copy in parts:
        copy.start()
    near = [
        remote(own_single.at[pl.ds(rows - HALO, HALO)], near_single.at[0],
               near_send.at[0], near_recv.at[0], right, mine),
        remote(own_single.at[pl.ds(0, HALO)], near_single.at[1],
               near_send.at[1], near_recv.at[1], left, mine),
        remote(cx.at[:, pl.ds(rows, HALO)], cx.at[:, pl.ds(0, HALO)],
               near_send.at[2], near_recv.at[2], right, mine),
        remote(cx.at[:, pl.ds(HALO, HALO)], cx.at[:, pl.ds(rows + HALO, HALO)],
               near_send.at[3], near_recv.at[3], left, mine),
    ]
    for copy in near:
        copy.start()

    def prepare(k, alone):
        at = pl.multiple_of(k * CHUNK, CHUNK)
        c = cx[:, pl.ds(at, CHUNK)]
        hi, mid, lo = pieces(c)
        coords = jnp.concatenate([hi, hi, hi, mid, mid, lo], axis=0).astype(bf16)
        hid[pl.ds(at, CHUNK), :] = alone.astype(f32) + dot(coords, coord_w, ((0,), (0,)))
        rel = c[3:4, :].astype(jnp.int32) - (first_tok - TOK_HALO + k * (CHUNK // 8))
        hot = jnp.where(lax.broadcasted_iota(jnp.int32, (CHANNELS, CHUNK), 0) == rel, 1.0, 0.0)
        hots[pl.ds(at, CHUNK), :] = hot.T.astype(bf16)

    def prepare_own(k, _):
        prepare(k, own_single[pl.ds(pl.multiple_of((k - 1) * CHUNK, CHUNK), CHUNK), :])
        return 0

    lax.fori_loop(1, 1 + rows // CHUNK, prepare_own, 0, unroll=4)
    for copy in parts:
        copy.wait_recv()
    total = partial[pl.ds(pl.multiple_of(mine * share, share), share), :]
    for step in range(1, sample_peers):
        total = total + arrived[step]
    slab[...] = total.astype(bf16)
    my_rows = pl.ds(pl.multiple_of(TOK_HALO + mine * share, 16), share)
    tok[my_rows, :] = slab[...]

    def tok_copy(step):
        return remote(
            slab, tok.at[my_rows], tok_send.at[step], tok_recv.at[step],
            me, lax.rem(mine + step, sample_peers),
        )

    toks = [tok_copy(step) for step in range(1, sample_peers)]
    for copy in toks:
        copy.start()
    tokens = tok.shape[0] - 2 * TOK_HALO
    rest = TOK_HALO - share
    edges = (
        (sample_peers - 1, pl.ds(0, share), pl.ds(rest, share), right),
        (sample_peers - 2, pl.ds(share - rest, rest), pl.ds(0, rest), right),
        (0, pl.ds(0, share), pl.ds(TOK_HALO + tokens, share), left),
        (1, pl.ds(0, rest), pl.ds(TOK_HALO + tokens + share, rest), left),
    )

    def edge_copy(i, step):
        _, src, dst, to = edges[i]
        return remote(
            slab.at[src], tok.at[dst], edge_send.at[step], edge_recv.at[i],
            to, lax.rem(mine + step, sample_peers),
        )

    for i, edge in enumerate(edges):
        @pl.when(mine == edge[0])
        def _(i=i):
            for step in range(sample_peers):
                edge_copy(i, step).start()

    true_gather.start_lines()
    for copy in near:
        copy.wait_recv()
    prepare(0, near_single[0])
    prepare(ext // CHUNK - 1, near_single[1])
    for copy in toks:
        copy.wait_recv()
    for i in range(len(edges)):
        edge_copy(i, 0).wait_recv()

    def project(layer, at, h):
        normed = (rms_scale(h) * gains[layer, 0:1, :]).astype(bf16)
        out = dot(normed, wqkv[layer])
        rows_at = pl.ds(at, h.shape[0])
        kv[layer % 2, rows_at, :] = out[:, 128:].astype(bf16)
        for t in range(h.shape[0] // CHANNELS):
            turned = (out[t * CHANNELS : (t + 1) * CHANNELS, :128] * q_scale).T
            shifted = [turned if r == 0 else pltpu.roll(turned, r * QBLK, 1) for r in range(HEADS)]
            for w in range(CHANNELS // QBLK):
                spread = jnp.concatenate(
                    [
                        jnp.where(lane == h, shifted[(h - w) % HEADS][h * QBLK : (h + 1) * QBLK], 0.0)
                        for h in range(HEADS)
                    ],
                    axis=0,
                )
                queries[layer % 2, at // QBLK + t * HEADS + w] = spread.astype(bf16)

    def first(k, _):
        at = pl.multiple_of(k * CHUNK, CHUNK)
        tok_at = pl.ds(pl.multiple_of(k * (CHUNK // 8), CHUNK // 8), TOK_WIN)
        h = hid[pl.ds(at, CHUNK), :] + dot(hots[pl.ds(at, CHUNK), 0:TOK_WIN], tok[tok_at, :])
        hid[pl.ds(at, CHUNK), :] = h
        project(0, at, h)
        return 0

    lax.fori_loop(0, ext // CHUNK, first, 0, unroll=FIRST_UNROLL)

    true_gather.forward_lines()

    def attend(layer, at, size):
        buf = layer % 2
        outs = []
        for w in range(size // QBLK):
            keys_at = pl.ds(at + (w * QBLK - 48), KWIN)
            keys = kv[buf, keys_at, 0:128]
            values = kv[buf, keys_at, 128:256]
            scores = dot(keys, queries[buf, at // QBLK + w]) + bias[keys_at, :]
            top = jnp.max(scores, axis=0, keepdims=True)
            weights = jnp.exp2(scores - top)
            weights = (weights * (1.0 / jnp.sum(weights, axis=0, keepdims=True))).astype(bf16)
            both = dot(weights, values, ((0,), (0,)))
            out = both[0:QBLK]
            for h in range(1, HEADS):
                out = jnp.where(lane == h, both[h * QBLK : (h + 1) * QBLK], out)
            outs.append(out.astype(bf16))
        return jnp.concatenate(outs, axis=0)

    def block(layer, at, size):
        h = hid[pl.ds(at, size), :]
        h = h + dot(attend(layer, at, size), wo[layer])
        normed = (rms_scale(h) * gains[layer, 1:2, :]).astype(bf16)
        gu = dot(normed, wgu[layer])
        gate = 0.5 * gu[:, :FF_ATOM]
        inner = (gate * (1.0 + jnp.tanh(gate)) * gu[:, FF_ATOM:]).astype(bf16)
        h = h + dot(inner, wdown[layer])
        if layer + 1 < LAYERS:
            hid[pl.ds(at, size), :] = h
            project(layer + 1, at, h)
        else:
            normed = rms_scale(h)
            hi = normed.astype(bf16)
            mid = (normed - hi.astype(f32)).astype(bf16)
            update = dot(jnp.concatenate([hi, mid, hi], axis=1), head)
            update = jnp.concatenate(
                [update[t * CHANNELS : (t + 1) * CHANNELS].T[0:8] for t in range(size // CHANNELS)],
                axis=1,
            )
            noisy = cx[:, pl.ds(at, size)]
            out = inv * (4.0 * noisy + (2.0 * sig) * update)
            pred[:, pl.ds(pl.multiple_of(at - HALO, 128), size)] = out
            first_block = (at - HALO) // PAIR_BLK
            for d in range(3):
                for i in range(size // PAIR_BLK):
                    wide[pl.ds(d * blocks + first_block + i, 1), :] = out[
                        d : d + 1, i * PAIR_BLK : (i + 1) * PAIR_BLK
                    ]

    for layer in range(LAYERS):
        low = HALO if layer == LAYERS - 1 else HALO - 128
        size = (rows if layer == LAYERS - 1 else rows + 256) // 2

        @pl.loop(0, 2)
        def _(k, layer=layer, low=low, size=size):
            block(layer, pl.multiple_of(low + k * size, 128), size)

    pay[...] = wide[0 : 3 * blocks, :].astype(bf16)
    pred_gather.start()

    diagonal = lax.broadcasted_iota(jnp.int32, (PAIR_BLK, PAIR_BLK), 0) == lax.broadcasted_iota(
        jnp.int32, (PAIR_BLK, PAIR_BLK), 1
    )
    none = jnp.zeros((16, PAIR_BLK), f32)

    def within(group):
        begun = []
        for b in group:
            at = slice(b * PAIR_BLK, (b + 1) * PAIR_BLK)
            ours = [pred[d : d + 1, at] for d in range(3)]
            known = [true[d : d + 1, at] for d in range(3)]
            own = jnp.concatenate(
                [
                    jnp.concatenate([own_features(*ours), none], axis=1),
                    jnp.concatenate([none, own_features(*known)], axis=1),
                ],
                axis=0,
            ).astype(bf16)
            owns[b] = own
            part = jnp.concatenate(
                [partner_features(*(v.astype(bf16).astype(f32) for v in vs)) for vs in (ours, known)],
                axis=0,
            ).astype(bf16)
            begun.append((part[0:16], dot(part, own, ((0,), (0,)))))
        coefs = [jnp.where(diagonal, 0.0, pair_coef(squares)).astype(bf16) for _, squares in begun]
        for b, (part, _), coef in zip(group, begun, coefs):
            selves[b] = dot(part, coef)[8:16]

    within(range(blocks // 2))
    pred_gather.forward()
    within(range(blocks // 2, blocks))
    for copy in parts + near + toks:
        copy.wait_send()
    for i, edge in enumerate(edges):
        @pl.when(mine == edge[0])
        def _(i=i):
            for step in range(sample_peers):
                edge_copy(i, step).wait_send()

    true_gather.finish_lines()
    pred_gather.finish()


def pairs_kernel(
    sigma, counts, partners, gathered_pred, gathered_true, owns, selves, pred, true,
    coord_grad, lddt_grad, wide_pred, wide_true, totals, held, parts,
):
    blocks = counts.shape[0]
    wide_pred[...] = gathered_pred[...].astype(f32)
    wide_true[...] = gathered_true[...].astype(f32)
    here = partners[0, 0] // blocks
    totals[0:blocks] = selves[...]
    totals[blocks] = jnp.zeros((8, PAIR_BLK), f32)

    def rows_of(wide, base):
        return partner_features(*(wide[pl.ds(base + d * blocks, 1), :] for d in range(3)))

    def begin(b, m):
        known = jnp.minimum(b, blocks - 1)
        p = partners[known, m]
        owner, place = p // blocks, p % blocks
        away = (here - owner) & (DEPTH - 1)
        slot = jnp.where(away <= DEPTH // 2, jnp.maximum(2 * away - 1, 0), 2 * (DEPTH - away))
        line = owner // DEPTH * DEPTH + slot
        part_pred = rows_of(wide_pred, line * (3 * blocks) + place)
        part_true = rows_of(wide_true, owner * (4 * blocks) + place)
        part = jnp.concatenate([part_pred, part_true], axis=0).astype(bf16)
        squares = dot(part, owns[known], ((0,), (0,)))
        count = counts[known]
        row = jnp.where(m < count, b, blocks)
        last = m + 1 >= count
        return part, squares, row, (jnp.where(last, jnp.minimum(b + 1, blocks), b), jnp.where(last, 1, m + 1))

    def start(slot, b, m):
        rows = []
        for i in range(UNROLL):
            part, squares, row, (b, m) = begin(b, m)
            parts[slot, i] = part[0:16]
            held[slot, i] = squares
            rows.append(row)
        return rows, (b, m)

    def end(slot, rows):
        coefs = [pair_coef(held[slot, i]).astype(bf16) for i in range(UNROLL)]
        found = [dot(parts[slot, i], coef)[8:16] for i, coef in enumerate(coefs)]
        for row, sums in zip(rows, found):
            totals[row] = totals[row] + sums

    def visit(_, carry):
        rows, place = carry
        more, place = start(1, *place)
        end(0, rows)
        rows, place = start(0, *place)
        end(1, more)
        return rows, place

    live = jnp.maximum(counts[0] - 1, 1)
    for b in range(1, blocks):
        live = live + jnp.maximum(counts[b] - 1, 1)
    groups = (live + UNROLL - 1) // UNROLL
    rows, _ = lax.fori_loop(0, groups // 2, visit, start(0, jnp.int32(0), jnp.int32(1)))

    @pl.when(groups % 2 == 1)
    def _():
        end(0, rows)

    square = sigma[0] * sigma[0]
    mse_scale = jnp.full((1, PAIR_BLK), square + 4.0, f32) / jnp.full((1, PAIR_BLK), 6.0 * square, f32)
    peers = gathered_true.shape[0] // (4 * blocks)
    listed = jnp.zeros((blocks, PAIR_BLK), f32)
    for peer in range(peers):
        listed = listed + wide_true[peer * 4 * blocks + 3 * blocks : (peer + 1) * 4 * blocks, :]
    listed = jnp.sum(listed, axis=0, keepdims=True)
    total_pairs = listed * (PAIR_BLK * PAIR_BLK) - float(PAIR_BLK * blocks * peers)
    pair_scale = -0.0625 * (blocks * peers * PAIR_BLK * PAIR_BLK) / total_pairs
    for b in range(blocks):
        at = slice(b * PAIR_BLK, (b + 1) * PAIR_BLK)
        total = totals[b]
        for d in range(3):
            pc, tc = pred[d : d + 1, at], true[d : d + 1, at]
            lg = pair_scale * (pc * total[4:5] - total[d : d + 1])
            lddt_grad[d, :, at] = lg
            coord_grad[d, :, at] = mse_scale * (pc - tc) - lg * (1.0 / PAIR_BLK)


def vmem(n):
    return [pl.BlockSpec(memory_space=pltpu.VMEM)] * n


def smem(n):
    return [pl.BlockSpec(memory_space=pltpu.SMEM)] * n


def run_atoms(
    sigma, counts, feats, proj, single, token, true, noise,
    coord_in, w_qkv, w_o, w_gu, w_down, gains, w_out,
):
    rows, tokens = single.shape[0], feats.shape[1]
    ext = rows + 2 * HALO
    blocks = rows // PAIR_BLK
    atom_peers, sample_peers = lax.axis_size("atoms"), lax.axis_size("samples")
    part = tokens // sample_peers
    dma = pltpu.SemaphoreType.DMA
    one_gather = [dma((DEPTH,)), dma((DEPTH,)), dma((atom_peers,)), dma((atom_peers,))]
    return pl.pallas_call(
        functools.partial(atoms_kernel, atom_peers, sample_peers),
        name="atoms",
        out_shape=(
            jax.ShapeDtypeStruct((8, rows), f32),
            jax.ShapeDtypeStruct((atom_peers * 3 * blocks, PAIR_BLK), bf16),
            jax.ShapeDtypeStruct((atom_peers * 4 * blocks, PAIR_BLK), bf16),
            jax.ShapeDtypeStruct((blocks, 32, 2 * PAIR_BLK), bf16),
            jax.ShapeDtypeStruct((blocks, 8, PAIR_BLK), f32),
        ),
        in_specs=smem(2) + vmem(13),
        out_specs=tuple(vmem(5)),
        scratch_shapes=[
            pltpu.VMEM((ext, CHANNELS), f32),
            pltpu.VMEM((2, ext, 2 * CHANNELS), bf16),
            pltpu.VMEM((2, ext // QBLK, CHANNELS, CHANNELS), bf16),
            pltpu.VMEM((ext, CHANNELS), f32),
            pltpu.VMEM((3 * blocks, PAIR_BLK), bf16),
            pltpu.VMEM((4 * blocks, PAIR_BLK), bf16),
            pltpu.VMEM((4 * blocks, PAIR_BLK), f32),
            pltpu.VMEM((tokens + 2 * TOK_HALO, CHANNELS), bf16),
            pltpu.VMEM((2, HALO, CHANNELS), bf16),
            pltpu.VMEM((8, ext), f32),
            pltpu.VMEM((ext, CHANNELS), bf16),
            pltpu.VMEM((tokens, CHANNELS), f32),
            pltpu.VMEM((sample_peers, part, CHANNELS), f32),
            pltpu.VMEM((part, CHANNELS), bf16),
            dma((sample_peers,)), dma((sample_peers,)), dma((sample_peers,)), dma((sample_peers,)),
            dma((sample_peers,)), dma((4,)), dma((4,)), dma((4,)),
        ]
        + 2 * one_gather,
        compiler_params=pltpu.CompilerParams(
            collective_id=0, has_side_effects=True, vmem_limit_bytes=VMEM_LIMIT
        ),
    )(
        sigma, counts, feats, proj, single, token, true, noise,
        coord_in, w_qkv, w_o, w_gu, w_down, gains, w_out.T,
    )


def run_pairs(sigma, counts, partners, gathered_pred, gathered_true, owns, selves, pred, true):
    rows = pred.shape[1]
    out = jax.ShapeDtypeStruct((3, 1, rows), f32)
    coord_grad, lddt_grad = pl.pallas_call(
        pairs_kernel,
        name="pairs",
        out_shape=(out, out),
        in_specs=smem(3) + vmem(6),
        out_specs=tuple(vmem(2)),
        scratch_shapes=[pltpu.VMEM(g.shape, f32) for g in (gathered_pred, gathered_true)]
        + [
            pltpu.VMEM((rows // PAIR_BLK + 1, 8, PAIR_BLK), f32),
            pltpu.VMEM((2, UNROLL, PAIR_BLK, 2 * PAIR_BLK), f32),
            pltpu.VMEM((2, UNROLL, 16, PAIR_BLK), bf16),
        ],
        compiler_params=pltpu.CompilerParams(vmem_limit_bytes=VMEM_LIMIT),
    )(sigma, counts, partners, gathered_pred, gathered_true, owns, selves, pred, true)
    return jnp.swapaxes(coord_grad, 0, 1), jnp.swapaxes(lddt_grad, 0, 1)


def on_device(
    token_feats, proj_w, atom_single, atom_token, true_coords, noise, sigma, coord_in,
    w_qkv, w_o, w_gu, w_down, gains, w_out, pair_blocks, pair_count,
):
    pred, gathered_pred, gathered_true, owns, selves = run_atoms(
        sigma, pair_count, token_feats.T, proj_w, atom_single, atom_token[None], true_coords,
        jnp.swapaxes(noise, 0, 1), coord_in, w_qkv, w_o, w_gu, w_down, gains, w_out,
    )
    return run_pairs(
        sigma, pair_count, pair_blocks, gathered_pred, gathered_true, owns, selves, pred, true_coords
    )


def solution(mesh):
    in_specs = (
        P("atoms", "samples"),
        P("samples", None),
        P("atoms", None),
        P("atoms"),
        P(None, "atoms"),
        P("samples", None, "atoms"),
        P("samples"),
        P(), P(), P(), P(), P(), P(), P(),
        P("atoms", None),
        P("atoms"),
    )
    out_specs = (P("samples", None, "atoms"), P("samples", None, "atoms"))
    return jax.shard_map(on_device, mesh=mesh, in_specs=in_specs, out_specs=out_specs, check_vma=False)
```

```python
import functools
import math

import jax
import jax.numpy as jnp
from jax import lax
from jax.experimental import pallas as pl
from jax.experimental.pallas import tpu as pltpu
from jax.sharding import PartitionSpec as P

HEADS = 4
HEAD_DIM = 32
FF_ATOM = 256
LAYERS = 3
QBLK = 32
KWIN = 128
PAIR_BLK = 128
CHANNELS = 128
CHUNK = 256
FIRST_UNROLL = 10
UNROLL = 8
HALO = 256
TOK_HALO = 48
TOK_WIN = 64
EPS = 1e-05
DEPTH = 8
VMEM_LIMIT = 56 * 1024 * 1024

f32 = jnp.float32
bf16 = jnp.bfloat16


def dot(a, b, dims=((1,), (0,)), precision=None):
    return lax.dot_general(a, b, (dims, ((), ())), precision=precision, preferred_element_type=f32)


def pieces(v):
    hi = v.astype(bf16).astype(f32)
    mid = (v - hi).astype(bf16).astype(f32)
    lo = (v - hi - mid).astype(bf16).astype(f32)
    return hi, mid, lo


def rms_scale(h):
    return h * lax.rsqrt(jnp.mean(h * h, axis=1, keepdims=True) + EPS)


MESH = pl.DeviceIdType.MESH


def remote(src, dst, send, recv, atom, sample):
    return pltpu.make_async_remote_copy(
        src_ref=src, dst_ref=dst, send_sem=send, recv_sem=recv,
        device_id=(atom, sample), device_id_type=MESH,
    )

def gather_plan(atom_peers):
    nz = DEPTH
    nx = atom_peers // nz
    me = lax.axis_index("atoms")
    x, z = me // nz, lax.rem(me, nz)

    def along_z(dz):
        return x * nz + lax.rem(z + dz + nz, nz)

    def along_x(dx):
        return lax.rem(x + dx, nx) * nz + z

    return nz, nx, me, along_z, along_x


class Gather:
    def __init__(self, atom_peers, pay, whole, sems):
        self.nz, self.nx, self.me, self.along_z, self.along_x = gather_plan(atom_peers)
        self.mine = lax.axis_index("samples")
        self.pay, self.whole = pay, whole
        self.z_send, self.z_recv, self.x_send, self.x_recv = sems
        self.order = [0]
        for step in range(1, self.nz // 2 + 1):
            self.order += [step, self.nz - step] if 2 * step != self.nz else [step]

    def rows(self, owner):
        size = self.pay.shape[0]
        return pl.ds(pl.multiple_of(owner * size, size), size)

    def z_copy(self, dz):
        return remote(
            self.pay, self.whole.at[self.rows(self.me)], self.z_send.at[dz], self.z_recv.at[dz],
            self.along_z(dz), self.mine,
        )

    def line_copy(self, dx):
        size = self.pay.shape[0] * self.nz
        at = pl.ds(pl.multiple_of(self.me // self.nz * size, size), size)
        line = self.whole.at[at]
        return remote(line, line, self.x_send.at[dx], self.x_recv.at[dx], self.along_x(dx), self.mine)

    def start_lines(self):
        self.whole[self.rows(self.me), :] = self.pay[...]
        for dz in self.order[1:]:
            self.z_copy(dz).start()

    def forward_lines(self):
        for dz in self.order[1:]:
            self.z_copy(dz).wait_recv()
        for dx in range(1, self.nx):
            self.line_copy(dx).start()

    def finish_lines(self):
        for dz in self.order[1:]:
            self.z_copy(dz).wait_send()
        for dx in range(1, self.nx):
            self.line_copy(dx).wait()

    groups = ((0, 1), (1, 2), (3, 2), (5, 3))

    def places(self, first, count):
        size = self.pay.shape[0]
        at = pl.multiple_of((self.me // self.nz * self.nz + first) * size, size)
        return self.whole.at[pl.ds(at, count * size)]

    def near_copy(self, i):
        return remote(
            self.pay, self.places(i, 1), self.z_send.at[i], self.z_recv.at[i],
            self.along_z(self.order[i]), self.mine,
        )

    def group_copy(self, j, dx):
        part = self.places(*self.groups[j])
        slot = j * self.nx + dx
        return remote(
            part, part, self.x_send.at[slot], self.x_recv.at[slot], self.along_x(dx), self.mine
        )

    def start(self):
        size = self.pay.shape[0]
        at = pl.multiple_of(self.me // self.nz * self.nz * size, size)
        self.whole[pl.ds(at, size), :] = self.pay[...]
        for i in range(1, self.nz):
            self.near_copy(i).start()
        for dx in range(1, self.nx):
            self.group_copy(0, dx).start()

    def forward(self):
        for j, (first, count) in enumerate(self.groups[1:], 1):
            for i in range(first, first + count):
                self.near_copy(i).wait_recv()
            for dx in range(1, self.nx):
                self.group_copy(j, dx).start()

    def finish(self):
        for i in range(1, self.nz):
            self.near_copy(i).wait_send()
        for j in range(len(self.groups)):
            for dx in range(1, self.nx):
                self.group_copy(j, dx).wait()


def partner_features(x, y, z):
    row8 = lax.broadcasted_iota(jnp.int32, (8, PAIR_BLK), 0)
    row4 = row8 & 3
    n1, n2, n3 = pieces(x * x + y * y + z * z)
    xyz = jnp.where(row4 == 0, x, jnp.where(row4 == 1, y, z))
    upper = jnp.where(row4 == 3, jnp.where(row8 == 3, n1, n2), xyz)
    ones = jnp.where(row8 < 7, 1.0, 0.0)
    lower = jnp.where(row8 < 3, xyz, jnp.where(row8 == 3, n3, ones))
    return jnp.concatenate([upper, lower], axis=0)


def own_features(x, y, z):
    row8 = lax.broadcasted_iota(jnp.int32, (8, PAIR_BLK), 0)
    row4 = row8 & 3
    n1, n2, n3 = pieces(0.25 * (x * x + y * y + z * z + 1.0))
    xp, yp, zp = pieces(-0.5 * x), pieces(-0.5 * y), pieces(-0.5 * z)

    def xyz(i):
        return jnp.where(row4 == 0, xp[i], jnp.where(row4 == 1, yp[i], zp[i]))

    upper = jnp.where(row4 == 3, 0.25, jnp.where(row8 < 4, xyz(0), xyz(1)))
    norms = jnp.where(row8 == 4, n1, jnp.where(row8 == 5, n2, n3))
    norms = jnp.where(row8 == 7, 0.0, norms)
    lower = jnp.where(row8 < 3, xyz(2), jnp.where(row8 == 3, 0.25, norms))
    return jnp.concatenate([upper, lower], axis=0)


def pair_coef(squares):
    sp, st = squares[:, :PAIR_BLK], squares[:, PAIR_BLK:]
    rp = lax.rsqrt(sp)
    gap = sp * rp - st * lax.rsqrt(st)
    e2 = gap * gap + 0.0025
    re = lax.rsqrt(e2)
    err = e2 * re
    th = [jnp.tanh(0.5 * t - err) for t in (0.5, 1.0, 2.0, 4.0)]
    slope = 4.0 - (th[0] * th[0] + th[1] * th[1] + th[2] * th[2] + th[3] * th[3])
    return slope * gap * (re * rp)


def atoms_kernel(
    atom_peers, sample_peers, sigma, counts, feats, proj, own_single, token, true, noise,
    coord_in, wqkv, wo, wgu, wdown, gains, wout,
    pred, gathered_pred, gathered_true, owns, selves,
    hid, kv, queries, bias, pay, true_pay, wide, tok, near_single, cx, hots, partial, arrived, slab, *sems,
):
    rows = own_single.shape[0]
    ext = rows + 2 * HALO
    blocks = rows // PAIR_BLK
    nz, nx, me, along_z, along_x = gather_plan(atom_peers)
    mine = lax.axis_index("samples")
    barrier = pltpu.get_barrier_semaphore()
    right = lax.rem(me + 1, atom_peers)
    left = lax.rem(me + atom_peers - 1, atom_peers)
    share = feats.shape[1] // sample_peers
    (part_send, part_recv, tok_send, tok_recv, edge_send, edge_recv, near_send, near_recv) = sems[:8]

    def greet(atom, sample):
        pl.semaphore_signal(barrier, inc=1, device_id=(atom, sample), device_id_type=MESH)

    for step in range(1, sample_peers):
        greet(me, lax.rem(mine + step, sample_peers))
    greet(left, mine)
    greet(right, mine)
    for owner in (0, 1):
        greet(right, owner)
        greet(left, sample_peers - 1 - owner)
    for dz in range(1, nz):
        greet(along_z(dz), mine)
    for dx in range(1, nx):
        greet(along_x(dx), mine)
    first_atom = me * rows
    total_atoms = rows * atom_peers
    first_tok = me * (tok.shape[0] - 2 * TOK_HALO)
    sig = sigma[0]
    inv = lax.rsqrt(jnp.full((8, CHANNELS), sig * sig + 4.0, f32))[0:1, 0:1]
    zero5 = jnp.zeros((5, CHANNELS), f32)
    hi, mid, lo = pieces(jnp.concatenate([coord_in[...], zero5], axis=0))
    coord_w = jnp.concatenate([hi, mid, lo, hi, mid, hi], axis=0).astype(bf16)
    head = jnp.concatenate([wout[...], jnp.zeros((CHANNELS - 3, CHANNELS), f32)], axis=0).T
    hi, mid, lo = pieces(head)
    head = jnp.concatenate([hi, hi, mid], axis=0).astype(bf16)
    q_scale = math.log2(math.e) / math.sqrt(HEAD_DIM)
    lane = lax.broadcasted_iota(jnp.int32, (1, CHANNELS), 1) // HEAD_DIM

    pos = first_atom - HALO + lax.broadcasted_iota(jnp.int32, (ext, CHANNELS), 0)
    partial[...] = dot(feats[...], proj[...], ((0,), (0,)))
    cx[3:8, pl.ds(HALO, rows)] = jnp.concatenate(
        [token[...].astype(f32), jnp.zeros((4, rows), f32)], axis=0
    )
    for d in range(3):
        cx[d : d + 1, pl.ds(HALO, rows)] = (true[d : d + 1, :] + sig * noise[d]) * inv
    for d in range(3):
        for b in range(blocks):
            wide[d * blocks + b : d * blocks + b + 1, :] = true[
                d : d + 1, b * PAIR_BLK : (b + 1) * PAIR_BLK
            ]
    for b in range(blocks):
        wide[3 * blocks + b : 3 * blocks + b + 1, :] = jnp.full((1, PAIR_BLK), counts[b], jnp.int32).astype(f32)
    true_pay[...] = wide[...].astype(bf16)
    bias[...] = jnp.where((pos >= 0) & (pos < total_atoms), 0.0, -1e30)
    expected = sample_peers + 1 + nz + nx - 2
    on_edge = (mine < 2) | (mine >= sample_peers - 2)
    pl.semaphore_wait(barrier, expected + jnp.where(on_edge, sample_peers, 0))
    true_gather = Gather(atom_peers, true_pay, gathered_true, sems[8:12])
    pred_gather = Gather(atom_peers, pay, gathered_pred, sems[12:16])

    def part_copy(step):
        peer = lax.rem(mine + step, sample_peers)
        at = pl.multiple_of(peer * share, share)
        return remote(
            partial.at[pl.ds(at, share)], arrived.at[step], part_send.at[step], part_recv.at[step],
            me, peer,
        )

    parts = [part_copy(step) for step in range(1, sample_peers)]
    for copy in parts:
        copy.start()
    near = [
        remote(own_single.at[pl.ds(rows - HALO, HALO)], near_single.at[0],
               near_send.at[0], near_recv.at[0], right, mine),
        remote(own_single.at[pl.ds(0, HALO)], near_single.at[1],
               near_send.at[1], near_recv.at[1], left, mine),
        remote(cx.at[:, pl.ds(rows, HALO)], cx.at[:, pl.ds(0, HALO)],
               near_send.at[2], near_recv.at[2], right, mine),
        remote(cx.at[:, pl.ds(HALO, HALO)], cx.at[:, pl.ds(rows + HALO, HALO)],
               near_send.at[3], near_recv.at[3], left, mine),
    ]
    for copy in near:
        copy.start()

    def prepare(k, alone):
        at = pl.multiple_of(k * CHUNK, CHUNK)
        c = cx[:, pl.ds(at, CHUNK)]
        hi, mid, lo = pieces(c)
        coords = jnp.concatenate([hi, hi, hi, mid, mid, lo], axis=0).astype(bf16)
        hid[pl.ds(at, CHUNK), :] = alone.astype(f32) + dot(coords, coord_w, ((0,), (0,)))
        rel = c[3:4, :].astype(jnp.int32) - (first_tok - TOK_HALO + k * (CHUNK // 8))
        hot = jnp.where(lax.broadcasted_iota(jnp.int32, (CHANNELS, CHUNK), 0) == rel, 1.0, 0.0)
        hots[pl.ds(at, CHUNK), :] = hot.T.astype(bf16)

    def prepare_own(k, _):
        prepare(k, own_single[pl.ds(pl.multiple_of((k - 1) * CHUNK, CHUNK), CHUNK), :])
        return 0

    lax.fori_loop(1, 1 + rows // CHUNK, prepare_own, 0, unroll=4)
    for copy in parts:
        copy.wait_recv()
    total = partial[pl.ds(pl.multiple_of(mine * share, share), share), :]
    for step in range(1, sample_peers):
        total = total + arrived[step]
    slab[...] = total.astype(bf16)
    my_rows = pl.ds(pl.multiple_of(TOK_HALO + mine * share, 16), share)
    tok[my_rows, :] = slab[...]

    def tok_copy(step):
        return remote(
            slab, tok.at[my_rows], tok_send.at[step], tok_recv.at[step],
            me, lax.rem(mine + step, sample_peers),
        )

    toks = [tok_copy(step) for step in range(1, sample_peers)]
    for copy in toks:
        copy.start()
    tokens = tok.shape[0] - 2 * TOK_HALO
    rest = TOK_HALO - share
    edges = (
        (sample_peers - 1, pl.ds(0, share), pl.ds(rest, share), right),
        (sample_peers - 2, pl.ds(share - rest, rest), pl.ds(0, rest), right),
        (0, pl.ds(0, share), pl.ds(TOK_HALO + tokens, share), left),
        (1, pl.ds(0, rest), pl.ds(TOK_HALO + tokens + share, rest), left),
    )

    def edge_copy(i, step):
        _, src, dst, to = edges[i]
        return remote(
            slab.at[src], tok.at[dst], edge_send.at[step], edge_recv.at[i],
            to, lax.rem(mine + step, sample_peers),
        )

    for i, edge in enumerate(edges):
        @pl.when(mine == edge[0])
        def _(i=i):
            for step in range(sample_peers):
                edge_copy(i, step).start()

    true_gather.start_lines()
    for copy in near:
        copy.wait_recv()
    prepare(0, near_single[0])
    prepare(ext // CHUNK - 1, near_single[1])
    for copy in toks:
        copy.wait_recv()
    for i in range(len(edges)):
        edge_copy(i, 0).wait_recv()

    def project(layer, at, h):
        normed = (rms_scale(h) * gains[layer, 0:1, :]).astype(bf16)
        out = dot(normed, wqkv[layer])
        rows_at = pl.ds(at, h.shape[0])
        kv[layer % 2, rows_at, :] = out[:, 128:].astype(bf16)
        for t in range(h.shape[0] // CHANNELS):
            turned = (out[t * CHANNELS : (t + 1) * CHANNELS, :128] * q_scale).T
            shifted = [turned if r == 0 else pltpu.roll(turned, r * QBLK, 1) for r in range(HEADS)]
            for w in range(CHANNELS // QBLK):
                spread = jnp.concatenate(
                    [
                        jnp.where(lane == h, shifted[(h - w) % HEADS][h * QBLK : (h + 1) * QBLK], 0.0)
                        for h in range(HEADS)
                    ],
                    axis=0,
                )
                queries[layer % 2, at // QBLK + t * HEADS + w] = spread.astype(bf16)

    def first(k, _):
        at = pl.multiple_of(k * CHUNK, CHUNK)
        tok_at = pl.ds(pl.multiple_of(k * (CHUNK // 8), CHUNK // 8), TOK_WIN)
        h = hid[pl.ds(at, CHUNK), :] + dot(hots[pl.ds(at, CHUNK), 0:TOK_WIN], tok[tok_at, :])
        hid[pl.ds(at, CHUNK), :] = h
        project(0, at, h)
        return 0

    lax.fori_loop(0, ext // CHUNK, first, 0, unroll=FIRST_UNROLL)

    true_gather.forward_lines()

    def attend(layer, at, size):
        buf = layer % 2
        outs = []
        for w in range(size // QBLK):
            keys_at = pl.ds(at + (w * QBLK - 48), KWIN)
            keys = kv[buf, keys_at, 0:128]
            values = kv[buf, keys_at, 128:256]
            scores = dot(keys, queries[buf, at // QBLK + w]) + bias[keys_at, :]
            top = jnp.max(scores, axis=0, keepdims=True)
            weights = jnp.exp2(scores - top)
            weights = (weights * (1.0 / jnp.sum(weights, axis=0, keepdims=True))).astype(bf16)
            both = dot(weights, values, ((0,), (0,)))
            out = both[0:QBLK]
            for h in range(1, HEADS):
                out = jnp.where(lane == h, both[h * QBLK : (h + 1) * QBLK], out)
            outs.append(out.astype(bf16))
        return jnp.concatenate(outs, axis=0)

    def block(layer, at, size):
        h = hid[pl.ds(at, size), :]
        h = h + dot(attend(layer, at, size), wo[layer])
        normed = (rms_scale(h) * gains[layer, 1:2, :]).astype(bf16)
        gu = dot(normed, wgu[layer])
        gate = 0.5 * gu[:, :FF_ATOM]
        inner = (gate * (1.0 + jnp.tanh(gate)) * gu[:, FF_ATOM:]).astype(bf16)
        h = h + dot(inner, wdown[layer])
        if layer + 1 < LAYERS:
            hid[pl.ds(at, size), :] = h
            project(layer + 1, at, h)
        else:
            normed = rms_scale(h)
            hi = normed.astype(bf16)
            mid = (normed - hi.astype(f32)).astype(bf16)
            update = dot(jnp.concatenate([hi, mid, hi], axis=1), head)
            update = jnp.concatenate(
                [update[t * CHANNELS : (t + 1) * CHANNELS].T[0:8] for t in range(size // CHANNELS)],
                axis=1,
            )
            noisy = cx[:, pl.ds(at, size)]
            out = inv * (4.0 * noisy + (2.0 * sig) * update)
            pred[:, pl.ds(pl.multiple_of(at - HALO, 128), size)] = out
            first_block = (at - HALO) // PAIR_BLK
            for d in range(3):
                for i in range(size // PAIR_BLK):
                    wide[pl.ds(d * blocks + first_block + i, 1), :] = out[
                        d : d + 1, i * PAIR_BLK : (i + 1) * PAIR_BLK
                    ]

    for layer in range(LAYERS):
        low = HALO if layer == LAYERS - 1 else HALO - 128
        block(layer, low, rows if layer == LAYERS - 1 else rows + 256)

    pay[...] = wide[0 : 3 * blocks, :].astype(bf16)
    pred_gather.start()

    diagonal = lax.broadcasted_iota(jnp.int32, (PAIR_BLK, PAIR_BLK), 0) == lax.broadcasted_iota(
        jnp.int32, (PAIR_BLK, PAIR_BLK), 1
    )
    none = jnp.zeros((16, PAIR_BLK), f32)

    def within(group):
        begun = []
        for b in group:
            at = slice(b * PAIR_BLK, (b + 1) * PAIR_BLK)
            ours = [pred[d : d + 1, at] for d in range(3)]
            known = [true[d : d + 1, at] for d in range(3)]
            own = jnp.concatenate(
                [
                    jnp.concatenate([own_features(*ours), none], axis=1),
                    jnp.concatenate([none, own_features(*known)], axis=1),
                ],
                axis=0,
            ).astype(bf16)
            owns[b] = own
            part = jnp.concatenate(
                [partner_features(*(v.astype(bf16).astype(f32) for v in vs)) for vs in (ours, known)],
                axis=0,
            ).astype(bf16)
            begun.append((part[0:16], dot(part, own, ((0,), (0,)))))
        coefs = [jnp.where(diagonal, 0.0, pair_coef(squares)).astype(bf16) for _, squares in begun]
        for b, (part, _), coef in zip(group, begun, coefs):
            selves[b] = dot(part, coef)[8:16]

    within(range(blocks // 2))
    pred_gather.forward()
    within(range(blocks // 2, blocks))
    for copy in parts + near + toks:
        copy.wait_send()
    for i, edge in enumerate(edges):
        @pl.when(mine == edge[0])
        def _(i=i):
            for step in range(sample_peers):
                edge_copy(i, step).wait_send()

    true_gather.finish_lines()
    pred_gather.finish()


def pairs_kernel(
    sigma, counts, partners, gathered_pred, gathered_true, owns, selves, pred, true,
    coord_grad, lddt_grad, wide_pred, wide_true, totals, held, parts,
):
    blocks = counts.shape[0]
    wide_pred[...] = gathered_pred[...].astype(f32)
    wide_true[...] = gathered_true[...].astype(f32)
    here = partners[0, 0] // blocks
    totals[0:blocks] = selves[...]
    totals[blocks] = jnp.zeros((8, PAIR_BLK), f32)

    def rows_of(wide, base):
        return partner_features(*(wide[pl.ds(base + d * blocks, 1), :] for d in range(3)))

    def begin(b, m):
        known = jnp.minimum(b, blocks - 1)
        p = partners[known, m]
        owner, place = p // blocks, p % blocks
        away = (here - owner) & (DEPTH - 1)
        slot = jnp.where(away <= DEPTH // 2, jnp.maximum(2 * away - 1, 0), 2 * (DEPTH - away))
        line = owner // DEPTH * DEPTH + slot
        part_pred = rows_of(wide_pred, line * (3 * blocks) + place)
        part_true = rows_of(wide_true, owner * (4 * blocks) + place)
        part = jnp.concatenate([part_pred, part_true], axis=0).astype(bf16)
        squares = dot(part, owns[known], ((0,), (0,)))
        count = counts[known]
        row = jnp.where(m < count, b, blocks)
        last = m + 1 >= count
        return part, squares, row, (jnp.where(last, jnp.minimum(b + 1, blocks), b), jnp.where(last, 1, m + 1))

    def start(slot, b, m):
        rows = []
        for i in range(UNROLL):
            part, squares, row, (b, m) = begin(b, m)
            parts[slot, i] = part[0:16]
            held[slot, i] = squares
            rows.append(row)
        return rows, (b, m)

    def end(slot, rows):
        coefs = [pair_coef(held[slot, i]).astype(bf16) for i in range(UNROLL)]
        found = [dot(parts[slot, i], coef)[8:16] for i, coef in enumerate(coefs)]
        for row, sums in zip(rows, found):
            totals[row] = totals[row] + sums

    def visit(_, carry):
        rows, place = carry
        more, place = start(1, *place)
        end(0, rows)
        rows, place = start(0, *place)
        end(1, more)
        return rows, place

    live = jnp.maximum(counts[0] - 1, 1)
    for b in range(1, blocks):
        live = live + jnp.maximum(counts[b] - 1, 1)
    groups = (live + UNROLL - 1) // UNROLL
    rows, _ = lax.fori_loop(0, groups // 2, visit, start(0, jnp.int32(0), jnp.int32(1)))

    @pl.when(groups % 2 == 1)
    def _():
        end(0, rows)

    square = sigma[0] * sigma[0]
    mse_scale = jnp.full((1, PAIR_BLK), square + 4.0, f32) / jnp.full((1, PAIR_BLK), 6.0 * square, f32)
    peers = gathered_true.shape[0] // (4 * blocks)
    listed = jnp.zeros((blocks, PAIR_BLK), f32)
    for peer in range(peers):
        listed = listed + wide_true[peer * 4 * blocks + 3 * blocks : (peer + 1) * 4 * blocks, :]
    listed = jnp.sum(listed, axis=0, keepdims=True)
    total_pairs = listed * (PAIR_BLK * PAIR_BLK) - float(PAIR_BLK * blocks * peers)
    pair_scale = -0.0625 * (blocks * peers * PAIR_BLK * PAIR_BLK) / total_pairs
    for b in range(blocks):
        at = slice(b * PAIR_BLK, (b + 1) * PAIR_BLK)
        total = totals[b]
        for d in range(3):
            pc, tc = pred[d : d + 1, at], true[d : d + 1, at]
            lg = pair_scale * (pc * total[4:5] - total[d : d + 1])
            lddt_grad[d, :, at] = lg
            coord_grad[d, :, at] = mse_scale * (pc - tc) - lg * (1.0 / PAIR_BLK)


def vmem(n):
    return [pl.BlockSpec(memory_space=pltpu.VMEM)] * n


def smem(n):
    return [pl.BlockSpec(memory_space=pltpu.SMEM)] * n


def run_atoms(
    sigma, counts, feats, proj, single, token, true, noise,
    coord_in, w_qkv, w_o, w_gu, w_down, gains, w_out,
):
    rows, tokens = single.shape[0], feats.shape[1]
    ext = rows + 2 * HALO
    blocks = rows // PAIR_BLK
    atom_peers, sample_peers = lax.axis_size("atoms"), lax.axis_size("samples")
    part = tokens // sample_peers
    dma = pltpu.SemaphoreType.DMA
    one_gather = [dma((DEPTH,)), dma((DEPTH,)), dma((atom_peers,)), dma((atom_peers,))]
    return pl.pallas_call(
        functools.partial(atoms_kernel, atom_peers, sample_peers),
        name="atoms",
        out_shape=(
            jax.ShapeDtypeStruct((8, rows), f32),
            jax.ShapeDtypeStruct((atom_peers * 3 * blocks, PAIR_BLK), bf16),
            jax.ShapeDtypeStruct((atom_peers * 4 * blocks, PAIR_BLK), bf16),
            jax.ShapeDtypeStruct((blocks, 32, 2 * PAIR_BLK), bf16),
            jax.ShapeDtypeStruct((blocks, 8, PAIR_BLK), f32),
        ),
        in_specs=smem(2) + vmem(13),
        out_specs=tuple(vmem(5)),
        scratch_shapes=[
            pltpu.VMEM((ext, CHANNELS), f32),
            pltpu.VMEM((2, ext, 2 * CHANNELS), bf16),
            pltpu.VMEM((2, ext // QBLK, CHANNELS, CHANNELS), bf16),
            pltpu.VMEM((ext, CHANNELS), f32),
            pltpu.VMEM((3 * blocks, PAIR_BLK), bf16),
            pltpu.VMEM((4 * blocks, PAIR_BLK), bf16),
            pltpu.VMEM((4 * blocks, PAIR_BLK), f32),
            pltpu.VMEM((tokens + 2 * TOK_HALO, CHANNELS), bf16),
            pltpu.VMEM((2, HALO, CHANNELS), bf16),
            pltpu.VMEM((8, ext), f32),
            pltpu.VMEM((ext, CHANNELS), bf16),
            pltpu.VMEM((tokens, CHANNELS), f32),
            pltpu.VMEM((sample_peers, part, CHANNELS), f32),
            pltpu.VMEM((part, CHANNELS), bf16),
            dma((sample_peers,)), dma((sample_peers,)), dma((sample_peers,)), dma((sample_peers,)),
            dma((sample_peers,)), dma((4,)), dma((4,)), dma((4,)),
        ]
        + 2 * one_gather,
        compiler_params=pltpu.CompilerParams(
            collective_id=0, has_side_effects=True, vmem_limit_bytes=VMEM_LIMIT
        ),
    )(
        sigma, counts, feats, proj, single, token, true, noise,
        coord_in, w_qkv, w_o, w_gu, w_down, gains, w_out.T,
    )


def run_pairs(sigma, counts, partners, gathered_pred, gathered_true, owns, selves, pred, true):
    rows = pred.shape[1]
    out = jax.ShapeDtypeStruct((3, 1, rows), f32)
    coord_grad, lddt_grad = pl.pallas_call(
        pairs_kernel,
        name="pairs",
        out_shape=(out, out),
        in_specs=smem(3) + vmem(6),
        out_specs=tuple(vmem(2)),
        scratch_shapes=[pltpu.VMEM(g.shape, f32) for g in (gathered_pred, gathered_true)]
        + [
            pltpu.VMEM((rows // PAIR_BLK + 1, 8, PAIR_BLK), f32),
            pltpu.VMEM((2, UNROLL, PAIR_BLK, 2 * PAIR_BLK), f32),
            pltpu.VMEM((2, UNROLL, 16, PAIR_BLK), bf16),
        ],
        compiler_params=pltpu.CompilerParams(vmem_limit_bytes=VMEM_LIMIT),
    )(sigma, counts, partners, gathered_pred, gathered_true, owns, selves, pred, true)
    return jnp.swapaxes(coord_grad, 0, 1), jnp.swapaxes(lddt_grad, 0, 1)


def on_device(
    token_feats, proj_w, atom_single, atom_token, true_coords, noise, sigma, coord_in,
    w_qkv, w_o, w_gu, w_down, gains, w_out, pair_blocks, pair_count,
):
    pred, gathered_pred, gathered_true, owns, selves = run_atoms(
        sigma, pair_count, token_feats.T, proj_w, atom_single, atom_token[None], true_coords,
        jnp.swapaxes(noise, 0, 1), coord_in, w_qkv, w_o, w_gu, w_down, gains, w_out,
    )
    return run_pairs(
        sigma, pair_count, pair_blocks, gathered_pred, gathered_true, owns, selves, pred, true_coords
    )


def solution(mesh):
    in_specs = (
        P("atoms", "samples"),
        P("samples", None),
        P("atoms", None),
        P("atoms"),
        P(None, "atoms"),
        P("samples", None, "atoms"),
        P("samples"),
        P(), P(), P(), P(), P(), P(), P(),
        P("atoms", None),
        P("atoms"),
    )
    out_specs = (P("samples", None, "atoms"), P("samples", None, "atoms"))
    return jax.shard_map(on_device, mesh=mesh, in_specs=in_specs, out_specs=out_specs, check_vma=False)
```

```python
import functools
import math

import jax
import jax.numpy as jnp
from jax import lax
from jax.experimental import pallas as pl
from jax.experimental.pallas import tpu as pltpu
from jax.sharding import PartitionSpec as P

HEADS = 4
HEAD_DIM = 32
FF_ATOM = 256
LAYERS = 3
QBLK = 32
KWIN = 128
PAIR_BLK = 128
CHANNELS = 128
CHUNK = 256
FIRST_UNROLL = 10
UNROLL = 8
HALO = 256
TOK_HALO = 48
TOK_WIN = 64
EPS = 1e-05
DEPTH = 8
VMEM_LIMIT = 56 * 1024 * 1024

f32 = jnp.float32
bf16 = jnp.bfloat16


def dot(a, b, dims=((1,), (0,)), precision=None):
    return lax.dot_general(a, b, (dims, ((), ())), precision=precision, preferred_element_type=f32)


def pieces(v):
    hi = v.astype(bf16).astype(f32)
    mid = (v - hi).astype(bf16).astype(f32)
    lo = (v - hi - mid).astype(bf16).astype(f32)
    return hi, mid, lo


def rms_scale(h):
    return h * lax.rsqrt(jnp.mean(h * h, axis=1, keepdims=True) + EPS)


MESH = pl.DeviceIdType.MESH


def remote(src, dst, send, recv, atom, sample):
    return pltpu.make_async_remote_copy(
        src_ref=src, dst_ref=dst, send_sem=send, recv_sem=recv,
        device_id=(atom, sample), device_id_type=MESH,
    )

def gather_plan(atom_peers):
    nz = DEPTH
    nx = atom_peers // nz
    me = lax.axis_index("atoms")
    x, z = me // nz, lax.rem(me, nz)

    def along_z(dz):
        return x * nz + lax.rem(z + dz + nz, nz)

    def along_x(dx):
        return lax.rem(x + dx, nx) * nz + z

    return nz, nx, me, along_z, along_x


class Gather:
    def __init__(self, atom_peers, pay, whole, sems):
        self.nz, self.nx, self.me, self.along_z, self.along_x = gather_plan(atom_peers)
        self.mine = lax.axis_index("samples")
        self.pay, self.whole = pay, whole
        self.z_send, self.z_recv, self.x_send, self.x_recv = sems
        self.order = [0]
        for step in range(1, self.nz // 2 + 1):
            self.order += [step, self.nz - step] if 2 * step != self.nz else [step]

    def rows(self, owner):
        size = self.pay.shape[0]
        return pl.ds(pl.multiple_of(owner * size, size), size)

    def z_copy(self, dz):
        return remote(
            self.pay, self.whole.at[self.rows(self.me)], self.z_send.at[dz], self.z_recv.at[dz],
            self.along_z(dz), self.mine,
        )

    def line_copy(self, dx):
        size = self.pay.shape[0] * self.nz
        at = pl.ds(pl.multiple_of(self.me // self.nz * size, size), size)
        line = self.whole.at[at]
        return remote(line, line, self.x_send.at[dx], self.x_recv.at[dx], self.along_x(dx), self.mine)

    def start_lines(self):
        self.whole[self.rows(self.me), :] = self.pay[...]
        for dz in self.order[1:]:
            self.z_copy(dz).start()

    def forward_lines(self):
        for dz in self.order[1:]:
            self.z_copy(dz).wait_recv()
        for dx in range(1, self.nx):
            self.line_copy(dx).start()

    def finish_lines(self):
        for dz in self.order[1:]:
            self.z_copy(dz).wait_send()
        for dx in range(1, self.nx):
            self.line_copy(dx).wait()

    groups = ((0, 1), (1, 2), (3, 2), (5, 3))

    def places(self, first, count):
        size = self.pay.shape[0]
        at = pl.multiple_of((self.me // self.nz * self.nz + first) * size, size)
        return self.whole.at[pl.ds(at, count * size)]

    def near_copy(self, i):
        return remote(
            self.pay, self.places(i, 1), self.z_send.at[i], self.z_recv.at[i],
            self.along_z(self.order[i]), self.mine,
        )

    def group_copy(self, j, dx):
        part = self.places(*self.groups[j])
        slot = j * self.nx + dx
        return remote(
            part, part, self.x_send.at[slot], self.x_recv.at[slot], self.along_x(dx), self.mine
        )

    def start(self):
        size = self.pay.shape[0]
        at = pl.multiple_of(self.me // self.nz * self.nz * size, size)
        self.whole[pl.ds(at, size), :] = self.pay[...]
        for i in range(1, self.nz):
            self.near_copy(i).start()
        for dx in range(1, self.nx):
            self.group_copy(0, dx).start()

    def forward(self):
        for j, (first, count) in enumerate(self.groups[1:], 1):
            for i in range(first, first + count):
                self.near_copy(i).wait_recv()
            for dx in range(1, self.nx):
                self.group_copy(j, dx).start()

    def finish(self):
        for i in range(1, self.nz):
            self.near_copy(i).wait_send()
        for j in range(len(self.groups)):
            for dx in range(1, self.nx):
                self.group_copy(j, dx).wait()


def partner_features(x, y, z):
    row8 = lax.broadcasted_iota(jnp.int32, (8, PAIR_BLK), 0)
    row4 = row8 & 3
    n1, n2, n3 = pieces(x * x + y * y + z * z)
    xyz = jnp.where(row4 == 0, x, jnp.where(row4 == 1, y, z))
    upper = jnp.where(row4 == 3, jnp.where(row8 == 3, n1, n2), xyz)
    ones = jnp.where(row8 < 7, 1.0, 0.0)
    lower = jnp.where(row8 < 3, xyz, jnp.where(row8 == 3, n3, ones))
    return jnp.concatenate([upper, lower], axis=0)


def own_features(x, y, z):
    row8 = lax.broadcasted_iota(jnp.int32, (8, PAIR_BLK), 0)
    row4 = row8 & 3
    n1, n2, n3 = pieces(0.25 * (x * x + y * y + z * z + 1.0))
    xp, yp, zp = pieces(-0.5 * x), pieces(-0.5 * y), pieces(-0.5 * z)

    def xyz(i):
        return jnp.where(row4 == 0, xp[i], jnp.where(row4 == 1, yp[i], zp[i]))

    upper = jnp.where(row4 == 3, 0.25, jnp.where(row8 < 4, xyz(0), xyz(1)))
    norms = jnp.where(row8 == 4, n1, jnp.where(row8 == 5, n2, n3))
    norms = jnp.where(row8 == 7, 0.0, norms)
    lower = jnp.where(row8 < 3, xyz(2), jnp.where(row8 == 3, 0.25, norms))
    return jnp.concatenate([upper, lower], axis=0)


def pair_coef(squares):
    sp, st = squares[:, :PAIR_BLK], squares[:, PAIR_BLK:]
    rp = lax.rsqrt(sp)
    gap = sp * rp - st * lax.rsqrt(st)
    e2 = gap * gap + 0.0025
    re = lax.rsqrt(e2)
    err = e2 * re
    th = [jnp.tanh(0.5 * t - err) for t in (0.5, 1.0, 2.0, 4.0)]
    slope = 4.0 - (th[0] * th[0] + th[1] * th[1] + th[2] * th[2] + th[3] * th[3])
    return slope * gap * (re * rp)


def atoms_kernel(
    atom_peers, sample_peers, sigma, counts, feats, proj, own_single, token, true, noise,
    coord_in, wqkv, wo, wgu, wdown, gains, wout,
    pred, gathered_pred, gathered_true, owns, selves,
    hid, kv, queries, bias, pay, true_pay, wide, tok, near_single, cx, hots, partial, arrived, slab, *sems,
):
    rows = own_single.shape[0]
    ext = rows + 2 * HALO
    blocks = rows // PAIR_BLK
    nz, nx, me, along_z, along_x = gather_plan(atom_peers)
    mine = lax.axis_index("samples")
    barrier = pltpu.get_barrier_semaphore()
    right = lax.rem(me + 1, atom_peers)
    left = lax.rem(me + atom_peers - 1, atom_peers)
    share = feats.shape[1] // sample_peers
    (part_send, part_recv, tok_send, tok_recv, edge_send, edge_recv, near_send, near_recv) = sems[:8]

    def greet(atom, sample):
        pl.semaphore_signal(barrier, inc=1, device_id=(atom, sample), device_id_type=MESH)

    for step in range(1, sample_peers):
        greet(me, lax.rem(mine + step, sample_peers))
    greet(left, mine)
    greet(right, mine)
    for owner in (0, 1):
        greet(right, owner)
        greet(left, sample_peers - 1 - owner)
    for dz in range(1, nz):
        greet(along_z(dz), mine)
    for dx in range(1, nx):
        greet(along_x(dx), mine)
    first_atom = me * rows
    total_atoms = rows * atom_peers
    first_tok = me * (tok.shape[0] - 2 * TOK_HALO)
    sig = sigma[0]
    inv = lax.rsqrt(jnp.full((8, CHANNELS), sig * sig + 4.0, f32))[0:1, 0:1]
    zero5 = jnp.zeros((5, CHANNELS), f32)
    hi, mid, lo = pieces(jnp.concatenate([coord_in[...], zero5], axis=0))
    coord_w = jnp.concatenate([hi, mid, lo, hi, mid, hi], axis=0).astype(bf16)
    head = jnp.concatenate([wout[...], jnp.zeros((CHANNELS - 3, CHANNELS), f32)], axis=0).T
    hi, mid, lo = pieces(head)
    head = jnp.concatenate([hi, hi, mid], axis=0).astype(bf16)
    q_scale = math.log2(math.e) / math.sqrt(HEAD_DIM)
    lane = lax.broadcasted_iota(jnp.int32, (1, CHANNELS), 1) // HEAD_DIM

    pos = first_atom - HALO + lax.broadcasted_iota(jnp.int32, (ext, CHANNELS), 0)
    partial[...] = dot(feats[...], proj[...], ((0,), (0,)))
    cx[3:8, pl.ds(HALO, rows)] = jnp.concatenate(
        [token[...].astype(f32), jnp.zeros((4, rows), f32)], axis=0
    )
    for d in range(3):
        cx[d : d + 1, pl.ds(HALO, rows)] = (true[d : d + 1, :] + sig * noise[d]) * inv
    for d in range(3):
        for b in range(blocks):
            wide[d * blocks + b : d * blocks + b + 1, :] = true[
                d : d + 1, b * PAIR_BLK : (b + 1) * PAIR_BLK
            ]
    for b in range(blocks):
        wide[3 * blocks + b : 3 * blocks + b + 1, :] = jnp.full((1, PAIR_BLK), counts[b], jnp.int32).astype(f32)
    true_pay[...] = wide[...].astype(bf16)
    bias[...] = jnp.where((pos >= 0) & (pos < total_atoms), 0.0, -1e30)
    expected = sample_peers + 1 + nz + nx - 2
    on_edge = (mine < 2) | (mine >= sample_peers - 2)
    pl.semaphore_wait(barrier, expected + jnp.where(on_edge, sample_peers, 0))
    true_gather = Gather(atom_peers, true_pay, gathered_true, sems[8:12])
    pred_gather = Gather(atom_peers, pay, gathered_pred, sems[12:16])

    def part_copy(step):
        peer = lax.rem(mine + step, sample_peers)
        at = pl.multiple_of(peer * share, share)
        return remote(
            partial.at[pl.ds(at, share)], arrived.at[step], part_send.at[step], part_recv.at[step],
            me, peer,
        )

    parts = [part_copy(step) for step in range(1, sample_peers)]
    for copy in parts:
        copy.start()
    near = [
        remote(own_single.at[pl.ds(rows - HALO, HALO)], near_single.at[0],
               near_send.at[0], near_recv.at[0], right, mine),
        remote(own_single.at[pl.ds(0, HALO)], near_single.at[1],
               near_send.at[1], near_recv.at[1], left, mine),
        remote(cx.at[:, pl.ds(rows, HALO)], cx.at[:, pl.ds(0, HALO)],
               near_send.at[2], near_recv.at[2], right, mine),
        remote(cx.at[:, pl.ds(HALO, HALO)], cx.at[:, pl.ds(rows + HALO, HALO)],
               near_send.at[3], near_recv.at[3], left, mine),
    ]
    for copy in near:
        copy.start()

    def prepare(k, alone):
        at = pl.multiple_of(k * CHUNK, CHUNK)
        c = cx[:, pl.ds(at, CHUNK)]
        hi, mid, lo = pieces(c)
        coords = jnp.concatenate([hi, hi, hi, mid, mid, lo], axis=0).astype(bf16)
        hid[pl.ds(at, CHUNK), :] = alone.astype(f32) + dot(coords, coord_w, ((0,), (0,)))
        rel = c[3:4, :].astype(jnp.int32) - (first_tok - TOK_HALO + k * (CHUNK // 8))
        hot = jnp.where(lax.broadcasted_iota(jnp.int32, (CHANNELS, CHUNK), 0) == rel, 1.0, 0.0)
        hots[pl.ds(at, CHUNK), :] = hot.T.astype(bf16)

    def prepare_own(k, _):
        prepare(k, own_single[pl.ds(pl.multiple_of((k - 1) * CHUNK, CHUNK), CHUNK), :])
        return 0

    lax.fori_loop(1, 1 + rows // CHUNK, prepare_own, 0, unroll=4)
    for copy in parts:
        copy.wait_recv()
    total = partial[pl.ds(pl.multiple_of(mine * share, share), share), :]
    for step in range(1, sample_peers):
        total = total + arrived[step]
    slab[...] = total.astype(bf16)
    my_rows = pl.ds(pl.multiple_of(TOK_HALO + mine * share, 16), share)
    tok[my_rows, :] = slab[...]

    def tok_copy(step):
        return remote(
            slab, tok.at[my_rows], tok_send.at[step], tok_recv.at[step],
            me, lax.rem(mine + step, sample_peers),
        )

    toks = [tok_copy(step) for step in range(1, sample_peers)]
    for copy in toks:
        copy.start()
    tokens = tok.shape[0] - 2 * TOK_HALO
    rest = TOK_HALO - share
    edges = (
        (sample_peers - 1, pl.ds(0, share), pl.ds(rest, share), right),
        (sample_peers - 2, pl.ds(share - rest, rest), pl.ds(0, rest), right),
        (0, pl.ds(0, share), pl.ds(TOK_HALO + tokens, share), left),
        (1, pl.ds(0, rest), pl.ds(TOK_HALO + tokens + share, rest), left),
    )

    def edge_copy(i, step):
        _, src, dst, to = edges[i]
        return remote(
            slab.at[src], tok.at[dst], edge_send.at[step], edge_recv.at[i],
            to, lax.rem(mine + step, sample_peers),
        )

    for i, edge in enumerate(edges):
        @pl.when(mine == edge[0])
        def _(i=i):
            for step in range(sample_peers):
                edge_copy(i, step).start()

    true_gather.start_lines()
    for copy in near:
        copy.wait_recv()
    prepare(0, near_single[0])
    prepare(ext // CHUNK - 1, near_single[1])
    for copy in toks:
        copy.wait_recv()
    for i in range(len(edges)):
        edge_copy(i, 0).wait_recv()

    def project(layer, at, h):
        normed = (rms_scale(h) * gains[layer, 0:1, :]).astype(bf16)
        out = dot(normed, wqkv[layer])
        rows_at = pl.ds(at, h.shape[0])
        kv[layer % 2, rows_at, :] = out[:, 128:].astype(bf16)
        for t in range(h.shape[0] // CHANNELS):
            turned = (out[t * CHANNELS : (t + 1) * CHANNELS, :128] * q_scale).T
            shifted = [turned if r == 0 else pltpu.roll(turned, r * QBLK, 1) for r in range(HEADS)]
            for w in range(CHANNELS // QBLK):
                spread = jnp.concatenate(
                    [
                        jnp.where(lane == h, shifted[(h - w) % HEADS][h * QBLK : (h + 1) * QBLK], 0.0)
                        for h in range(HEADS)
                    ],
                    axis=0,
                )
                queries[layer % 2, at // QBLK + t * HEADS + w] = spread.astype(bf16)

    def first(k, _):
        at = pl.multiple_of(k * CHUNK, CHUNK)
        tok_at = pl.ds(pl.multiple_of(k * (CHUNK // 8), CHUNK // 8), TOK_WIN)
        h = hid[pl.ds(at, CHUNK), :] + dot(hots[pl.ds(at, CHUNK), 0:TOK_WIN], tok[tok_at, :])
        hid[pl.ds(at, CHUNK), :] = h
        project(0, at, h)
        return 0

    lax.fori_loop(0, ext // CHUNK, first, 0, unroll=FIRST_UNROLL)

    true_gather.forward_lines()

    def attend(layer, at, size):
        buf = layer % 2
        outs = []
        for w in range(size // QBLK):
            keys_at = pl.ds(at + (w * QBLK - 48), KWIN)
            keys = kv[buf, keys_at, 0:128]
            values = kv[buf, keys_at, 128:256]
            scores = dot(keys, queries[buf, at // QBLK + w]) + bias[keys_at, :]
            top = jnp.max(scores, axis=0, keepdims=True)
            weights = jnp.exp2(scores - top)
            weights = (weights * (1.0 / jnp.sum(weights, axis=0, keepdims=True))).astype(bf16)
            both = dot(weights, values, ((0,), (0,)))
            out = both[0:QBLK]
            for h in range(1, HEADS):
                out = jnp.where(lane == h, both[h * QBLK : (h + 1) * QBLK], out)
            outs.append(out.astype(bf16))
        return jnp.concatenate(outs, axis=0)

    def block(layer, at, size):
        h = hid[pl.ds(at, size), :]
        h = h + dot(attend(layer, at, size), wo[layer])
        normed = (rms_scale(h) * gains[layer, 1:2, :]).astype(bf16)
        gu = dot(normed, wgu[layer])
        gate = 0.5 * gu[:, :FF_ATOM]
        inner = (gate * (1.0 + jnp.tanh(gate)) * gu[:, FF_ATOM:]).astype(bf16)
        h = h + dot(inner, wdown[layer])
        if layer + 1 < LAYERS:
            hid[pl.ds(at, size), :] = h
            project(layer + 1, at, h)
        else:
            normed = rms_scale(h)
            hi = normed.astype(bf16)
            mid = (normed - hi.astype(f32)).astype(bf16)
            update = dot(jnp.concatenate([hi, mid, hi], axis=1), head)
            update = jnp.concatenate(
                [update[t * CHANNELS : (t + 1) * CHANNELS].T[0:8] for t in range(size // CHANNELS)],
                axis=1,
            )
            noisy = cx[:, pl.ds(at, size)]
            out = inv * (4.0 * noisy + (2.0 * sig) * update)
            pred[:, pl.ds(pl.multiple_of(at - HALO, 128), size)] = out
            first_block = (at - HALO) // PAIR_BLK
            for d in range(3):
                for i in range(size // PAIR_BLK):
                    wide[pl.ds(d * blocks + first_block + i, 1), :] = out[
                        d : d + 1, i * PAIR_BLK : (i + 1) * PAIR_BLK
                    ]

    for layer in range(LAYERS):
        beyond = (128, 64, 0)[layer]
        block(layer, HALO - beyond, rows + 2 * beyond)

    pay[...] = wide[0 : 3 * blocks, :].astype(bf16)
    pred_gather.start()

    diagonal = lax.broadcasted_iota(jnp.int32, (PAIR_BLK, PAIR_BLK), 0) == lax.broadcasted_iota(
        jnp.int32, (PAIR_BLK, PAIR_BLK), 1
    )
    none = jnp.zeros((16, PAIR_BLK), f32)

    def within(group):
        begun = []
        for b in group:
            at = slice(b * PAIR_BLK, (b + 1) * PAIR_BLK)
            ours = [pred[d : d + 1, at] for d in range(3)]
            known = [true[d : d + 1, at] for d in range(3)]
            own = jnp.concatenate(
                [
                    jnp.concatenate([own_features(*ours), none], axis=1),
                    jnp.concatenate([none, own_features(*known)], axis=1),
                ],
                axis=0,
            ).astype(bf16)
            owns[b] = own
            part = jnp.concatenate(
                [partner_features(*(v.astype(bf16).astype(f32) for v in vs)) for vs in (ours, known)],
                axis=0,
            ).astype(bf16)
            begun.append((part[0:16], dot(part, own, ((0,), (0,)))))
        coefs = [jnp.where(diagonal, 0.0, pair_coef(squares)).astype(bf16) for _, squares in begun]
        for b, (part, _), coef in zip(group, begun, coefs):
            selves[b] = dot(part, coef)[8:16]

    within(range(blocks // 2))
    pred_gather.forward()
    within(range(blocks // 2, blocks))
    for copy in parts + near + toks:
        copy.wait_send()
    for i, edge in enumerate(edges):
        @pl.when(mine == edge[0])
        def _(i=i):
            for step in range(sample_peers):
                edge_copy(i, step).wait_send()

    true_gather.finish_lines()
    pred_gather.finish()


def pairs_kernel(
    sigma, counts, partners, gathered_pred, gathered_true, owns, selves, pred, true,
    coord_grad, lddt_grad, wide_pred, wide_true, totals, held, parts,
):
    blocks = counts.shape[0]
    wide_pred[...] = gathered_pred[...].astype(f32)
    wide_true[...] = gathered_true[...].astype(f32)
    here = partners[0, 0] // blocks
    totals[0:blocks] = selves[...]
    totals[blocks] = jnp.zeros((8, PAIR_BLK), f32)

    def rows_of(wide, base):
        return partner_features(*(wide[pl.ds(base + d * blocks, 1), :] for d in range(3)))

    def begin(b, m):
        known = jnp.minimum(b, blocks - 1)
        p = partners[known, m]
        owner, place = p // blocks, p % blocks
        away = (here - owner) & (DEPTH - 1)
        slot = jnp.where(away <= DEPTH // 2, jnp.maximum(2 * away - 1, 0), 2 * (DEPTH - away))
        line = owner // DEPTH * DEPTH + slot
        part_pred = rows_of(wide_pred, line * (3 * blocks) + place)
        part_true = rows_of(wide_true, owner * (4 * blocks) + place)
        part = jnp.concatenate([part_pred, part_true], axis=0).astype(bf16)
        squares = dot(part, owns[known], ((0,), (0,)))
        count = counts[known]
        row = jnp.where(m < count, b, blocks)
        last = m + 1 >= count
        return part, squares, row, (jnp.where(last, jnp.minimum(b + 1, blocks), b), jnp.where(last, 1, m + 1))

    def start(slot, b, m):
        rows = []
        for i in range(UNROLL):
            part, squares, row, (b, m) = begin(b, m)
            parts[slot, i] = part[0:16]
            held[slot, i] = squares
            rows.append(row)
        return rows, (b, m)

    def end(slot, rows):
        coefs = [pair_coef(held[slot, i]).astype(bf16) for i in range(UNROLL)]
        found = [dot(parts[slot, i], coef)[8:16] for i, coef in enumerate(coefs)]
        for row, sums in zip(rows, found):
            totals[row] = totals[row] + sums

    def visit(_, carry):
        rows, place = carry
        more, place = start(1, *place)
        end(0, rows)
        rows, place = start(0, *place)
        end(1, more)
        return rows, place

    live = jnp.maximum(counts[0] - 1, 1)
    for b in range(1, blocks):
        live = live + jnp.maximum(counts[b] - 1, 1)
    groups = (live + UNROLL - 1) // UNROLL
    rows, _ = lax.fori_loop(0, groups // 2, visit, start(0, jnp.int32(0), jnp.int32(1)))

    @pl.when(groups % 2 == 1)
    def _():
        end(0, rows)

    square = sigma[0] * sigma[0]
    mse_scale = jnp.full((1, PAIR_BLK), square + 4.0, f32) / jnp.full((1, PAIR_BLK), 6.0 * square, f32)
    peers = gathered_true.shape[0] // (4 * blocks)
    listed = jnp.zeros((blocks, PAIR_BLK), f32)
    for peer in range(peers):
        listed = listed + wide_true[peer * 4 * blocks + 3 * blocks : (peer + 1) * 4 * blocks, :]
    listed = jnp.sum(listed, axis=0, keepdims=True)
    total_pairs = listed * (PAIR_BLK * PAIR_BLK) - float(PAIR_BLK * blocks * peers)
    pair_scale = -0.0625 * (blocks * peers * PAIR_BLK * PAIR_BLK) / total_pairs
    for b in range(blocks):
        at = slice(b * PAIR_BLK, (b + 1) * PAIR_BLK)
        total = totals[b]
        for d in range(3):
            pc, tc = pred[d : d + 1, at], true[d : d + 1, at]
            lg = pair_scale * (pc * total[4:5] - total[d : d + 1])
            lddt_grad[d, :, at] = lg
            coord_grad[d, :, at] = mse_scale * (pc - tc) - lg * (1.0 / PAIR_BLK)


def vmem(n):
    return [pl.BlockSpec(memory_space=pltpu.VMEM)] * n


def smem(n):
    return [pl.BlockSpec(memory_space=pltpu.SMEM)] * n


def run_atoms(
    sigma, counts, feats, proj, single, token, true, noise,
    coord_in, w_qkv, w_o, w_gu, w_down, gains, w_out,
):
    rows, tokens = single.shape[0], feats.shape[1]
    ext = rows + 2 * HALO
    blocks = rows // PAIR_BLK
    atom_peers, sample_peers = lax.axis_size("atoms"), lax.axis_size("samples")
    part = tokens // sample_peers
    dma = pltpu.SemaphoreType.DMA
    one_gather = [dma((DEPTH,)), dma((DEPTH,)), dma((atom_peers,)), dma((atom_peers,))]
    return pl.pallas_call(
        functools.partial(atoms_kernel, atom_peers, sample_peers),
        name="atoms",
        out_shape=(
            jax.ShapeDtypeStruct((8, rows), f32),
            jax.ShapeDtypeStruct((atom_peers * 3 * blocks, PAIR_BLK), bf16),
            jax.ShapeDtypeStruct((atom_peers * 4 * blocks, PAIR_BLK), bf16),
            jax.ShapeDtypeStruct((blocks, 32, 2 * PAIR_BLK), bf16),
            jax.ShapeDtypeStruct((blocks, 8, PAIR_BLK), f32),
        ),
        in_specs=smem(2) + vmem(13),
        out_specs=tuple(vmem(5)),
        scratch_shapes=[
            pltpu.VMEM((ext, CHANNELS), f32),
            pltpu.VMEM((2, ext, 2 * CHANNELS), bf16),
            pltpu.VMEM((2, ext // QBLK, CHANNELS, CHANNELS), bf16),
            pltpu.VMEM((ext, CHANNELS), f32),
            pltpu.VMEM((3 * blocks, PAIR_BLK), bf16),
            pltpu.VMEM((4 * blocks, PAIR_BLK), bf16),
            pltpu.VMEM((4 * blocks, PAIR_BLK), f32),
            pltpu.VMEM((tokens + 2 * TOK_HALO, CHANNELS), bf16),
            pltpu.VMEM((2, HALO, CHANNELS), bf16),
            pltpu.VMEM((8, ext), f32),
            pltpu.VMEM((ext, CHANNELS), bf16),
            pltpu.VMEM((tokens, CHANNELS), f32),
            pltpu.VMEM((sample_peers, part, CHANNELS), f32),
            pltpu.VMEM((part, CHANNELS), bf16),
            dma((sample_peers,)), dma((sample_peers,)), dma((sample_peers,)), dma((sample_peers,)),
            dma((sample_peers,)), dma((4,)), dma((4,)), dma((4,)),
        ]
        + 2 * one_gather,
        compiler_params=pltpu.CompilerParams(
            collective_id=0, has_side_effects=True, vmem_limit_bytes=VMEM_LIMIT
        ),
    )(
        sigma, counts, feats, proj, single, token, true, noise,
        coord_in, w_qkv, w_o, w_gu, w_down, gains, w_out.T,
    )


def run_pairs(sigma, counts, partners, gathered_pred, gathered_true, owns, selves, pred, true):
    rows = pred.shape[1]
    out = jax.ShapeDtypeStruct((3, 1, rows), f32)
    coord_grad, lddt_grad = pl.pallas_call(
        pairs_kernel,
        name="pairs",
        out_shape=(out, out),
        in_specs=smem(3) + vmem(6),
        out_specs=tuple(vmem(2)),
        scratch_shapes=[pltpu.VMEM(g.shape, f32) for g in (gathered_pred, gathered_true)]
        + [
            pltpu.VMEM((rows // PAIR_BLK + 1, 8, PAIR_BLK), f32),
            pltpu.VMEM((2, UNROLL, PAIR_BLK, 2 * PAIR_BLK), f32),
            pltpu.VMEM((2, UNROLL, 16, PAIR_BLK), bf16),
        ],
        compiler_params=pltpu.CompilerParams(vmem_limit_bytes=VMEM_LIMIT),
    )(sigma, counts, partners, gathered_pred, gathered_true, owns, selves, pred, true)
    return jnp.swapaxes(coord_grad, 0, 1), jnp.swapaxes(lddt_grad, 0, 1)


def on_device(
    token_feats, proj_w, atom_single, atom_token, true_coords, noise, sigma, coord_in,
    w_qkv, w_o, w_gu, w_down, gains, w_out, pair_blocks, pair_count,
):
    pred, gathered_pred, gathered_true, owns, selves = run_atoms(
        sigma, pair_count, token_feats.T, proj_w, atom_single, atom_token[None], true_coords,
        jnp.swapaxes(noise, 0, 1), coord_in, w_qkv, w_o, w_gu, w_down, gains, w_out,
    )
    return run_pairs(
        sigma, pair_count, pair_blocks, gathered_pred, gathered_true, owns, selves, pred, true_coords
    )


def solution(mesh):
    in_specs = (
        P("atoms", "samples"),
        P("samples", None),
        P("atoms", None),
        P("atoms"),
        P(None, "atoms"),
        P("samples", None, "atoms"),
        P("samples"),
        P(), P(), P(), P(), P(), P(), P(),
        P("atoms", None),
        P("atoms"),
    )
    out_specs = (P("samples", None, "atoms"), P("samples", None, "atoms"))
    return jax.shard_map(on_device, mesh=mesh, in_specs=in_specs, out_specs=out_specs, check_vma=False)
```
